32 devices in a mesh: dev: 32 (over z, y, x, core).
Axes of the slice: x: 2, y: 2, z: 4, core: 2. Of those that a mesh axis runs over, the one named last changes fastest.
Arguments:
- peripheral: bfloat16 [131072, 256], P('dev'), may hold values from -6 to 6
- hubs: bfloat16 [2048, 256], P('dev'), may hold values from -6 to 6
- tiles: bfloat16 [4608, 128, 128], P('dev'), may hold values from -0.5 to 0.5
- tile_rows: int32 [4608], P('dev'), may hold values from 0 to 1039, as said below
- local_cols: int32 [3584], P('dev'), may hold values from 0 to 1039, as said below
- tile_count: int32 [32], P('dev'), may hold values from 32 to 144, as said below
- send_list: int32 [32, 32], P('dev'), may hold values from 0 to 31
- hub_place: int32 [2048], replicated, may hold values from 0 to 2047, each once
- w_in: bfloat16 [2, 256, 2048], replicated, may hold values from -0.375 to 0.375
- w_out: bfloat16 [2, 2048, 256], replicated, may hold values from -0.125 to 0.125
Outputs:
- peripheral_out: bfloat16 [131072, 256], P('dev')
- hubs_out: bfloat16 [2048, 256], P('dev')
The draws below stay inside these ranges and needn't reach their ends.
Inputs may be any that keep to these rules, and one draw needn't show every extreme that they name: `tile_rows`: row blocks of device d's slots are hub blocks (below 16) or d's own blocks 16 + d * 32 to 16 + d * 32 + 31; slots below 32 always name an own block. `local_cols`: column blocks of device d's slots from 32 on are hub blocks or d's own blocks. `tile_count`: every device holds at least 32 live slots; some device is full in every draw.
All inputs are finite; a program needn't handle non-finite values.
Results may differ from the reference program's by a relative error of at most 0.005.
Values may be sent and summed in bfloat16 or wider, within the bound.
No kernel may reach another device: no remote copies, remote signals or barrier semaphores. Data moves between devices by JAX's collectives and lax.ppermute only.
A program may use at most 128 MiB of HBM per device.

```python
import jax
import jax.numpy as jnp
from jax import lax

F = 256
FF = 2048
BLK = 128
HB = 16
LAYERS = 2
PB = 32
EX = 16
NDEV = 32
H = 2048
CAP = 144
PDEV = 4096
PERI = 131072


def graph_plan(key):
    keys = [jax.random.fold_in(key, 101 + number) for number in range(10)]
    sending = jax.random.randint(keys[0], (NDEV, NDEV), 0, PB, dtype=jnp.int32)
    device_ids = jnp.arange(NDEV, dtype=jnp.int32)[:, None]
    slot_index = jnp.arange(CAP, dtype=jnp.int32)[None, :]
    own_row = jax.random.randint(keys[1], (NDEV, CAP), 0, PB, dtype=jnp.int32)
    hub_row = jax.random.randint(keys[2], (NDEV, CAP), 0, HB, dtype=jnp.int32)
    pick_row = jax.random.randint(keys[3], (NDEV, CAP), 0, 2, dtype=jnp.int32)
    rows_all = jnp.where((slot_index >= NDEV) & (pick_row == 0), hub_row, HB + device_ids * PB + own_row)
    own_col = jax.random.randint(keys[4], (NDEV, CAP - NDEV), 0, PB, dtype=jnp.int32)
    hub_col = jax.random.randint(keys[5], (NDEV, CAP - NDEV), 0, HB, dtype=jnp.int32)
    pick_col = jax.random.randint(keys[6], (NDEV, CAP - NDEV), 0, 2, dtype=jnp.int32)
    cols_all = jnp.where(pick_col == 0, hub_col, HB + device_ids * PB + own_col)
    base_count = NDEV + jax.random.randint(keys[7], (NDEV,), 0, 2 * EX + 1, dtype=jnp.int32)
    forced = jax.random.randint(keys[8], (), 0, NDEV, dtype=jnp.int32)
    heavy = (jax.random.randint(keys[9], (NDEV,), 0, 8, dtype=jnp.int32) == 0) | (jnp.arange(NDEV, dtype=jnp.int32) == forced)
    counts = jnp.where(heavy, CAP, base_count).astype(jnp.int32)
    return (sending, rows_all.reshape(-1).astype(jnp.int32), cols_all.reshape(-1).astype(jnp.int32), counts)


def draw_tile_rows(key, part):
    return graph_plan(key)[1]


def draw_local_cols(key, part):
    return graph_plan(key)[2]


def draw_tile_count(key, part):
    return graph_plan(key)[3]


def draw_send_list(key, part):
    return graph_plan(key)[0]


def steps_of(key, dims, pieces, least, top_value):
    def one(dim, shards_of):
        draws = jax.random.uniform(jax.random.fold_in(jax.random.fold_in(key, 6), dim), (shards_of,), jnp.float32, least / len(pieces), top_value / len(pieces))
        return jnp.repeat(jnp.exp(draws), dims[dim] // shards_of).reshape((-1,) + (1,) * (len(dims) - dim - 1))

    level = one(*pieces[0])
    for cut in pieces[1:]:
        level = level * one(*cut)
    return level


def centred(stream_key, shape, spread, bound, pieces=(), kind=jnp.bfloat16):
    array = jax.random.normal(stream_key, shape, jnp.float32) * spread
    if len(pieces) > 0:
        array = steps_of(stream_key, shape, pieces, -0.22, 0.18) * array
    return jnp.clip(array, min=-bound, max=bound).astype(kind)


def setup_inputs(seed: int = 0) -> dict:
    key_list = jax.random.split(jax.random.key(seed), 11)
    peripheral = centred(key_list[0], (PERI, F), 1.0, 6.0, ((0, 32),))
    hubs = centred(key_list[1], (H, F), 1.0, 6.0, ((0, 32),))
    tiles = centred(key_list[2], (NDEV * CAP, BLK, BLK), (BLK * NDEV // PB) ** -0.5, 0.5, ((0, 32),))
    tile_rows = draw_tile_rows(jax.random.fold_in(key_list[10], 71), 0)
    local_cols = draw_local_cols(jax.random.fold_in(key_list[10], 71), 0)
    tile_count = draw_tile_count(jax.random.fold_in(key_list[10], 71), 0)
    send_list = draw_send_list(jax.random.fold_in(key_list[10], 71), 0)
    hub_place = jax.random.permutation(key_list[7], H).astype(jnp.int32)
    w_in = centred(key_list[8], (LAYERS, F, FF), F ** -0.5, 0.375)
    w_out = centred(key_list[9], (LAYERS, FF, F), FF ** -0.5, 0.125)
    return {"peripheral": peripheral, "hubs": hubs, "tiles": tiles, "tile_rows": tile_rows, "local_cols": local_cols, "tile_count": tile_count, "send_list": send_list, "hub_place": hub_place, "w_in": w_in, "w_out": w_out}


epsilon = 1e-06

def feed_forward(rows_in, summed, first, second):
    united = rows_in.astype(jnp.float32) + summed
    normed = (united * lax.rsqrt(lax.optimization_barrier(jnp.mean(united * united, axis=-1, keepdims=True)) + epsilon)).astype(jnp.bfloat16)
    hidden = jnp.maximum(jnp.dot(normed, first, preferred_element_type=jnp.float32), 0.0).astype(jnp.bfloat16)
    return (united + jnp.dot(hidden, second, preferred_element_type=jnp.float32)).astype(jnp.bfloat16)

def reference(peripheral, hubs, tiles, tile_rows, local_cols, tile_count, send_list, hub_place, w_in, w_out):
    devices = NDEV
    remote_cols = HB + jnp.arange(devices, dtype=jnp.int32)[None, :] * PB + send_list.T.astype(jnp.int32)
    columns = jnp.concatenate([remote_cols, local_cols.reshape(devices, CAP - devices).astype(jnp.int32)], axis=1)
    rows_all = tile_rows.reshape(devices, CAP).astype(jnp.int32)
    live_slot = (jnp.arange(CAP, dtype=jnp.int32)[None, :] < tile_count[:, None]).astype(jnp.float32)
    tiles_dev = tiles.reshape(devices, CAP, BLK, BLK)
    inverse = jnp.argsort(hub_place).astype(jnp.int32)
    peri_rows, hub_rows = (peripheral, hubs)
    for layer_index in range(LAYERS):
        column_table = jnp.concatenate([hub_rows[hub_place].reshape(HB, BLK, F), peri_rows.reshape(devices * PB, BLK, F)], axis=0)

        def device_step(total, items):
            tile_block, row_block, col_block, live = items
            products = jnp.einsum('tij,tjf->tif', tile_block.astype(jnp.float32), column_table[col_block].astype(jnp.float32), precision=lax.Precision.HIGHEST)
            return (total.at[row_block].add(products * live[:, None, None]), None)
        start = jnp.zeros((HB + devices * PB, BLK, F), jnp.float32)
        summed, unused = lax.scan(device_step, start, (tiles_dev, rows_all, columns, live_slot))
        hub_sum = summed[:HB].reshape(H, F)[inverse]
        peri_sum = summed[HB:].reshape(devices, PDEV, F)
        first, second = (w_in[layer_index], w_out[layer_index])
        new_peri = lax.map(lambda pair: feed_forward(pair[0], pair[1], first, second), (peri_rows.reshape(devices, PDEV, F), peri_sum))
        hub_rows = feed_forward(hub_rows, hub_sum, first, second)
        peri_rows = new_peri.reshape(devices * PDEV, F)
    return (peri_rows, hub_rows)
```

```python
import functools

import jax
import jax.numpy as jnp
from jax import lax
from jax.experimental import pallas as pl
from jax.experimental.pallas import tpu as pltpu
from jax.sharding import PartitionSpec as P

epsilon = 1e-06
f32 = jnp.float32
bf16 = jnp.bfloat16
MIB = 1024 * 1024
VMEM = pl.BlockSpec(memory_space=pltpu.VMEM)
SMEM = pl.BlockSpec(memory_space=pltpu.SMEM)
ANY = pl.BlockSpec(memory_space=pl.ANY)


def dot(a, b):
    return jnp.dot(a, b, preferred_element_type=f32)


def params(mib):
    return pltpu.CompilerParams(vmem_limit_bytes=mib * MIB)


def normalise(u):
    return (u * lax.rsqrt(jnp.mean(u * u, axis=-1, keepdims=True) + epsilon)).astype(bf16)


def network(u, first, second, hidden_step):
    normed = normalise(u)
    total = u
    for start in range(0, first.shape[-1], hidden_step):
        cut = slice(start, start + hidden_step)
        hidden = jnp.maximum(dot(normed, first[:, cut]), 0.0).astype(bf16)
        total = total + dot(hidden, second[cut, :])
    return total.astype(bf16)


def listed_slots(rows, cols, count, picked, begin, hub_count, want_hub):
    def step(slot, found):
        picked[found] = slot
        is_hub = (rows[slot] < hub_count).astype(jnp.int32)
        return found + (is_hub if want_hub else 1 - is_hub)

    return lax.fori_loop(begin, count[0], step, jnp.int32(0))


def add_products(rows, cols, picked, found, begin, tiles, table, total, row_shift, spare, group):
    def step(number, unused):
        where, products = [], []
        for lane in range(group):
            place = number * group + lane
            live = place < found
            slot = picked[jnp.minimum(place, found - 1)]
            where.append(jnp.where(live, rows[slot] - row_shift, spare))
            products.append(dot(tiles[slot], table[cols[slot - begin]]))
        for row, product in zip(where, products):
            total[row] += product
        return unused

    lax.fori_loop(0, (found + group - 1) // group, step, 0)


def place_rows(place_col, source, out):
    count = source.shape[0]
    step = 256

    def rows_step(number, unused):
        cut = pl.ds(pl.multiple_of(number * step, step), step)
        lanes = lax.broadcasted_iota(jnp.int32, (step, count), 1)
        unit = jnp.where(place_col[cut, :] == lanes, 1.0, 0.0).astype(bf16)
        out[cut, :] = dot(unit, source[...]).astype(bf16)
        return unused

    lax.fori_loop(0, count // step, rows_step, 0)


def pack_kernel(chosen, blocks, outgoing, sems):
    copies = []
    for number in range(outgoing.shape[0]):
        copy = pltpu.make_async_copy(
            blocks.at[chosen[0, number]], outgoing.at[number], sems.at[number]
        )
        copy.start()
        copies.append(copy)
    for copy in copies:
        copy.wait()


def pack(chosen, blocks):
    devices = chosen.shape[1]
    return pl.pallas_call(
        pack_kernel,
        out_shape=jax.ShapeDtypeStruct((devices,) + blocks.shape[1:], bf16),
        in_specs=[SMEM, ANY],
        out_specs=ANY,
        scratch_shapes=[pltpu.SemaphoreType.DMA((devices,))],
        name="pack",
    )(chosen, blocks)


def hub_first_kernel(rows, cols, count, place_col, gathered, own, tiles, part, table, total, picked):
    hub_count, block_size, width = part.shape
    begin = tiles.shape[0] - cols.shape[0]
    flat = table.at[pl.ds(0, hub_count)].reshape(hub_count * block_size, width)
    place_rows(place_col, gathered, flat)
    table[hub_count:] = own[...]
    total[...] = jnp.zeros_like(total)
    found = listed_slots(rows, cols, count, picked, begin, hub_count, True)
    add_products(rows, cols, picked, found, begin, tiles, table, total, 0, hub_count, 4)
    part[...] = total[:hub_count].astype(bf16)


def hub_first(rows, cols, count, place_col, gathered, own, tiles):
    block_size, width = own.shape[1:]
    hub_count = gathered.shape[0] // block_size
    targets = hub_count + own.shape[0]
    return pl.pallas_call(
        hub_first_kernel,
        out_shape=(
            jax.ShapeDtypeStruct((hub_count, block_size, width), bf16),
            jax.ShapeDtypeStruct((targets, block_size, width), bf16),
        ),
        in_specs=[SMEM, SMEM, SMEM, VMEM, VMEM, VMEM, VMEM],
        out_specs=(VMEM, VMEM),
        scratch_shapes=[
            pltpu.VMEM((hub_count + 1, block_size, width), f32),
            pltpu.SMEM((rows.shape[0],), jnp.int32),
        ],
        compiler_params=params(50),
        name="hub_first",
    )(rows, cols, count, place_col, gathered, own, tiles)


def hub_second_kernel(rows, cols, count, mine_rows, place_row, hubs, own, tiles, part, mine, table, total, picked):
    hub_count, block_size, width = hubs.shape
    begin = tiles.shape[0] - cols.shape[0]
    hub_rows = hub_count * block_size
    table[:hub_count] = hubs[...]
    table[hub_count:] = own[...]
    total[...] = jnp.zeros_like(total)
    found = listed_slots(rows, cols, count, picked, begin, hub_count, True)
    add_products(rows, cols, picked, found, begin, tiles, table, total, 0, hub_count, 4)
    sums = total[:hub_count].astype(bf16).reshape(hub_rows, width)
    step = 256

    def rows_step(number, unused):
        cut = pl.ds(pl.multiple_of(number * step, step), step)
        down = lax.broadcasted_iota(jnp.int32, (step, hub_rows), 0) + number * step
        unit = jnp.where(place_row[...] == down, 1.0, 0.0).astype(bf16)
        part[cut, :] = dot(unit, sums).astype(bf16)
        return unused

    lax.fori_loop(0, hub_rows // step, rows_step, 0)
    own_rows = mine.shape[0]
    down = lax.broadcasted_iota(jnp.int32, (own_rows, hub_rows), 0) + mine_rows[0]
    unit = jnp.where(place_row[...] == down, 1.0, 0.0).astype(bf16)
    mine[...] = dot(unit, hubs[...].reshape(hub_rows, width)).astype(bf16)


def hub_second(rows, cols, count, mine_rows, place_row, hubs, own, tiles, hub_local):
    hub_count, block_size, width = hubs.shape
    targets = hub_count + own.shape[0]
    return pl.pallas_call(
        hub_second_kernel,
        out_shape=(
            jax.ShapeDtypeStruct((hub_count * block_size, width), bf16),
            jax.ShapeDtypeStruct((hub_local, width), bf16),
            jax.ShapeDtypeStruct((targets, block_size, width), bf16),
        ),
        in_specs=[SMEM, SMEM, SMEM, SMEM, VMEM, VMEM, VMEM, VMEM],
        out_specs=(VMEM, VMEM, VMEM),
        scratch_shapes=[
            pltpu.VMEM((hub_count + 1, block_size, width), f32),
            pltpu.SMEM((rows.shape[0],), jnp.int32),
        ],
        compiler_params=params(50),
        name="hub_second",
    )(rows, cols, count, mine_rows, place_row, hubs, own, tiles)


def own_kernel(rows, cols, count, table, tiles, total, scratch, picked):
    own_count = total.shape[0]
    hub_count = table.shape[0] - own_count
    begin = tiles.shape[0] - cols.shape[0]
    scratch[:own_count] = table[hub_count:].astype(f32)
    found = listed_slots(rows, cols, count, picked, begin, hub_count, False)
    add_products(
        rows, cols, picked, found, begin, tiles, table, scratch, hub_count, own_count, 4
    )
    total[...] = scratch[:own_count]


def own_sums(rows, cols, count, table, tiles, own_count):
    block_size, width = table.shape[1:]
    return pl.pallas_call(
        own_kernel,
        out_shape=jax.ShapeDtypeStruct((own_count, block_size, width), f32),
        in_specs=[SMEM, SMEM, SMEM, VMEM, VMEM],
        out_specs=VMEM,
        scratch_shapes=[
            pltpu.VMEM((own_count + 1, block_size, width), f32),
            pltpu.SMEM((rows.shape[0],), jnp.int32),
        ],
        compiler_params=params(50),
        name="own_sums",
    )(rows, cols, count, table, tiles)


def hub_network_kernel(rows_in, summed, first, second, out):
    u = rows_in[...].astype(f32) + summed[...]
    out[...] = network(u, first, second, first.shape[-1])


def hub_network(rows_in, summed, first, second):
    return pl.pallas_call(
        hub_network_kernel,
        out_shape=jax.ShapeDtypeStruct(rows_in.shape, bf16),
        in_specs=[VMEM] * 4,
        out_specs=VMEM,
        compiler_params=params(24),
        name="hub_network",
    )(rows_in, summed, first, second)


def network_kernel(row_step, with_send, rows, chosen, base, incoming, tiles, first, second, *refs):
    if with_send:
        out, outgoing, u, inc, adj, one, two, result, sems = refs
    else:
        out, u, inc, adj, one, two, result, sems = refs
        outgoing = None
    own_count, block_size, width = u.shape
    remote = incoming.shape[0]
    loads = [
        pltpu.make_async_copy(base, u, sems.at[0]),
        pltpu.make_async_copy(incoming, inc, sems.at[1]),
        pltpu.make_async_copy(tiles.at[pl.ds(0, remote)], adj, sems.at[2]),
        pltpu.make_async_copy(first, one, sems.at[3]),
        pltpu.make_async_copy(second, two, sems.at[4]),
    ]
    for load in loads:
        load.start()
    for load in loads[:3]:
        load.wait()
    group = 4

    def slots_step(number, unused):
        products = [
            dot(adj[number * group + lane], inc[number * group + lane]) for lane in range(group)
        ]
        for lane in range(group):
            u[rows[number * group + lane]] += products[lane]
        return unused

    lax.fori_loop(0, remote // group, slots_step, 0)
    for load in loads[3:]:
        load.wait()
    blocks = row_step // block_size
    steps = own_count // blocks

    def rows_step(number, unused):
        cut = pl.ds(number * blocks, blocks)
        values = u[cut].reshape(row_step, width)
        result[cut] = network(values, one, two, 512).reshape(blocks, block_size, width)
        return unused

    lax.fori_loop(0, steps, rows_step, 0)
    copies = [pltpu.make_async_copy(result, out, sems.at[0])]
    if with_send:
        for number in range(remote):
            copies.append(
                pltpu.make_async_copy(
                    result.at[chosen[0, number]], outgoing.at[number], sems.at[1 + number]
                )
            )
    for copy in copies:
        copy.start()
    for copy in copies:
        copy.wait()


def peripheral_network(rows, chosen, base, incoming, tiles, first, second, with_send):
    own_count, block_size, width = base.shape
    remote = incoming.shape[0]
    shapes = [jax.ShapeDtypeStruct(base.shape, bf16)]
    if with_send:
        shapes.append(jax.ShapeDtypeStruct(incoming.shape, bf16))
    return pl.pallas_call(
        functools.partial(network_kernel, 512, with_send),
        out_shape=tuple(shapes),
        in_specs=[SMEM, SMEM] + [ANY] * 5,
        out_specs=(ANY,) * len(shapes),
        scratch_shapes=[
            pltpu.VMEM(base.shape, f32),
            pltpu.VMEM(incoming.shape, bf16),
            pltpu.VMEM((remote,) + tiles.shape[1:], bf16),
            pltpu.VMEM(first.shape, bf16),
            pltpu.VMEM(second.shape, bf16),
            pltpu.VMEM(base.shape, bf16),
            pltpu.SemaphoreType.DMA((5 + remote,)),
        ],
        compiler_params=params(50),
        name="peripheral_network",
    )(rows, chosen, base, incoming, tiles, first, second)


def exchange(x, bit):
    devices = lax.axis_size("dev")
    return lax.ppermute(x, "dev", [(i, i ^ bit) for i in range(devices)])


def gather_step(x, bit):
    position = lax.axis_index("dev")
    other = exchange(x, bit)
    mine_first = jnp.stack([x, other], axis=-3)
    other_first = jnp.stack([other, x], axis=-3)
    return jnp.where((position & bit) == 0, mine_first, other_first)


def scatter_step(x, bit):
    position = lax.axis_index("dev")
    mine = ((position & bit) != 0).astype(jnp.int32)
    axis = x.ndim - 3
    kept = lax.dynamic_index_in_dim(x, mine, axis, keepdims=False)
    sent = lax.dynamic_index_in_dim(x, 1 - mine, axis, keepdims=False)
    other = exchange(sent.astype(bf16), bit)
    return kept.astype(f32) + other.astype(f32)


def all_bits():
    devices = lax.axis_size("dev")
    bits = []
    bit = devices // 2
    while bit:
        bits.append(bit)
        bit //= 2
    return bits


def gather_rows(x, early):
    bits = all_bits()
    width = x.shape[-1]
    mark = None
    for number, bit in enumerate(bits):
        x = gather_step(x, bit)
        if number + 1 == early:
            mark = x
    return x.reshape(-1, width), mark


def scatter_rows(x):
    bits = all_bits()
    devices = lax.axis_size("dev")
    width = x.shape[-1]
    x = x.reshape((2,) * len(bits) + (x.shape[0] // devices, width))
    for bit in reversed(bits):
        x = scatter_step(x, bit)
    return x


def body(
    peripheral, hubs, tiles, tile_rows, local_cols, tile_count, send_list, hub_place, w_in, w_out
):
    position = lax.axis_index("dev")
    block_size = tiles.shape[1]
    width = peripheral.shape[1]
    own_count = peripheral.shape[0] // block_size
    hub_rows = hub_place.shape[0]
    hub_count = hub_rows // block_size
    hub_local = hubs.shape[0]
    rows = jnp.where(tile_rows < hub_count, tile_rows, tile_rows - position * own_count)
    cols = jnp.where(local_cols < hub_count, local_cols, local_cols - position * own_count)
    remote_rows = rows[: send_list.shape[1]] - hub_count
    place_col = hub_place.reshape(hub_rows, 1)
    place_row = hub_place.reshape(1, hub_rows)
    mine_rows = (position * hub_local).astype(jnp.int32).reshape(1)
    own = peripheral.reshape(own_count, block_size, width)

    outgoing = pack(send_list, own)
    gathered, mark = gather_rows(hubs, 2)
    outgoing, mark = lax.optimization_barrier((outgoing, mark))
    incoming = lax.all_to_all(outgoing, "dev", split_axis=0, concat_axis=0, tiled=True)
    part, table = hub_first(rows, cols, tile_count, place_col, gathered, own, tiles)
    base = own_sums(rows, cols, tile_count, table, tiles, own_count)
    hub_sum = scatter_rows(part.reshape(hub_rows, width))
    hub_own = lax.dynamic_slice_in_dim(
        table[:hub_count].reshape(hub_rows, width), position * hub_local, hub_local, 0
    )
    hub_new = hub_network(hub_own, hub_sum, w_in[0], w_out[0])
    own, outgoing = peripheral_network(
        remote_rows, send_list, base, incoming, tiles, w_in[0], w_out[0], True
    )

    gathered, mark = gather_rows(hub_new, 2)
    outgoing, mark = lax.optimization_barrier((outgoing, mark))
    incoming = lax.all_to_all(outgoing, "dev", split_axis=0, concat_axis=0, tiled=True)
    part, hub_own, table = hub_second(
        rows,
        cols,
        tile_count,
        mine_rows,
        place_row,
        gathered.reshape(hub_count, block_size, width),
        own,
        tiles,
        hub_local,
    )
    base = own_sums(rows, cols, tile_count, table, tiles, own_count)
    hub_sum = scatter_rows(part)
    hub_out = hub_network(hub_own, hub_sum, w_in[1], w_out[1])
    (peri_out,) = peripheral_network(
        remote_rows, send_list, base, incoming, tiles, w_in[1], w_out[1], False
    )
    return (peri_out.reshape(peripheral.shape), hub_out)


def solution(mesh):
    in_specs = (
        P("dev", None),
        P("dev", None),
        P("dev", None, None),
        P("dev"),
        P("dev"),
        P("dev"),
        P("dev", None),
        P(),
        P(),
        P(),
    )
    out_specs = (P("dev", None), P("dev", None))
    return jax.shard_map(body, mesh=mesh, in_specs=in_specs, out_specs=out_specs, check_vma=False)
```

```python
import functools

import jax
import jax.numpy as jnp
from jax import lax
from jax.experimental import pallas as pl
from jax.experimental.pallas import tpu as pltpu
from jax.sharding import PartitionSpec as P

epsilon = 1e-06
f32 = jnp.float32
bf16 = jnp.bfloat16
MIB = 1024 * 1024
VMEM = pl.BlockSpec(memory_space=pltpu.VMEM)
SMEM = pl.BlockSpec(memory_space=pltpu.SMEM)
ANY = pl.BlockSpec(memory_space=pl.ANY)
GROUP = 4


def dot(a, b):
    return jnp.dot(a, b, preferred_element_type=f32)


def shape_of(shape, dtype):
    return jax.ShapeDtypeStruct(tuple(shape), dtype)


def call(kernel, name, mib, flops, moved, out_shape, in_specs, out_specs, scratch, args):
    return pl.pallas_call(
        kernel,
        out_shape=out_shape,
        in_specs=in_specs,
        out_specs=out_specs,
        scratch_shapes=scratch,
        compiler_params=pltpu.CompilerParams(vmem_limit_bytes=mib * MIB),
        cost_estimate=pl.CostEstimate(flops=flops, bytes_accessed=moved, transcendentals=0),
        name=name,
    )(*args)


def normalise(u):
    return (u * lax.rsqrt(jnp.mean(u * u, axis=-1, keepdims=True) + epsilon)).astype(bf16)


def network(u, first, second, hidden_step):
    normed = normalise(u)
    total = u
    for start in range(0, first.shape[-1], hidden_step):
        cut = slice(start, start + hidden_step)
        hidden = jnp.maximum(dot(normed, first[:, cut]), 0.0).astype(bf16)
        total = total + dot(hidden, second[cut, :])
    return total.astype(bf16)


def list_slots(rows, count, picked, begin, hub_count, want_hub):
    def step(slot, found):
        picked[found] = slot
        is_hub = (rows[slot] < hub_count).astype(jnp.int32)
        return found + (is_hub if want_hub else 1 - is_hub)

    return lax.fori_loop(begin, count[0], step, jnp.int32(0))


def add_products(rows, cols, picked, found, begin, tiles, hubs, own, total, shift, spare):
    hub_count = hubs.shape[0]

    def step(number, unused):
        where, products = [], []
        for lane in range(GROUP):
            place = number * GROUP + lane
            live = place < found
            slot = picked[jnp.minimum(place, found - 1)]
            where.append(jnp.where(live, rows[slot] - shift, spare))
            col = cols[slot - begin]
            of_hub = hubs[jnp.minimum(col, hub_count - 1)]
            of_own = own[jnp.maximum(col - hub_count, 0)]
            products.append(dot(tiles[slot - begin], jnp.where(col < hub_count, of_hub, of_own)))
        for row, product in zip(where, products):
            total[row] += product
        return unused

    lax.fori_loop(0, (found + GROUP - 1) // GROUP, step, 0)


def list_blocks(rows, remote, own_count, hub_count, marks, listed, want_remote):
    def clear(block, unused):
        marks[block] = 0
        return unused

    def mark(slot, unused):
        marks[rows[slot] - hub_count] = 1
        return unused

    def take(block, found):
        listed[found] = block
        return found + (marks[block] if want_remote else 1 - marks[block])

    lax.fori_loop(0, own_count, clear, 0)
    lax.fori_loop(0, remote, mark, 0)
    return lax.fori_loop(0, own_count, take, jnp.int32(0))


def network_blocks(listed, found, u, first, second, result):
    def step(number, unused):
        blocks = [
            listed[jnp.minimum(number * GROUP + lane, found - 1)] for lane in range(GROUP)
        ]
        values = jnp.concatenate([u[block] for block in blocks], axis=0)
        values = network(values, first, second, 512)
        size = u.shape[1]
        for lane, block in enumerate(blocks):
            result[block] = values[lane * size : (lane + 1) * size]
        return unused

    lax.fori_loop(0, (found + GROUP - 1) // GROUP, step, 0)


def pack_kernel(chosen, blocks, outgoing, held, sems):
    load = pltpu.make_async_copy(blocks, held, sems.at[0])
    load.start()
    load.wait()
    copies = []
    for number in range(outgoing.shape[0]):
        copy = pltpu.make_async_copy(
            held.at[chosen[0, number]], outgoing.at[number], sems.at[number]
        )
        copy.start()
        copies.append(copy)
    for copy in copies:
        copy.wait()


def pack(chosen, blocks):
    devices = chosen.shape[1]
    return call(
        pack_kernel,
        "pack",
        8,
        0,
        2 * blocks.size * 2,
        shape_of((devices,) + blocks.shape[1:], bf16),
        [SMEM, ANY],
        ANY,
        [pltpu.VMEM(blocks.shape, bf16), pltpu.SemaphoreType.DMA((devices,))],
        (chosen, blocks),
    )


def slot_place(slot, bits):
    place, weight = 0, 1
    for bit in bits[:2][::-1] + bits[2:-1]:
        place += weight * ((slot // bit) % 2)
        weight *= 2
    return slot % 2, place


def place_shards(me, halves, table, bits, local):
    for slot in range(2 * bits[0]):
        half, place = slot_place(slot, bits)
        start = pl.multiple_of((me ^ slot) * local, local)
        table[pl.ds(start, local), :] = halves[half][place * local : (place + 1) * local, :]


def split_sums(me, sums, local, kept, sent):
    odd = me % 2
    width = sums.shape[-1]
    pairs = sums.reshape(-1, 2, local, width)
    kept[...] = jnp.where(odd == 1, pairs[:, 1], pairs[:, 0]).reshape(kept.shape).astype(kept.dtype)
    sent[...] = jnp.where(odd == 1, pairs[:, 0], pairs[:, 1]).reshape(sent.shape).astype(sent.dtype)


def hub_first_kernel(
    bits, rows, cols, count, position, place_col, half0, half1, own_hbm, tiles_hbm,
    hubs, mine, kept, sent, own, tiles, table, total, picked, sems,
):
    hub_count, block_size, width = hubs.shape
    hub_rows = hub_count * block_size
    local = mine.shape[0]
    begin = rows.shape[0] - cols.shape[0]
    loads = [
        pltpu.make_async_copy(own_hbm, own, sems.at[0]),
        pltpu.make_async_copy(tiles_hbm.at[pl.ds(begin, cols.shape[0])], tiles, sems.at[1]),
    ]
    for load in loads:
        load.start()
    me = position[0]
    place_shards(me, (half0, half1), table, bits, local)
    total[...] = jnp.zeros_like(total)
    found = list_slots(rows, count, picked, begin, hub_count, True)
    step = 2 * block_size

    def rows_step(number, unused):
        cut = pl.ds(pl.multiple_of(number * step, step), step)
        lanes = lax.broadcasted_iota(jnp.int32, (step, hub_rows), 1)
        unit = jnp.where(place_col[cut, :] == lanes, 1.0, 0.0).astype(bf16)
        placed = dot(unit, table[...]).astype(bf16)
        hubs[pl.ds(number * 2, 2)] = placed.reshape(2, block_size, width)
        return unused

    lax.fori_loop(0, hub_rows // step, rows_step, 0)
    for load in loads:
        load.wait()
    add_products(rows, cols, picked, found, begin, tiles, hubs, own, total, 0, hub_count)
    split_sums(me, total[:hub_count], local, kept, sent)
    flat = hubs.reshape(hub_rows, width)
    mine[...] = flat[pl.ds(pl.multiple_of(me * local, local), local), :]


def hub_first(bits, rows, cols, count, position, place_col, halves, own, tiles, local):
    block_size, width = own.shape[1:]
    hub_rows = place_col.shape[0]
    hub_count = hub_rows // block_size
    half = shape_of((hub_rows // 2, width), f32)
    return call(
        functools.partial(hub_first_kernel, bits),
        "hub_first",
        28,
        2 * hub_rows * hub_rows * width,
        14 * MIB,
        (
            shape_of((hub_count, block_size, width), bf16),
            shape_of((local, width), bf16),
            half,
            half,
        ),
        [SMEM] * 4 + [VMEM] * 3 + [ANY] * 2,
        (VMEM,) * 4,
        [
            pltpu.VMEM(own.shape, bf16),
            pltpu.VMEM((cols.shape[0],) + tiles.shape[1:], bf16),
            pltpu.VMEM((hub_rows, width), bf16),
            pltpu.VMEM((hub_count + 1, block_size, width), f32),
            pltpu.SMEM((rows.shape[0],), jnp.int32),
            pltpu.SemaphoreType.DMA((2,)),
        ],
        (rows, cols, count, position, place_col) + tuple(halves) + (own, tiles),
    )


def hub_second_kernel(
    bits, rows, cols, count, position, place_row, half0, half1, own_hbm, tiles_hbm,
    hubs, mine, kept, sent, own, tiles, total, placed, picked, sems,
):
    hub_count, block_size, width = hubs.shape
    hub_rows = hub_count * block_size
    local = mine.shape[0]
    begin = rows.shape[0] - cols.shape[0]
    loads = [
        pltpu.make_async_copy(own_hbm, own, sems.at[0]),
        pltpu.make_async_copy(tiles_hbm.at[pl.ds(begin, cols.shape[0])], tiles, sems.at[1]),
    ]
    for load in loads:
        load.start()
    me = position[0]
    flat = hubs.reshape(hub_rows, width)
    place_shards(me, (half0, half1), flat, bits, local)
    total[...] = jnp.zeros_like(total)
    found = list_slots(rows, count, picked, begin, hub_count, True)

    def unit_rows(start, step):
        down = lax.broadcasted_iota(jnp.int32, (step, hub_rows), 0) + start
        return jnp.where(place_row[...] == down, 1.0, 0.0).astype(bf16)

    mine[...] = dot(unit_rows(me * local, local), flat[...]).astype(bf16)
    for load in loads:
        load.wait()
    add_products(rows, cols, picked, found, begin, tiles, hubs, own, total, 0, hub_count)
    sums = total[:hub_count].astype(bf16).reshape(hub_rows, width)
    step = 2 * block_size

    def rows_step(number, unused):
        start = number * step
        placed[pl.ds(pl.multiple_of(start, step), step), :] = dot(unit_rows(start, step), sums)
        return unused

    lax.fori_loop(0, hub_rows // step, rows_step, 0)
    split_sums(me, placed[...], local, kept, sent)


def hub_second(bits, rows, cols, count, position, place_row, halves, own, tiles, local):
    block_size, width = own.shape[1:]
    hub_rows = place_row.shape[1]
    hub_count = hub_rows // block_size
    return call(
        functools.partial(hub_second_kernel, bits),
        "hub_second",
        28,
        2 * hub_rows * hub_rows * width,
        14 * MIB,
        (
            shape_of((hub_count, block_size, width), bf16),
            shape_of((local, width), bf16),
            shape_of((hub_rows // 2, width), f32),
            shape_of((hub_rows // 2, width), bf16),
        ),
        [SMEM] * 4 + [VMEM] * 3 + [ANY] * 2,
        (VMEM,) * 4,
        [
            pltpu.VMEM(own.shape, bf16),
            pltpu.VMEM((cols.shape[0],) + tiles.shape[1:], bf16),
            pltpu.VMEM((hub_count + 1, block_size, width), f32),
            pltpu.VMEM((hub_rows, width), f32),
            pltpu.SMEM((rows.shape[0],), jnp.int32),
            pltpu.SemaphoreType.DMA((2,)),
        ],
        (rows, cols, count, position, place_row) + tuple(halves) + (own, tiles),
    )


def combine(position, kept, received, bit, radix, local, sent_type):
    rows = kept.shape[0] // radix
    width = kept.shape[1]

    def kernel(position, kept_in, received, *outs):
        total = kept_in[...].astype(f32) + received[...].astype(f32)
        digit = (position[0] // bit) % radix
        parts = total.reshape(rows // local, radix, local, width)
        for offset, out in enumerate(outs):
            value = parts[:, 0]
            for number in range(1, radix):
                value = jnp.where((digit ^ offset) == number, parts[:, number], value)
            out[...] = value.reshape(rows, width).astype(out.dtype)

    shapes = [shape_of((rows, width), f32)] + [shape_of((rows, width), sent_type)] * (radix - 1)
    return call(
        kernel,
        "combine",
        16,
        kept.size,
        12 * kept.size,
        tuple(shapes),
        [SMEM, VMEM, VMEM],
        (VMEM,) * radix,
        [],
        (position, kept, received),
    )


def load_weights(layer, first_in, second_in, first, second, sems):
    loads = [
        pltpu.make_async_copy(first_in.at[layer], first, sems.at[0]),
        pltpu.make_async_copy(second_in.at[layer], second, sems.at[1]),
    ]
    for load in loads:
        load.start()
    return loads


def hub_network_kernel(layer, rows_in, *refs):
    parts, (first_in, second_in, out, first, second, sems) = refs[:-6], refs[-6:]
    loads = load_weights(layer, first_in, second_in, first, second, sems)
    u = rows_in[...].astype(f32)
    for part in parts:
        u = u + part[...].astype(f32)
    for load in loads:
        load.wait()
    out[...] = network(u, first, second, first.shape[-1])


def hub_network(layer, rows_in, parts, first, second):
    return call(
        functools.partial(hub_network_kernel, layer),
        "hub_network",
        20,
        4 * rows_in.size * first.shape[-1],
        2 * first.size,
        shape_of(rows_in.shape, bf16),
        [VMEM] * (1 + len(parts)) + [ANY] * 2,
        VMEM,
        [
            pltpu.VMEM(first.shape[1:], bf16),
            pltpu.VMEM(second.shape[1:], bf16),
            pltpu.SemaphoreType.DMA((2,)),
        ],
        (rows_in,) + tuple(parts) + (first, second),
    )


def before_kernel(
    layer, rows, cols, count, hubs_in, own_in, tiles_in, first_in, second_in, base, out,
    hubs, own, tiles, first, second, u, result, picked, marks, sems,
):
    own_count, block_size, width = own.shape
    hub_count = hubs.shape[0]
    begin = rows.shape[0] - cols.shape[0]
    loads = [
        pltpu.make_async_copy(own_in, own, sems.at[0]),
        pltpu.make_async_copy(hubs_in, hubs, sems.at[1]),
        pltpu.make_async_copy(tiles_in.at[pl.ds(begin, cols.shape[0])], tiles, sems.at[2]),
        pltpu.make_async_copy(first_in.at[layer], first, sems.at[3]),
        pltpu.make_async_copy(second_in.at[layer], second, sems.at[4]),
    ]
    for load in loads:
        load.start()
    found = list_slots(rows, count, picked, begin, hub_count, False)
    loads[0].wait()
    u[:own_count] = own[...].astype(f32)
    loads[1].wait()
    loads[2].wait()
    add_products(rows, cols, picked, found, begin, tiles, hubs, own, u, hub_count, own_count)
    store = pltpu.make_async_copy(u.at[pl.ds(0, own_count)], base, sems.at[5])
    store.start()
    found = list_blocks(rows, begin, own_count, hub_count, marks, picked, False)
    loads[3].wait()
    loads[4].wait()
    network_blocks(picked, found, u, first, second, result)
    last = pltpu.make_async_copy(result, out, sems.at[6])
    last.start()
    store.wait()
    last.wait()


def before(layer, rows, cols, count, hubs, own, tiles, first, second):
    own_count, block_size, width = own.shape
    return call(
        functools.partial(before_kernel, layer),
        "before",
        36,
        4 * own.size * first.shape[-1] // 3,
        18 * MIB,
        (shape_of(own.shape, f32), shape_of(own.shape, bf16)),
        [SMEM] * 3 + [ANY] * 5,
        (ANY, ANY),
        [
            pltpu.VMEM(hubs.shape, bf16),
            pltpu.VMEM(own.shape, bf16),
            pltpu.VMEM((cols.shape[0],) + tiles.shape[1:], bf16),
            pltpu.VMEM(first.shape[1:], bf16),
            pltpu.VMEM(second.shape[1:], bf16),
            pltpu.VMEM((own_count + 1, block_size, width), f32),
            pltpu.VMEM(own.shape, bf16),
            pltpu.SMEM((max(rows.shape[0], own_count),), jnp.int32),
            pltpu.SMEM((own_count,), jnp.int32),
            pltpu.SemaphoreType.DMA((7,)),
        ],
        (rows, cols, count, hubs, own, tiles, first, second),
    )


def after_kernel(
    layer, with_send, hub_count, rows, chosen, base, done, incoming, tiles, first_in, second_in, *refs
):
    out, refs = refs[0], refs[1:]
    if with_send:
        outgoing, refs = refs[0], refs[1:]
    u, inc, adj, first, second, result, listed, marks, sems = refs
    own_count = u.shape[0]
    remote = incoming.shape[0]
    loads = [
        pltpu.make_async_copy(incoming, inc, sems.at[0]),
        pltpu.make_async_copy(tiles.at[pl.ds(0, remote)], adj, sems.at[1]),
        pltpu.make_async_copy(base, u, sems.at[2]),
        pltpu.make_async_copy(first_in.at[layer], first, sems.at[3]),
        pltpu.make_async_copy(second_in.at[layer], second, sems.at[4]),
        pltpu.make_async_copy(done, result, sems.at[5]),
    ]
    for load in loads:
        load.start()
    found = list_blocks(rows, remote, own_count, hub_count, marks, listed, True)
    for load in loads[:3]:
        load.wait()

    def slots_step(number, unused):
        slots = [number * GROUP + lane for lane in range(GROUP)]
        products = [dot(adj[slot], inc[slot]) for slot in slots]
        for slot, product in zip(slots, products):
            u[rows[slot] - hub_count] += product
        return unused

    lax.fori_loop(0, remote // GROUP, slots_step, 0)
    for load in loads[3:]:
        load.wait()
    network_blocks(listed, found, u, first, second, result)
    copies = []
    if with_send:
        for number in range(remote):
            copies.append(
                pltpu.make_async_copy(
                    result.at[chosen[0, number]], outgoing.at[number], sems.at[number]
                )
            )
    copies.append(pltpu.make_async_copy(result, out, sems.at[remote]))
    for copy in copies:
        copy.start()
    for copy in copies:
        copy.wait()


def after(layer, rows, chosen, base, done, incoming, tiles, first, second, hub_count, with_send):
    own_count, block_size, width = base.shape
    remote = incoming.shape[0]
    shapes = [shape_of(base.shape, bf16)]
    if with_send:
        shapes.append(shape_of(incoming.shape, bf16))
    return call(
        functools.partial(after_kernel, layer, with_send, hub_count),
        "after",
        36,
        4 * base.size * first.shape[-1],
        16 * MIB,
        tuple(shapes),
        [SMEM, SMEM] + [ANY] * 6,
        (ANY,) * len(shapes),
        [
            pltpu.VMEM(base.shape, f32),
            pltpu.VMEM(incoming.shape, bf16),
            pltpu.VMEM((remote,) + tiles.shape[1:], bf16),
            pltpu.VMEM(first.shape[1:], bf16),
            pltpu.VMEM(second.shape[1:], bf16),
            pltpu.VMEM(base.shape, bf16),
            pltpu.SMEM((own_count,), jnp.int32),
            pltpu.SMEM((own_count,), jnp.int32),
            pltpu.SemaphoreType.DMA((max(6, 1 + remote),)),
        ],
        (rows, chosen, base, done, incoming, tiles, first, second),
    )


def exchange(x, bit):
    devices = lax.axis_size("dev")
    return lax.ppermute(x, "dev", [(i, i ^ bit) for i in range(devices)])


def all_bits():
    bits = []
    bit = lax.axis_size("dev") // 2
    while bit:
        bits.append(bit)
        bit //= 2
    return bits


def gather_far(x, bits):
    high, low = bits[:2]
    return [x, exchange(x, low), exchange(x, high), exchange(x, high + low)]


def gather_near(pieces, bits):
    x = jnp.concatenate(pieces, axis=0)
    for bit in bits[2:-1]:
        x = jnp.concatenate([x, exchange(x, bit)], axis=0)
    return x, exchange(x, bits[-1])


def scatter_rows(position, kept, sent, bits, local):
    near = bits[2:][::-1]
    for number, bit in enumerate(near):
        received = exchange(sent, bit)
        if number + 1 < len(near):
            kept, sent = combine(position, kept, received, near[number + 1], 2, local, bf16)
    kept, *sent = combine(position, kept, received, bits[1], 4, local, f32)
    masks = (bits[1], bits[0], bits[0] + bits[1])
    return [kept] + [exchange(part, mask) for part, mask in zip(sent, masks)]


def body(
    peripheral, hubs, tiles, tile_rows, local_cols, tile_count, send_list, hub_place, w_in, w_out
):
    position = lax.axis_index("dev")
    bits = all_bits()
    block_size = tiles.shape[1]
    width = peripheral.shape[1]
    own_count = peripheral.shape[0] // block_size
    hub_rows = hub_place.shape[0]
    hub_count = hub_rows // block_size
    local = hubs.shape[0]
    rows = jnp.where(tile_rows < hub_count, tile_rows, tile_rows - position * own_count)
    cols = jnp.where(local_cols < hub_count, local_cols, local_cols - position * own_count)
    place_col = hub_place.reshape(hub_rows, 1)
    place_row = hub_place.reshape(1, hub_rows)
    me = position.astype(jnp.int32).reshape(1)
    own = peripheral.reshape(own_count, block_size, width)
    all_to_all = functools.partial(
        lax.all_to_all, axis_name="dev", split_axis=0, concat_axis=0, tiled=True
    )

    outgoing = pack(send_list, own)
    pieces = gather_far(hubs, bits)
    outgoing, *pieces = lax.optimization_barrier((outgoing, *pieces))
    incoming = all_to_all(outgoing)
    halves = gather_near(pieces, bits)
    hub_table, mine, kept, sent = hub_first(
        bits, rows, cols, tile_count, me, place_col, halves, own, tiles, local
    )
    base, done = before(0, rows, cols, tile_count, hub_table, own, tiles, w_in, w_out)
    parts = scatter_rows(me, kept, sent, bits, local)
    hub_new = hub_network(0, mine, parts, w_in, w_out)
    own, outgoing = after(
        0, rows, send_list, base, done, incoming, tiles, w_in, w_out, hub_count, True
    )

    pieces = gather_far(hub_new, bits)
    outgoing, *pieces = lax.optimization_barrier((outgoing, *pieces))
    incoming = all_to_all(outgoing)
    halves = gather_near(pieces, bits)
    hub_table, mine, kept, sent = hub_second(
        bits, rows, cols, tile_count, me, place_row, halves, own, tiles, local
    )
    base, done = before(1, rows, cols, tile_count, hub_table, own, tiles, w_in, w_out)
    parts = scatter_rows(me, kept, sent, bits, local)
    hub_out = hub_network(1, mine, parts, w_in, w_out)
    (peri_out,) = after(
        1, rows, send_list, base, done, incoming, tiles, w_in, w_out, hub_count, False
    )
    return (peri_out.reshape(peripheral.shape), hub_out)


def solution(mesh):
    in_specs = (
        P("dev", None),
        P("dev", None),
        P("dev", None, None),
        P("dev"),
        P("dev"),
        P("dev"),
        P("dev", None),
        P(),
        P(),
        P(),
    )
    out_specs = (P("dev", None), P("dev", None))
    return jax.shard_map(body, mesh=mesh, in_specs=in_specs, out_specs=out_specs, check_vma=False)
```

```python
import functools

import jax
import jax.numpy as jnp
from jax import lax
from jax.experimental import pallas as pl
from jax.experimental.pallas import tpu as pltpu
from jax.sharding import PartitionSpec as P

epsilon = 1e-06
f32 = jnp.float32
bf16 = jnp.bfloat16
MIB = 1024 * 1024
VMEM = pl.BlockSpec(memory_space=pltpu.VMEM)
SMEM = pl.BlockSpec(memory_space=pltpu.SMEM)
ANY = pl.BlockSpec(memory_space=pl.ANY)
GROUP = 4


def dot(a, b):
    return jnp.dot(a, b, preferred_element_type=f32)


def shape_of(shape, dtype):
    return jax.ShapeDtypeStruct(tuple(shape), dtype)


def call(kernel, name, mib, flops, moved, out_shape, in_specs, out_specs, scratch, args):
    return pl.pallas_call(
        kernel,
        out_shape=out_shape,
        in_specs=in_specs,
        out_specs=out_specs,
        scratch_shapes=scratch,
        compiler_params=pltpu.CompilerParams(vmem_limit_bytes=mib * MIB),
        cost_estimate=pl.CostEstimate(flops=flops, bytes_accessed=moved, transcendentals=0),
        name=name,
    )(*args)


def normalise(u):
    return (u * lax.rsqrt(jnp.mean(u * u, axis=-1, keepdims=True) + epsilon)).astype(bf16)


def network(u, first, second, hidden_step):
    normed = normalise(u)
    total = u
    for start in range(0, first.shape[-1], hidden_step):
        cut = slice(start, start + hidden_step)
        hidden = jnp.maximum(dot(normed, first[:, cut]), 0.0).astype(bf16)
        total = total + dot(hidden, second[cut, :])
    return total.astype(bf16)


def list_slots(rows, count, picked, begin, hub_count, want_hub):
    def step(slot, found):
        picked[found] = slot
        is_hub = (rows[slot] < hub_count).astype(jnp.int32)
        return found + (is_hub if want_hub else 1 - is_hub)

    return lax.fori_loop(begin, count[0], step, jnp.int32(0))


def add_products(rows, cols, picked, found, begin, tiles, hubs, own, total, shift, spare):
    hub_count = hubs.shape[0]

    def step(number, unused):
        where, products = [], []
        for lane in range(GROUP):
            place = number * GROUP + lane
            live = place < found
            slot = picked[jnp.minimum(place, found - 1)]
            where.append(jnp.where(live, rows[slot] - shift, spare))
            col = cols[slot - begin]
            of_hub = hubs[jnp.minimum(col, hub_count - 1)]
            of_own = own[jnp.maximum(col - hub_count, 0)]
            products.append(dot(tiles[slot - begin], jnp.where(col < hub_count, of_hub, of_own)))
        for row, product in zip(where, products):
            total[row] += product
        return unused

    lax.fori_loop(0, (found + GROUP - 1) // GROUP, step, 0)


def list_blocks(rows, remote, own_count, hub_count, marks, listed, want_remote):
    def clear(block, unused):
        marks[block] = 0
        return unused

    def mark(slot, unused):
        marks[rows[slot] - hub_count] = 1
        return unused

    def take(block, found):
        listed[found] = block
        return found + (marks[block] if want_remote else 1 - marks[block])

    lax.fori_loop(0, own_count, clear, 0)
    lax.fori_loop(0, remote, mark, 0)
    return lax.fori_loop(0, own_count, take, jnp.int32(0))


def network_blocks(listed, found, u, first, second, result):
    def step(number, unused):
        blocks = [
            listed[jnp.minimum(number * GROUP + lane, found - 1)] for lane in range(GROUP)
        ]
        values = jnp.concatenate([u[block] for block in blocks], axis=0)
        values = network(values, first, second, 512)
        size = u.shape[1]
        for lane, block in enumerate(blocks):
            result[block] = values[lane * size : (lane + 1) * size]
        return unused

    lax.fori_loop(0, (found + GROUP - 1) // GROUP, step, 0)


def pack_kernel(chosen, blocks, outgoing, held, sems):
    load = pltpu.make_async_copy(blocks, held, sems.at[0])
    load.start()
    load.wait()
    copies = []
    for number in range(outgoing.shape[0]):
        copy = pltpu.make_async_copy(
            held.at[chosen[0, number]], outgoing.at[number], sems.at[number]
        )
        copy.start()
        copies.append(copy)
    for copy in copies:
        copy.wait()


def pack(chosen, blocks):
    devices = chosen.shape[1]
    return call(
        pack_kernel,
        "pack",
        58,
        0,
        2 * blocks.size * 2,
        shape_of((devices,) + blocks.shape[1:], bf16),
        [SMEM, ANY],
        ANY,
        [pltpu.VMEM(blocks.shape, bf16), pltpu.SemaphoreType.DMA((devices,))],
        (chosen, blocks),
    )


def slot_place(slot, digits):
    place, weight = 0, 1
    for bit, radix in digits[:0:-1]:
        place += weight * ((slot // bit) % radix)
        weight *= radix
    return slot % 2, place


def place_shards(me, halves, table, digits, local):
    for slot in range(table.shape[0] // local):
        half, place = slot_place(slot, digits)
        start = pl.multiple_of((me ^ slot) * local, local)
        table[pl.ds(start, local), :] = halves[half][place * local : (place + 1) * local, :]


def split_sums(me, sums, local, kept, sent):
    odd = me % 2
    width = sums.shape[-1]
    pairs = sums.reshape(-1, 2, local, width)
    kept[...] = jnp.where(odd == 1, pairs[:, 1], pairs[:, 0]).reshape(kept.shape).astype(kept.dtype)
    sent[...] = jnp.where(odd == 1, pairs[:, 0], pairs[:, 1]).reshape(sent.shape).astype(sent.dtype)


def hub_first_kernel(
    digits, rows, cols, count, position, place_col, half0, half1, own_hbm, tiles_hbm,
    hubs, mine, kept, sent, own, tiles, table, total, picked, sems,
):
    hub_count, block_size, width = hubs.shape
    hub_rows = hub_count * block_size
    local = mine.shape[0]
    begin = rows.shape[0] - cols.shape[0]
    loads = [
        pltpu.make_async_copy(own_hbm, own, sems.at[0]),
        pltpu.make_async_copy(tiles_hbm.at[pl.ds(begin, cols.shape[0])], tiles, sems.at[1]),
    ]
    for load in loads:
        load.start()
    me = position[0]
    place_shards(me, (half0, half1), table, digits, local)
    total[...] = jnp.zeros_like(total)
    found = list_slots(rows, count, picked, begin, hub_count, True)
    step = 2 * block_size

    def rows_step(number, unused):
        cut = pl.ds(pl.multiple_of(number * step, step), step)
        lanes = lax.broadcasted_iota(jnp.int32, (step, hub_rows), 1)
        unit = jnp.where(place_col[cut, :] == lanes, 1.0, 0.0).astype(bf16)
        placed = dot(unit, table[...]).astype(bf16)
        hubs[pl.ds(number * 2, 2)] = placed.reshape(2, block_size, width)
        return unused

    lax.fori_loop(0, hub_rows // step, rows_step, 0)
    for load in loads:
        load.wait()
    add_products(rows, cols, picked, found, begin, tiles, hubs, own, total, 0, hub_count)
    split_sums(me, total[:hub_count], local, kept, sent)
    flat = hubs.reshape(hub_rows, width)
    mine[...] = flat[pl.ds(pl.multiple_of(me * local, local), local), :]


def hub_first(digits, rows, cols, count, position, place_col, halves, own, tiles, local):
    block_size, width = own.shape[1:]
    hub_rows = place_col.shape[0]
    hub_count = hub_rows // block_size
    half = shape_of((hub_rows // 2, width), f32)
    return call(
        functools.partial(hub_first_kernel, digits),
        "hub_first",
        54,
        2 * hub_rows * hub_rows * width,
        14 * MIB,
        (
            shape_of((hub_count, block_size, width), bf16),
            shape_of((local, width), bf16),
            half,
            half,
        ),
        [SMEM] * 4 + [VMEM] * 3 + [ANY] * 2,
        (VMEM,) * 4,
        [
            pltpu.VMEM(own.shape, bf16),
            pltpu.VMEM((cols.shape[0],) + tiles.shape[1:], bf16),
            pltpu.VMEM((hub_rows, width), bf16),
            pltpu.VMEM((hub_count + 1, block_size, width), f32),
            pltpu.SMEM((rows.shape[0],), jnp.int32),
            pltpu.SemaphoreType.DMA((2,)),
        ],
        (rows, cols, count, position, place_col) + tuple(halves) + (own, tiles),
    )


def hub_second_kernel(
    digits, rows, cols, count, position, place_row, half0, half1, own_hbm, tiles_hbm,
    hubs, mine, kept, sent, own, tiles, total, placed, picked, sems,
):
    hub_count, block_size, width = hubs.shape
    hub_rows = hub_count * block_size
    local = mine.shape[0]
    begin = rows.shape[0] - cols.shape[0]
    loads = [
        pltpu.make_async_copy(own_hbm, own, sems.at[0]),
        pltpu.make_async_copy(tiles_hbm.at[pl.ds(begin, cols.shape[0])], tiles, sems.at[1]),
    ]
    for load in loads:
        load.start()
    me = position[0]
    flat = hubs.reshape(hub_rows, width)
    place_shards(me, (half0, half1), flat, digits, local)
    total[...] = jnp.zeros_like(total)
    found = list_slots(rows, count, picked, begin, hub_count, True)

    def unit_rows(start, step):
        down = lax.broadcasted_iota(jnp.int32, (step, hub_rows), 0) + start
        return jnp.where(place_row[...] == down, 1.0, 0.0).astype(bf16)

    mine[...] = dot(unit_rows(me * local, local), flat[...]).astype(bf16)
    for load in loads:
        load.wait()
    add_products(rows, cols, picked, found, begin, tiles, hubs, own, total, 0, hub_count)
    sums = total[:hub_count].astype(bf16).reshape(hub_rows, width)
    step = 2 * block_size

    def rows_step(number, unused):
        start = number * step
        placed[pl.ds(pl.multiple_of(start, step), step), :] = dot(unit_rows(start, step), sums)
        return unused

    lax.fori_loop(0, hub_rows // step, rows_step, 0)
    split_sums(me, placed[...], local, kept, sent)


def hub_second(digits, rows, cols, count, position, place_row, halves, own, tiles, local):
    block_size, width = own.shape[1:]
    hub_rows = place_row.shape[1]
    hub_count = hub_rows // block_size
    return call(
        functools.partial(hub_second_kernel, digits),
        "hub_second",
        54,
        2 * hub_rows * hub_rows * width,
        14 * MIB,
        (
            shape_of((hub_count, block_size, width), bf16),
            shape_of((local, width), bf16),
            shape_of((hub_rows // 2, width), f32),
            shape_of((hub_rows // 2, width), bf16),
        ),
        [SMEM] * 4 + [VMEM] * 3 + [ANY] * 2,
        (VMEM,) * 4,
        [
            pltpu.VMEM(own.shape, bf16),
            pltpu.VMEM((cols.shape[0],) + tiles.shape[1:], bf16),
            pltpu.VMEM((hub_count + 1, block_size, width), f32),
            pltpu.VMEM((hub_rows, width), f32),
            pltpu.SMEM((rows.shape[0],), jnp.int32),
            pltpu.SemaphoreType.DMA((2,)),
        ],
        (rows, cols, count, position, place_row) + tuple(halves) + (own, tiles),
    )


def combine(position, kept, received, bit, radix, local, sent_type):
    rows = kept.shape[0] // radix
    width = kept.shape[1]

    def kernel(position, kept_in, *refs):
        received, outs = refs[: -radix], refs[-radix:]
        total = kept_in[...].astype(f32)
        for part in received:
            total = total + part[...].astype(f32)
        digit = (position[0] // bit) % radix
        parts = total.reshape(rows // local, radix, local, width)
        for offset, out in enumerate(outs):
            value = parts[:, 0]
            for number in range(1, radix):
                value = jnp.where((digit ^ offset) == number, parts[:, number], value)
            out[...] = value.reshape(rows, width).astype(out.dtype)

    shapes = [shape_of((rows, width), f32)] + [shape_of((rows, width), sent_type)] * (radix - 1)
    return call(
        kernel,
        "combine",
        16,
        kept.size,
        12 * kept.size,
        tuple(shapes),
        [SMEM] + [VMEM] * (1 + len(received)),
        (VMEM,) * radix,
        [],
        (position, kept) + tuple(received),
    )


def load_weights(layer, first_in, second_in, first, second, sems):
    loads = [
        pltpu.make_async_copy(first_in.at[layer], first, sems.at[0]),
        pltpu.make_async_copy(second_in.at[layer], second, sems.at[1]),
    ]
    for load in loads:
        load.start()
    return loads


def hub_network_kernel(layer, rows_in, *refs):
    parts, (first_in, second_in, out, first, second, sems) = refs[:-6], refs[-6:]
    loads = load_weights(layer, first_in, second_in, first, second, sems)
    u = rows_in[...].astype(f32)
    for part in parts:
        u = u + part[...].astype(f32)
    for load in loads:
        load.wait()
    out[...] = network(u, first, second, first.shape[-1])


def hub_network(layer, rows_in, parts, first, second):
    return call(
        functools.partial(hub_network_kernel, layer),
        "hub_network",
        58,
        4 * rows_in.size * first.shape[-1],
        2 * first.size,
        shape_of(rows_in.shape, bf16),
        [VMEM] * (1 + len(parts)) + [ANY] * 2,
        VMEM,
        [
            pltpu.VMEM(first.shape[1:], bf16),
            pltpu.VMEM(second.shape[1:], bf16),
            pltpu.SemaphoreType.DMA((2,)),
        ],
        (rows_in,) + tuple(parts) + (first, second),
    )


def before_kernel(
    layer, rows, cols, count, hubs_in, own_in, tiles_in, first_in, second_in, base, out,
    hubs, own, tiles, first, second, u, result, picked, marks, sems,
):
    own_count, block_size, width = own.shape
    hub_count = hubs.shape[0]
    begin = rows.shape[0] - cols.shape[0]
    loads = [
        pltpu.make_async_copy(own_in, own, sems.at[0]),
        pltpu.make_async_copy(hubs_in, hubs, sems.at[1]),
        pltpu.make_async_copy(tiles_in.at[pl.ds(begin, cols.shape[0])], tiles, sems.at[2]),
        pltpu.make_async_copy(first_in.at[layer], first, sems.at[3]),
        pltpu.make_async_copy(second_in.at[layer], second, sems.at[4]),
    ]
    for load in loads:
        load.start()
    found = list_slots(rows, count, picked, begin, hub_count, False)
    loads[0].wait()
    u[:own_count] = own[...].astype(f32)
    loads[1].wait()
    loads[2].wait()
    add_products(rows, cols, picked, found, begin, tiles, hubs, own, u, hub_count, own_count)
    store = pltpu.make_async_copy(u.at[pl.ds(0, own_count)], base, sems.at[5])
    store.start()
    found = list_blocks(rows, begin, own_count, hub_count, marks, picked, False)
    loads[3].wait()
    loads[4].wait()
    network_blocks(picked, found, u, first, second, result)
    last = pltpu.make_async_copy(result, out, sems.at[6])
    last.start()
    store.wait()
    last.wait()


def before(layer, rows, cols, count, hubs, own, tiles, first, second):
    own_count, block_size, width = own.shape
    return call(
        functools.partial(before_kernel, layer),
        "before",
        58,
        4 * own.size * first.shape[-1] // 3,
        18 * MIB,
        (shape_of(own.shape, f32), shape_of(own.shape, bf16)),
        [SMEM] * 3 + [ANY] * 5,
        (ANY, ANY),
        [
            pltpu.VMEM(hubs.shape, bf16),
            pltpu.VMEM(own.shape, bf16),
            pltpu.VMEM((cols.shape[0],) + tiles.shape[1:], bf16),
            pltpu.VMEM(first.shape[1:], bf16),
            pltpu.VMEM(second.shape[1:], bf16),
            pltpu.VMEM((own_count + 1, block_size, width), f32),
            pltpu.VMEM(own.shape, bf16),
            pltpu.SMEM((max(rows.shape[0], own_count),), jnp.int32),
            pltpu.SMEM((own_count,), jnp.int32),
            pltpu.SemaphoreType.DMA((7,)),
        ],
        (rows, cols, count, hubs, own, tiles, first, second),
    )


def after_kernel(
    layer, with_send, hub_count, rows, chosen, base, done, incoming, tiles, first_in, second_in, *refs
):
    out, refs = refs[0], refs[1:]
    if with_send:
        outgoing, refs = refs[0], refs[1:]
    u, inc, adj, first, second, result, listed, marks, sems = refs
    own_count = u.shape[0]
    remote = incoming.shape[0]
    loads = [
        pltpu.make_async_copy(incoming, inc, sems.at[0]),
        pltpu.make_async_copy(tiles.at[pl.ds(0, remote)], adj, sems.at[1]),
        pltpu.make_async_copy(base, u, sems.at[2]),
        pltpu.make_async_copy(first_in.at[layer], first, sems.at[3]),
        pltpu.make_async_copy(second_in.at[layer], second, sems.at[4]),
        pltpu.make_async_copy(done, result, sems.at[5]),
    ]
    for load in loads[:3]:
        load.start()
    found = list_blocks(rows, remote, own_count, hub_count, marks, listed, True)
    for load in loads[:3]:
        load.wait()
    for load in loads[3:]:
        load.start()
    group = 2 * GROUP

    def slots_step(number, unused):
        slots = [number * group + lane for lane in range(group)]
        products = [dot(adj[slot], inc[slot]) for slot in slots]
        for slot, product in zip(slots, products):
            u[rows[slot] - hub_count] += product
        return unused

    lax.fori_loop(0, remote // group, slots_step, 0)
    for load in loads[3:]:
        load.wait()
    network_blocks(listed, found, u, first, second, result)
    copies = []
    if with_send:
        for number in range(remote):
            copies.append(
                pltpu.make_async_copy(
                    result.at[chosen[0, number]], outgoing.at[number], sems.at[number]
                )
            )
    copies.append(pltpu.make_async_copy(result, out, sems.at[remote]))
    for copy in copies:
        copy.start()
    for copy in copies:
        copy.wait()


def after(layer, rows, chosen, base, done, incoming, tiles, first, second, hub_count, with_send):
    own_count, block_size, width = base.shape
    remote = incoming.shape[0]
    shapes = [shape_of(base.shape, bf16)]
    if with_send:
        shapes.append(shape_of(incoming.shape, bf16))
    return call(
        functools.partial(after_kernel, layer, with_send, hub_count),
        "after",
        58,
        4 * base.size * first.shape[-1],
        16 * MIB,
        tuple(shapes),
        [SMEM, SMEM] + [ANY] * 6,
        (ANY,) * len(shapes),
        [
            pltpu.VMEM(base.shape, f32),
            pltpu.VMEM(incoming.shape, bf16),
            pltpu.VMEM((remote,) + tiles.shape[1:], bf16),
            pltpu.VMEM(first.shape[1:], bf16),
            pltpu.VMEM(second.shape[1:], bf16),
            pltpu.VMEM(base.shape, bf16),
            pltpu.SMEM((own_count,), jnp.int32),
            pltpu.SMEM((own_count,), jnp.int32),
            pltpu.SemaphoreType.DMA((max(6, 1 + remote),)),
        ],
        (rows, chosen, base, done, incoming, tiles, first, second),
    )


def exchange(x, bit):
    devices = lax.axis_size("dev")
    return lax.ppermute(x, "dev", [(i, i ^ bit) for i in range(devices)])


def all_digits():
    devices = lax.axis_size("dev")
    digits, bit = [(1, 2)], 2
    while bit < devices:
        radix = 4 if 4 * bit <= devices else 2
        digits.append((bit, radix))
        bit *= radix
    return digits


def gather_step(x, bit, radix):
    return [x] + [exchange(x, bit * offset) for offset in range(1, radix)]


def gather_far(x, digits):
    return gather_step(x, *digits[-1])


def gather_near(pieces, digits):
    for digit in digits[-2:0:-1]:
        pieces = gather_step(jnp.concatenate(pieces, axis=0), *digit)
    x = jnp.concatenate(pieces, axis=0)
    return x, exchange(x, digits[0][0])


def scatter_near(position, kept, sent, digits, local):
    received = [exchange(sent, digits[0][0])]
    for bit, radix in digits[1:-1]:
        kept, *sent = combine(position, kept, received, bit, radix, local, bf16)
        received = [exchange(part, bit * (1 + number)) for number, part in enumerate(sent)]
    return kept, received


def scatter_far(position, kept, received, digits, local):
    bit, radix = digits[-1]
    kept, *sent = combine(position, kept, received, bit, radix, local, f32)
    return [kept] + [exchange(part, bit * (1 + number)) for number, part in enumerate(sent)]


def body(
    peripheral, hubs, tiles, tile_rows, local_cols, tile_count, send_list, hub_place, w_in, w_out
):
    position = lax.axis_index("dev")
    digits = all_digits()
    block_size = tiles.shape[1]
    width = peripheral.shape[1]
    own_count = peripheral.shape[0] // block_size
    hub_rows = hub_place.shape[0]
    hub_count = hub_rows // block_size
    local = hubs.shape[0]
    rows = jnp.where(tile_rows < hub_count, tile_rows, tile_rows - position * own_count)
    cols = jnp.where(local_cols < hub_count, local_cols, local_cols - position * own_count)
    place_col = hub_place.reshape(hub_rows, 1)
    place_row = hub_place.reshape(1, hub_rows)
    me = position.astype(jnp.int32).reshape(1)
    own = peripheral.reshape(own_count, block_size, width)
    all_to_all = functools.partial(
        lax.all_to_all, axis_name="dev", split_axis=0, concat_axis=0, tiled=True
    )

    outgoing = pack(send_list, own)
    pieces = gather_far(hubs, digits)
    outgoing, *pieces = lax.optimization_barrier((outgoing, *pieces))
    incoming = all_to_all(outgoing)
    halves = gather_near(pieces, digits)
    hub_table, mine, kept, sent = hub_first(
        digits, rows, cols, tile_count, me, place_col, halves, own, tiles, local
    )
    base, done = before(0, rows, cols, tile_count, hub_table, own, tiles, w_in, w_out)
    kept, received = scatter_near(me, kept, sent, digits, local)
    base, done, *received = lax.optimization_barrier((base, done, *received))
    parts = scatter_far(me, kept, received, digits, local)
    hub_new = hub_network(0, mine, parts, w_in, w_out)
    own, outgoing = after(
        0, rows, send_list, base, done, incoming, tiles, w_in, w_out, hub_count, True
    )

    pieces = gather_far(hub_new, digits)
    outgoing, *pieces = lax.optimization_barrier((outgoing, *pieces))
    incoming = all_to_all(outgoing)
    halves = gather_near(pieces, digits)
    hub_table, mine, kept, sent = hub_second(
        digits, rows, cols, tile_count, me, place_row, halves, own, tiles, local
    )
    base, done = before(1, rows, cols, tile_count, hub_table, own, tiles, w_in, w_out)
    kept, received = scatter_near(me, kept, sent, digits, local)
    base, done, *received = lax.optimization_barrier((base, done, *received))
    parts = scatter_far(me, kept, received, digits, local)
    hub_out = hub_network(1, mine, parts, w_in, w_out)
    (peri_out,) = after(
        1, rows, send_list, base, done, incoming, tiles, w_in, w_out, hub_count, False
    )
    return (peri_out.reshape(peripheral.shape), hub_out)


def solution(mesh):
    in_specs = (
        P("dev", None),
        P("dev", None),
        P("dev", None, None),
        P("dev"),
        P("dev"),
        P("dev"),
        P("dev", None),
        P(),
        P(),
        P(),
    )
    out_specs = (P("dev", None), P("dev", None))
    return jax.shard_map(body, mesh=mesh, in_specs=in_specs, out_specs=out_specs, check_vma=False)
```

```python
import functools

import jax
import jax.numpy as jnp
from jax import lax
from jax.experimental import pallas as pl
from jax.experimental.pallas import tpu as pltpu
from jax.sharding import PartitionSpec as P

epsilon = 1e-06
f32 = jnp.float32
bf16 = jnp.bfloat16
MIB = 1024 * 1024
VMEM = pl.BlockSpec(memory_space=pltpu.VMEM)
SMEM = pl.BlockSpec(memory_space=pltpu.SMEM)
ANY = pl.BlockSpec(memory_space=pl.ANY)
GROUP = 4


def dot(a, b):
    return jnp.dot(a, b, preferred_element_type=f32)


def shape_of(shape, dtype):
    return jax.ShapeDtypeStruct(tuple(shape), dtype)


def call(kernel, name, mib, flops, moved, out_shape, in_specs, out_specs, scratch, args):
    return pl.pallas_call(
        kernel,
        out_shape=out_shape,
        in_specs=in_specs,
        out_specs=out_specs,
        scratch_shapes=scratch,
        compiler_params=pltpu.CompilerParams(vmem_limit_bytes=mib * MIB),
        cost_estimate=pl.CostEstimate(flops=flops, bytes_accessed=moved, transcendentals=0),
        name=name,
    )(*args)


def normalise(u):
    return (u * lax.rsqrt(jnp.mean(u * u, axis=-1, keepdims=True) + epsilon)).astype(bf16)


def network(u, first, second, hidden_step):
    normed = normalise(u)
    total = u
    for start in range(0, first.shape[-1], hidden_step):
        cut = slice(start, start + hidden_step)
        hidden = jnp.maximum(dot(normed, first[:, cut]), 0.0).astype(bf16)
        total = total + dot(hidden, second[cut, :])
    return total.astype(bf16)


def list_slots(rows, count, picked, begin, hub_count, want_hub):
    def step(slot, found):
        picked[found] = slot
        is_hub = (rows[slot] < hub_count).astype(jnp.int32)
        return found + (is_hub if want_hub else 1 - is_hub)

    return lax.fori_loop(begin, count[0], step, jnp.int32(0))


def start_tiles(picked, found, source, tiles, sems):
    def step(place, unused):
        pltpu.make_async_copy(source.at[picked[place]], tiles.at[place], sems.at[place]).start()
        return unused

    lax.fori_loop(0, found, step, 0)


def wait_tiles(picked, found, source, tiles, sems):
    def step(place, unused):
        pltpu.make_async_copy(source.at[picked[place]], tiles.at[place], sems.at[place]).wait()
        return unused

    lax.fori_loop(0, found, step, 0)


def add_products(rows, cols, picked, found, begin, tiles, hubs, own, total, shift, spare):
    hub_count = hubs.shape[0]

    def step(number, unused):
        where, products = [], []
        for lane in range(GROUP):
            place = number * GROUP + lane
            live = place < found
            place = jnp.minimum(place, found - 1)
            slot = picked[place]
            where.append(jnp.where(live, rows[slot] - shift, spare))
            col = cols[slot - begin]
            of_hub = hubs[jnp.minimum(col, hub_count - 1)]
            of_own = own[jnp.maximum(col - hub_count, 0)]
            products.append(dot(tiles[place], jnp.where(col < hub_count, of_hub, of_own)))
        for row, product in zip(where, products):
            total[row] += product
        return unused

    lax.fori_loop(0, (found + GROUP - 1) // GROUP, step, 0)


def each_block(listed, found, copy_of, act):
    def step(number, unused):
        act(copy_of(listed[number]))
        return unused

    lax.fori_loop(0, found, step, 0)


def start(copy):
    copy.start()


def wait(copy):
    copy.wait()


def list_blocks(rows, remote, own_count, hub_count, marks, fed, free):
    def clear(block, unused):
        marks[block] = 0
        return unused

    def mark(slot, unused):
        marks[rows[slot] - hub_count] = 1
        return unused

    def take(block, found):
        fed[found] = block
        free[block - found] = block
        return found + marks[block]

    lax.fori_loop(0, own_count, clear, 0)
    lax.fori_loop(0, remote, mark, 0)
    found = lax.fori_loop(0, own_count, take, jnp.int32(0))
    return found, own_count - found


def network_blocks(listed, found, read, first, second, result, finish):
    size = result.shape[1]

    def step(number, unused):
        blocks = [
            listed[jnp.minimum(number * GROUP + lane, found - 1)] for lane in range(GROUP)
        ]
        values = jnp.concatenate([read(block) for block in blocks], axis=0)
        values = network(values, first, second, 512)
        for lane, block in enumerate(blocks):
            result[block] = values[lane * size : (lane + 1) * size]
        for lane, block in enumerate(blocks):

            @pl.when(number * GROUP + lane < found)
            def _(block=block):
                finish(block).start()

        return unused

    lax.fori_loop(0, (found + GROUP - 1) // GROUP, step, 0)


def pack_kernel(chosen, blocks, outgoing, held, sems):
    load = pltpu.make_async_copy(blocks, held, sems.at[0])
    load.start()
    load.wait()
    copies = []
    for number in range(outgoing.shape[0]):
        copy = pltpu.make_async_copy(
            held.at[chosen[0, number]], outgoing.at[number], sems.at[number]
        )
        copy.start()
        copies.append(copy)
    for copy in copies:
        copy.wait()


def pack(chosen, blocks):
    devices = chosen.shape[1]
    return call(
        pack_kernel,
        "pack",
        58,
        0,
        2 * blocks.size * 2,
        shape_of((devices,) + blocks.shape[1:], bf16),
        [SMEM, ANY],
        ANY,
        [pltpu.VMEM(blocks.shape, bf16), pltpu.SemaphoreType.DMA((devices,))],
        (chosen, blocks),
    )


def slot_place(slot, digits):
    place, weight = 0, 1
    for bit, radix in digits[:0:-1]:
        place += weight * ((slot // bit) % radix)
        weight *= radix
    return slot % 2, place


def place_shards(me, halves, table, digits, local):
    for slot in range(table.shape[0] // local):
        half, place = slot_place(slot, digits)
        start = pl.multiple_of((me ^ slot) * local, local)
        table[pl.ds(start, local), :] = halves[half][place * local : (place + 1) * local, :]


def split_sums(me, sums, local, kept, sent):
    odd = me % 2
    width = sums.shape[-1]
    pairs = sums.reshape(-1, 2, local, width)
    kept[...] = jnp.where(odd == 1, pairs[:, 1], pairs[:, 0]).reshape(kept.shape).astype(kept.dtype)
    sent[...] = jnp.where(odd == 1, pairs[:, 0], pairs[:, 1]).reshape(sent.shape).astype(sent.dtype)


def hub_first_kernel(
    digits, rows, cols, count, position, place_col, half0, half1, own_hbm, tiles_hbm,
    hubs, mine, kept, sent, own, tiles, table, total, picked, sems,
):
    hub_count, block_size, width = hubs.shape
    hub_rows = hub_count * block_size
    local = mine.shape[0]
    begin = rows.shape[0] - cols.shape[0]
    found = list_slots(rows, count, picked, begin, hub_count, True)
    start_tiles(picked, found, tiles_hbm, tiles, sems)
    load = pltpu.make_async_copy(own_hbm, own, sems.at[cols.shape[0]])
    load.start()
    me = position[0]
    place_shards(me, (half0, half1), table, digits, local)
    total[...] = jnp.zeros_like(total)
    step = 2 * block_size

    def rows_step(number, unused):
        cut = pl.ds(pl.multiple_of(number * step, step), step)
        lanes = lax.broadcasted_iota(jnp.int32, (step, hub_rows), 1)
        unit = jnp.where(place_col[cut, :] == lanes, 1.0, 0.0).astype(bf16)
        placed = dot(unit, table[...]).astype(bf16)
        hubs[pl.ds(number * 2, 2)] = placed.reshape(2, block_size, width)
        return unused

    lax.fori_loop(0, hub_rows // step, rows_step, 0)
    load.wait()
    wait_tiles(picked, found, tiles_hbm, tiles, sems)
    add_products(rows, cols, picked, found, begin, tiles, hubs, own, total, 0, hub_count)
    split_sums(me, total[:hub_count], local, kept, sent)
    flat = hubs.reshape(hub_rows, width)
    mine[...] = flat[pl.ds(pl.multiple_of(me * local, local), local), :]


def hub_first(digits, rows, cols, count, position, place_col, halves, own, tiles, local):
    block_size, width = own.shape[1:]
    hub_rows = place_col.shape[0]
    hub_count = hub_rows // block_size
    half = shape_of((hub_rows // 2, width), f32)
    return call(
        functools.partial(hub_first_kernel, digits),
        "hub_first",
        54,
        2 * hub_rows * hub_rows * width,
        14 * MIB,
        (
            shape_of((hub_count, block_size, width), bf16),
            shape_of((local, width), bf16),
            half,
            half,
        ),
        [SMEM] * 4 + [VMEM] * 3 + [ANY] * 2,
        (VMEM,) * 4,
        [
            pltpu.VMEM(own.shape, bf16),
            pltpu.VMEM((cols.shape[0],) + tiles.shape[1:], bf16),
            pltpu.VMEM((hub_rows, width), bf16),
            pltpu.VMEM((hub_count + 1, block_size, width), f32),
            pltpu.SMEM((rows.shape[0],), jnp.int32),
            pltpu.SemaphoreType.DMA((cols.shape[0] + 1,)),
        ],
        (rows, cols, count, position, place_col) + tuple(halves) + (own, tiles),
    )


def hub_second_kernel(
    digits, rows, cols, count, position, place_row, half0, half1, own_hbm, tiles_hbm,
    hubs, mine, kept, sent, own, tiles, total, placed, picked, sems,
):
    hub_count, block_size, width = hubs.shape
    hub_rows = hub_count * block_size
    local = mine.shape[0]
    begin = rows.shape[0] - cols.shape[0]
    found = list_slots(rows, count, picked, begin, hub_count, True)
    start_tiles(picked, found, tiles_hbm, tiles, sems)
    load = pltpu.make_async_copy(own_hbm, own, sems.at[cols.shape[0]])
    load.start()
    me = position[0]
    flat = hubs.reshape(hub_rows, width)
    place_shards(me, (half0, half1), flat, digits, local)
    total[...] = jnp.zeros_like(total)

    def unit_rows(start, step):
        down = lax.broadcasted_iota(jnp.int32, (step, hub_rows), 0) + start
        return jnp.where(place_row[...] == down, 1.0, 0.0).astype(bf16)

    mine[...] = dot(unit_rows(me * local, local), flat[...]).astype(bf16)
    load.wait()
    wait_tiles(picked, found, tiles_hbm, tiles, sems)
    add_products(rows, cols, picked, found, begin, tiles, hubs, own, total, 0, hub_count)
    sums = total[:hub_count].astype(bf16).reshape(hub_rows, width)
    step = 2 * block_size

    def rows_step(number, unused):
        start = number * step
        placed[pl.ds(pl.multiple_of(start, step), step), :] = dot(unit_rows(start, step), sums)
        return unused

    lax.fori_loop(0, hub_rows // step, rows_step, 0)
    split_sums(me, placed[...], local, kept, sent)


def hub_second(digits, rows, cols, count, position, place_row, halves, own, tiles, local):
    block_size, width = own.shape[1:]
    hub_rows = place_row.shape[1]
    hub_count = hub_rows // block_size
    return call(
        functools.partial(hub_second_kernel, digits),
        "hub_second",
        54,
        2 * hub_rows * hub_rows * width,
        14 * MIB,
        (
            shape_of((hub_count, block_size, width), bf16),
            shape_of((local, width), bf16),
            shape_of((hub_rows // 2, width), f32),
            shape_of((hub_rows // 2, width), bf16),
        ),
        [SMEM] * 4 + [VMEM] * 3 + [ANY] * 2,
        (VMEM,) * 4,
        [
            pltpu.VMEM(own.shape, bf16),
            pltpu.VMEM((cols.shape[0],) + tiles.shape[1:], bf16),
            pltpu.VMEM((hub_count + 1, block_size, width), f32),
            pltpu.VMEM((hub_rows, width), f32),
            pltpu.SMEM((rows.shape[0],), jnp.int32),
            pltpu.SemaphoreType.DMA((cols.shape[0] + 1,)),
        ],
        (rows, cols, count, position, place_row) + tuple(halves) + (own, tiles),
    )


def combine(position, kept, received, bit, radix, local, sent_type):
    rows = kept.shape[0] // radix
    width = kept.shape[1]

    def kernel(position, kept_in, *refs):
        received, outs = refs[: -radix], refs[-radix:]
        total = kept_in[...].astype(f32)
        for part in received:
            total = total + part[...].astype(f32)
        digit = (position[0] // bit) % radix
        parts = total.reshape(rows // local, radix, local, width)
        for offset, out in enumerate(outs):
            value = parts[:, 0]
            for number in range(1, radix):
                value = jnp.where((digit ^ offset) == number, parts[:, number], value)
            out[...] = value.reshape(rows, width).astype(out.dtype)

    shapes = [shape_of((rows, width), f32)] + [shape_of((rows, width), sent_type)] * (radix - 1)
    return call(
        kernel,
        "combine",
        16,
        kept.size,
        12 * kept.size,
        tuple(shapes),
        [SMEM] + [VMEM] * (1 + len(received)),
        (VMEM,) * radix,
        [],
        (position, kept) + tuple(received),
    )


def load_weights(layer, first_in, second_in, first, second, sems):
    loads = [
        pltpu.make_async_copy(first_in.at[layer], first, sems.at[0]),
        pltpu.make_async_copy(second_in.at[layer], second, sems.at[1]),
    ]
    for load in loads:
        load.start()
    return loads


def hub_network_kernel(layer, rows_in, *refs):
    parts, (first_in, second_in, out, first, second, sems) = refs[:-6], refs[-6:]
    loads = load_weights(layer, first_in, second_in, first, second, sems)
    u = rows_in[...].astype(f32)
    for part in parts:
        u = u + part[...].astype(f32)
    for load in loads:
        load.wait()
    out[...] = network(u, first, second, first.shape[-1])


def hub_network(layer, rows_in, parts, first, second):
    return call(
        functools.partial(hub_network_kernel, layer),
        "hub_network",
        24,
        4 * rows_in.size * first.shape[-1],
        2 * first.size,
        shape_of(rows_in.shape, bf16),
        [VMEM] * (1 + len(parts)) + [ANY] * 2,
        VMEM,
        [
            pltpu.VMEM(first.shape[1:], bf16),
            pltpu.VMEM(second.shape[1:], bf16),
            pltpu.SemaphoreType.DMA((2,)),
        ],
        (rows_in,) + tuple(parts) + (first, second),
    )


def before_kernel(
    layer, rows, cols, count, hubs_in, own_in, tiles_in, first_in, second_in, base, out,
    hubs, own, tiles, first, second, u, result, picked, marks, fed, free, sems, block_sems, sem,
):
    own_count = own.shape[0]
    hub_count = hubs.shape[0]
    begin = rows.shape[0] - cols.shape[0]
    load_own = pltpu.make_async_copy(own_in, own, sem.at[0])
    load_hubs = pltpu.make_async_copy(hubs_in, hubs, sem.at[1])
    load_own.start()
    load_hubs.start()
    found = list_slots(rows, count, picked, begin, hub_count, False)
    start_tiles(picked, found, tiles_in, tiles, sems)
    n_fed, n_free = list_blocks(rows, begin, own_count, hub_count, marks, fed, free)
    load_own.wait()
    u[:own_count] = own[...].astype(f32)
    load_hubs.wait()
    wait_tiles(picked, found, tiles_in, tiles, sems)
    loads = load_weights(layer, first_in, second_in, first, second, sem.at[pl.ds(2, 2)])
    add_products(rows, cols, picked, found, begin, tiles, hubs, own, u, hub_count, own_count)
    for load in loads:
        load.wait()

    def save(block):
        return pltpu.make_async_copy(u.at[block], base.at[block], block_sems.at[block])

    def finish(block):
        return pltpu.make_async_copy(result.at[block], out.at[block], block_sems.at[block])

    each_block(fed, n_fed, save, start)
    network_blocks(free, n_free, lambda block: u[block], first, second, result, finish)
    each_block(fed, n_fed, save, wait)
    each_block(free, n_free, finish, wait)


def before(layer, rows, cols, count, hubs, own, tiles, first, second):
    own_count, block_size, width = own.shape
    return call(
        functools.partial(before_kernel, layer),
        "before",
        58,
        4 * own.size * first.shape[-1] // 3,
        18 * MIB,
        (shape_of(own.shape, f32), shape_of(own.shape, bf16)),
        [SMEM] * 3 + [ANY] * 5,
        (ANY, ANY),
        [
            pltpu.VMEM(hubs.shape, bf16),
            pltpu.VMEM(own.shape, bf16),
            pltpu.VMEM((cols.shape[0],) + tiles.shape[1:], bf16),
            pltpu.VMEM(first.shape[1:], bf16),
            pltpu.VMEM(second.shape[1:], bf16),
            pltpu.VMEM((own_count + 1, block_size, width), f32),
            pltpu.VMEM(own.shape, bf16),
            pltpu.SMEM((rows.shape[0],), jnp.int32),
            pltpu.SMEM((own_count,), jnp.int32),
            pltpu.SMEM((own_count,), jnp.int32),
            pltpu.SMEM((own_count,), jnp.int32),
            pltpu.SemaphoreType.DMA((cols.shape[0],)),
            pltpu.SemaphoreType.DMA((own_count,)),
            pltpu.SemaphoreType.DMA((4,)),
        ],
        (rows, cols, count, hubs, own, tiles, first, second),
    )


def after_kernel(
    layer, with_send, hub_count, rows, chosen, base, done, incoming, tiles, first_in, second_in, *refs
):
    out, refs = refs[0], refs[1:]
    if with_send:
        outgoing, refs = refs[0], refs[1:]
    u, extra, inc, adj, first, second, result, marks, fed, free, block_sems, out_sems, sem = refs
    own_count = u.shape[0]
    remote = incoming.shape[0]
    parts = 4
    size = remote // parts
    loads = []
    for part in range(parts):
        cut = pl.ds(part * size, size)
        loads.append(
            (
                pltpu.make_async_copy(tiles.at[cut], adj.at[cut], sem.at[2 + 2 * part]),
                pltpu.make_async_copy(incoming.at[cut], inc.at[cut], sem.at[3 + 2 * part]),
            )
        )
        for load in loads[-1]:
            load.start()

    def load_base(block):
        return pltpu.make_async_copy(base.at[block], u.at[block], block_sems.at[block])

    def load_done(block):
        return pltpu.make_async_copy(done.at[block], result.at[block], block_sems.at[block])

    def finish(block):
        return pltpu.make_async_copy(result.at[block], out.at[block], out_sems.at[block])

    extra[...] = jnp.zeros_like(extra)
    n_fed, n_free = list_blocks(rows, remote, own_count, hub_count, marks, fed, free)
    for part in range(parts):
        for load in loads[part]:
            load.wait()
        if part == 0:
            weights = load_weights(layer, first_in, second_in, first, second, sem.at[pl.ds(0, 2)])
            each_block(fed, n_fed, load_base, start)
            if with_send:
                each_block(free, n_free, load_done, start)
        products = [dot(adj[slot], inc[slot]) for slot in range(part * size, (part + 1) * size)]
        for lane, product in enumerate(products):
            extra[rows[part * size + lane] - hub_count] += product
    each_block(fed, n_fed, load_base, wait)
    for load in weights:
        load.wait()
    network_blocks(
        fed, n_fed, lambda block: u[block] + extra[block], first, second, result, finish
    )
    copies = []
    if with_send:
        each_block(free, n_free, load_done, wait)
        for number in range(remote):
            copy = pltpu.make_async_copy(
                result.at[chosen[0, number]], outgoing.at[number], sem.at[number]
            )
            copy.start()
            copies.append(copy)
    each_block(fed, n_fed, finish, wait)
    for copy in copies:
        copy.wait()


def after(layer, rows, chosen, base, done, incoming, tiles, first, second, hub_count, with_send):
    own_count = base.shape[0]
    remote = incoming.shape[0]
    shapes = [shape_of(base.shape, bf16)]
    if with_send:
        shapes.append(shape_of(incoming.shape, bf16))
    return pl.pallas_call(
        functools.partial(after_kernel, layer, with_send, hub_count),
        out_shape=tuple(shapes),
        in_specs=[SMEM, SMEM] + [ANY] * 6,
        out_specs=(ANY,) * len(shapes),
        scratch_shapes=[
            pltpu.VMEM(base.shape, f32),
            pltpu.VMEM(base.shape, f32),
            pltpu.VMEM(incoming.shape, bf16),
            pltpu.VMEM((remote,) + tiles.shape[1:], bf16),
            pltpu.VMEM(first.shape[1:], bf16),
            pltpu.VMEM(second.shape[1:], bf16),
            pltpu.VMEM(base.shape, bf16),
            pltpu.SMEM((own_count,), jnp.int32),
            pltpu.SMEM((own_count,), jnp.int32),
            pltpu.SMEM((own_count,), jnp.int32),
            pltpu.SemaphoreType.DMA((own_count,)),
            pltpu.SemaphoreType.DMA((own_count,)),
            pltpu.SemaphoreType.DMA((max(10, remote),)),
        ],
        input_output_aliases={3: 0},
        compiler_params=pltpu.CompilerParams(vmem_limit_bytes=58 * MIB),
        cost_estimate=pl.CostEstimate(
            flops=4 * base.size * first.shape[-1], bytes_accessed=16 * MIB, transcendentals=0
        ),
        name="after",
    )(rows, chosen, base, done, incoming, tiles, first, second)


def exchange(x, bit):
    devices = lax.axis_size("dev")
    return lax.ppermute(x, "dev", [(i, i ^ bit) for i in range(devices)])


def all_digits():
    devices = lax.axis_size("dev")
    digits, bit = [(1, 2)], 2
    while bit < devices:
        radix = 4 if 4 * bit <= devices else 2
        digits.append((bit, radix))
        bit *= radix
    return digits


def gather_step(x, bit, radix):
    return [x] + [exchange(x, bit * offset) for offset in range(1, radix)]


def gather_far(x, digits):
    return gather_step(x, *digits[-1])


def gather_near(pieces, digits):
    for digit in digits[-2:0:-1]:
        pieces = gather_step(jnp.concatenate(pieces, axis=0), *digit)
    return pieces


def gather_last(pieces, digits):
    x = jnp.concatenate(pieces, axis=0)
    return x, exchange(x, digits[0][0])


def scatter_near(position, kept, sent, digits, local):
    received = [exchange(sent, digits[0][0])]
    for bit, radix in digits[1:-1]:
        kept, *sent = combine(position, kept, received, bit, radix, local, bf16)
        received = [exchange(part, bit * (1 + number)) for number, part in enumerate(sent)]
    return kept, received


def scatter_far(position, kept, received, digits, local):
    bit, radix = digits[-1]
    kept, *sent = combine(position, kept, received, bit, radix, local, f32)
    return [kept] + [exchange(part, bit * (1 + number)) for number, part in enumerate(sent)]


def body(
    peripheral, hubs, tiles, tile_rows, local_cols, tile_count, send_list, hub_place, w_in, w_out
):
    position = lax.axis_index("dev")
    digits = all_digits()
    block_size = tiles.shape[1]
    width = peripheral.shape[1]
    own_count = peripheral.shape[0] // block_size
    hub_rows = hub_place.shape[0]
    hub_count = hub_rows // block_size
    local = hubs.shape[0]
    rows = jnp.where(tile_rows < hub_count, tile_rows, tile_rows - position * own_count)
    cols = jnp.where(local_cols < hub_count, local_cols, local_cols - position * own_count)
    place_col = hub_place.reshape(hub_rows, 1)
    place_row = hub_place.reshape(1, hub_rows)
    me = position.astype(jnp.int32).reshape(1)
    own = peripheral.reshape(own_count, block_size, width)
    all_to_all = functools.partial(
        lax.all_to_all, axis_name="dev", split_axis=0, concat_axis=0, tiled=True
    )

    outgoing = pack(send_list, own)
    pieces = gather_far(hubs, digits)
    outgoing, *pieces = lax.optimization_barrier((outgoing, *pieces))
    incoming = all_to_all(outgoing)
    pieces = gather_near(pieces, digits)
    rows, cols, place_col, *pieces = lax.optimization_barrier((rows, cols, place_col, *pieces))
    halves = gather_last(pieces, digits)
    hub_table, mine, kept, sent = hub_first(
        digits, rows, cols, tile_count, me, place_col, halves, own, tiles, local
    )
    base, done = before(0, rows, cols, tile_count, hub_table, own, tiles, w_in, w_out)
    kept, received = scatter_near(me, kept, sent, digits, local)
    base, done, *received = lax.optimization_barrier((base, done, *received))
    parts = scatter_far(me, kept, received, digits, local)
    hub_new = hub_network(0, mine, parts, w_in, w_out)
    own, outgoing = after(
        0, rows, send_list, base, done, incoming, tiles, w_in, w_out, hub_count, True
    )

    pieces = gather_far(hub_new, digits)
    outgoing, *pieces = lax.optimization_barrier((outgoing, *pieces))
    incoming = all_to_all(outgoing)
    halves = gather_last(gather_near(pieces, digits), digits)
    hub_table, mine, kept, sent = hub_second(
        digits, rows, cols, tile_count, me, place_row, halves, own, tiles, local
    )
    base, done = before(1, rows, cols, tile_count, hub_table, own, tiles, w_in, w_out)
    kept, received = scatter_near(me, kept, sent, digits, local)
    base, done, *received = lax.optimization_barrier((base, done, *received))
    parts = scatter_far(me, kept, received, digits, local)
    hub_out = hub_network(1, mine, parts, w_in, w_out)
    (peri_out,) = after(
        1, rows, send_list, base, done, incoming, tiles, w_in, w_out, hub_count, False
    )
    return (peri_out.reshape(peripheral.shape), hub_out)


def solution(mesh):
    in_specs = (
        P("dev", None),
        P("dev", None),
        P("dev", None, None),
        P("dev"),
        P("dev"),
        P("dev"),
        P("dev", None),
        P(),
        P(),
        P(),
    )
    out_specs = (P("dev", None), P("dev", None))
    return jax.shard_map(body, mesh=mesh, in_specs=in_specs, out_specs=out_specs, check_vma=False)
```

```python
import functools

import jax
import jax.numpy as jnp
from jax import lax
from jax.experimental import pallas as pl
from jax.experimental.pallas import tpu as pltpu
from jax.sharding import PartitionSpec as P

epsilon = 1e-06
f32 = jnp.float32
bf16 = jnp.bfloat16
MIB = 1024 * 1024
VMEM = pl.BlockSpec(memory_space=pltpu.VMEM)
SMEM = pl.BlockSpec(memory_space=pltpu.SMEM)
ANY = pl.BlockSpec(memory_space=pl.ANY)
GROUP = 4


def dot(a, b):
    return jnp.dot(a, b, preferred_element_type=f32)


def shape_of(shape, dtype):
    return jax.ShapeDtypeStruct(tuple(shape), dtype)


def call(kernel, name, mib, flops, moved, out_shape, in_specs, out_specs, scratch, args):
    return pl.pallas_call(
        kernel,
        out_shape=out_shape,
        in_specs=in_specs,
        out_specs=out_specs,
        scratch_shapes=scratch,
        compiler_params=pltpu.CompilerParams(vmem_limit_bytes=mib * MIB),
        cost_estimate=pl.CostEstimate(flops=flops, bytes_accessed=moved, transcendentals=0),
        name=name,
    )(*args)


def normalise(u):
    return (u * lax.rsqrt(jnp.mean(u * u, axis=-1, keepdims=True) + epsilon)).astype(bf16)


def network(u, first, second, hidden_step):
    normed = normalise(u)
    total = u
    for start in range(0, first.shape[-1], hidden_step):
        cut = slice(start, start + hidden_step)
        hidden = jnp.maximum(dot(normed, first[:, cut]), 0.0).astype(bf16)
        total = total + dot(hidden, second[cut, :])
    return total.astype(bf16)


def list_slots(rows, count, picked, begin, hub_count, want_hub):
    def step(slot, found):
        picked[found] = slot
        is_hub = (rows[slot] < hub_count).astype(jnp.int32)
        return found + (is_hub if want_hub else 1 - is_hub)

    return lax.fori_loop(begin, count[0], step, jnp.int32(0))


def start_tiles(picked, found, source, tiles, sems):
    def step(place, unused):
        pltpu.make_async_copy(source.at[picked[place]], tiles.at[place], sems.at[place]).start()
        return unused

    lax.fori_loop(0, found, step, 0)


def wait_tiles(picked, found, source, tiles, sems):
    def step(place, unused):
        pltpu.make_async_copy(source.at[picked[place]], tiles.at[place], sems.at[place]).wait()
        return unused

    lax.fori_loop(0, found, step, 0)


def add_products(rows, cols, picked, found, begin, tiles, hubs, own, total, shift, spare):
    hub_count = hubs.shape[0]

    def step(number, unused):
        where, products = [], []
        for lane in range(GROUP):
            place = number * GROUP + lane
            live = place < found
            place = jnp.minimum(place, found - 1)
            slot = picked[place]
            where.append(jnp.where(live, rows[slot] - shift, spare))
            col = cols[slot - begin]
            of_hub = hubs[jnp.minimum(col, hub_count - 1)]
            of_own = own[jnp.maximum(col - hub_count, 0)]
            products.append(dot(tiles[place], jnp.where(col < hub_count, of_hub, of_own)))
        for row, product in zip(where, products):
            total[row] += product
        return unused

    lax.fori_loop(0, (found + GROUP - 1) // GROUP, step, 0)


def each_block(listed, found, copy_of, act):
    def step(number, unused):
        act(copy_of(listed[number]))
        return unused

    lax.fori_loop(0, found, step, 0)


def start(copy):
    copy.start()


def wait(copy):
    copy.wait()


def list_blocks(rows, remote, own_count, hub_count, marks, fed, free):
    def clear(block, unused):
        marks[block] = 0
        return unused

    def mark(slot, unused):
        marks[rows[slot] - hub_count] = 1
        return unused

    def take(block, found):
        fed[found] = block
        free[block - found] = block
        return found + marks[block]

    lax.fori_loop(0, own_count, clear, 0)
    lax.fori_loop(0, remote, mark, 0)
    found = lax.fori_loop(0, own_count, take, jnp.int32(0))
    return found, own_count - found


def network_blocks(listed, found, read, first, second, result, finish):
    size = result.shape[1]

    def step(number, unused):
        blocks = [
            listed[jnp.minimum(number * GROUP + lane, found - 1)] for lane in range(GROUP)
        ]
        values = jnp.concatenate([read(block) for block in blocks], axis=0)
        values = network(values, first, second, 512)
        for lane, block in enumerate(blocks):
            result[block] = values[lane * size : (lane + 1) * size]
        for lane, block in enumerate(blocks):

            @pl.when(number * GROUP + lane < found)
            def _(block=block):
                finish(block).start()

        return unused

    lax.fori_loop(0, (found + GROUP - 1) // GROUP, step, 0)


def pack_kernel(chosen, blocks, outgoing, held, sems):
    load = pltpu.make_async_copy(blocks, held, sems.at[0])
    load.start()
    load.wait()
    copies = []
    for number in range(outgoing.shape[0]):
        copy = pltpu.make_async_copy(
            held.at[chosen[0, number]], outgoing.at[number], sems.at[number]
        )
        copy.start()
        copies.append(copy)
    for copy in copies:
        copy.wait()


def pack(chosen, blocks):
    devices = chosen.shape[1]
    return call(
        pack_kernel,
        "pack",
        58,
        0,
        2 * blocks.size * 2,
        shape_of((devices,) + blocks.shape[1:], bf16),
        [SMEM, ANY],
        ANY,
        [pltpu.VMEM(blocks.shape, bf16), pltpu.SemaphoreType.DMA((devices,))],
        (chosen, blocks),
    )


def slot_place(slot, digits):
    place, weight = 0, 1
    for bit, radix in digits[:0:-1]:
        place += weight * ((slot // bit) % radix)
        weight *= radix
    return slot % 2, place


def place_shards(me, halves, table, digits, local):
    for slot in range(table.shape[0] // local):
        half, place = slot_place(slot, digits)
        start = pl.multiple_of((me ^ slot) * local, local)
        table[pl.ds(start, local), :] = halves[half][place * local : (place + 1) * local, :]


def split_sums(me, sums, local, kept, sent):
    odd = me % 2
    width = sums.shape[-1]
    pairs = sums.reshape(-1, 2, local, width)
    kept[...] = jnp.where(odd == 1, pairs[:, 1], pairs[:, 0]).reshape(kept.shape).astype(kept.dtype)
    sent[...] = jnp.where(odd == 1, pairs[:, 0], pairs[:, 1]).reshape(sent.shape).astype(sent.dtype)


def hub_first_kernel(
    digits, rows, cols, count, position, place_col, half0, half1, own_hbm, tiles_hbm,
    hubs, mine, kept, sent, own, tiles, table, total, picked, sems,
):
    hub_count, block_size, width = hubs.shape
    hub_rows = hub_count * block_size
    local = mine.shape[0]
    begin = rows.shape[0] - cols.shape[0]
    found = list_slots(rows, count, picked, begin, hub_count, True)
    start_tiles(picked, found, tiles_hbm, tiles, sems)
    load = pltpu.make_async_copy(own_hbm, own, sems.at[cols.shape[0]])
    load.start()
    me = position[0]
    place_shards(me, (half0, half1), table, digits, local)
    total[...] = jnp.zeros_like(total)
    step = 2 * block_size

    def rows_step(number, unused):
        cut = pl.ds(pl.multiple_of(number * step, step), step)
        lanes = lax.broadcasted_iota(jnp.int32, (step, hub_rows), 1)
        unit = jnp.where(place_col[cut, :] == lanes, 1.0, 0.0).astype(bf16)
        placed = dot(unit, table[...]).astype(bf16)
        hubs[pl.ds(number * 2, 2)] = placed.reshape(2, block_size, width)
        return unused

    lax.fori_loop(0, hub_rows // step, rows_step, 0)
    load.wait()
    wait_tiles(picked, found, tiles_hbm, tiles, sems)
    add_products(rows, cols, picked, found, begin, tiles, hubs, own, total, 0, hub_count)
    split_sums(me, total[:hub_count], local, kept, sent)
    flat = hubs.reshape(hub_rows, width)
    mine[...] = flat[pl.ds(pl.multiple_of(me * local, local), local), :]


def hub_first(digits, rows, cols, count, position, place_col, halves, own, tiles, local):
    block_size, width = own.shape[1:]
    hub_rows = place_col.shape[0]
    hub_count = hub_rows // block_size
    half = shape_of((hub_rows // 2, width), f32)
    return call(
        functools.partial(hub_first_kernel, digits),
        "hub_first",
        48,
        2 * hub_rows * hub_rows * width,
        14 * MIB,
        (
            shape_of((hub_count, block_size, width), bf16),
            shape_of((local, width), bf16),
            half,
            half,
        ),
        [SMEM] * 4 + [VMEM] * 3 + [ANY] * 2,
        (VMEM,) * 4,
        [
            pltpu.VMEM(own.shape, bf16),
            pltpu.VMEM((cols.shape[0],) + tiles.shape[1:], bf16),
            pltpu.VMEM((hub_rows, width), bf16),
            pltpu.VMEM((hub_count + 1, block_size, width), f32),
            pltpu.SMEM((rows.shape[0],), jnp.int32),
            pltpu.SemaphoreType.DMA((cols.shape[0] + 1,)),
        ],
        (rows, cols, count, position, place_col) + tuple(halves) + (own, tiles),
    )


def hub_second_kernel(
    digits, rows, cols, count, position, place_row, half0, half1, own_hbm, tiles_hbm,
    hubs, mine, kept, sent, own, tiles, total, placed, picked, sems,
):
    hub_count, block_size, width = hubs.shape
    hub_rows = hub_count * block_size
    local = mine.shape[0]
    begin = rows.shape[0] - cols.shape[0]
    found = list_slots(rows, count, picked, begin, hub_count, True)
    start_tiles(picked, found, tiles_hbm, tiles, sems)
    load = pltpu.make_async_copy(own_hbm, own, sems.at[cols.shape[0]])
    load.start()
    me = position[0]
    flat = hubs.reshape(hub_rows, width)
    place_shards(me, (half0, half1), flat, digits, local)
    total[...] = jnp.zeros_like(total)

    def unit_rows(start, step):
        down = lax.broadcasted_iota(jnp.int32, (step, hub_rows), 0) + start
        return jnp.where(place_row[...] == down, 1.0, 0.0).astype(bf16)

    mine[...] = dot(unit_rows(me * local, local), flat[...]).astype(bf16)
    load.wait()
    wait_tiles(picked, found, tiles_hbm, tiles, sems)
    add_products(rows, cols, picked, found, begin, tiles, hubs, own, total, 0, hub_count)
    sums = total[:hub_count].astype(bf16).reshape(hub_rows, width)
    step = 2 * block_size

    def rows_step(number, unused):
        start = number * step
        placed[pl.ds(pl.multiple_of(start, step), step), :] = dot(unit_rows(start, step), sums)
        return unused

    lax.fori_loop(0, hub_rows // step, rows_step, 0)
    split_sums(me, placed[...], local, kept, sent)


def hub_second(digits, rows, cols, count, position, place_row, halves, own, tiles, local):
    block_size, width = own.shape[1:]
    hub_rows = place_row.shape[1]
    hub_count = hub_rows // block_size
    return call(
        functools.partial(hub_second_kernel, digits),
        "hub_second",
        48,
        2 * hub_rows * hub_rows * width,
        14 * MIB,
        (
            shape_of((hub_count, block_size, width), bf16),
            shape_of((local, width), bf16),
            shape_of((hub_rows // 2, width), f32),
            shape_of((hub_rows // 2, width), bf16),
        ),
        [SMEM] * 4 + [VMEM] * 3 + [ANY] * 2,
        (VMEM,) * 4,
        [
            pltpu.VMEM(own.shape, bf16),
            pltpu.VMEM((cols.shape[0],) + tiles.shape[1:], bf16),
            pltpu.VMEM((hub_count + 1, block_size, width), f32),
            pltpu.VMEM((hub_rows, width), f32),
            pltpu.SMEM((rows.shape[0],), jnp.int32),
            pltpu.SemaphoreType.DMA((cols.shape[0] + 1,)),
        ],
        (rows, cols, count, position, place_row) + tuple(halves) + (own, tiles),
    )


def combine(position, kept, received, bit, radix, local, sent_type):
    rows = kept.shape[0] // radix
    width = kept.shape[1]

    def kernel(position, kept_in, *refs):
        received, outs = refs[: -radix], refs[-radix:]
        total = kept_in[...].astype(f32)
        for part in received:
            total = total + part[...].astype(f32)
        digit = (position[0] // bit) % radix
        parts = total.reshape(rows // local, radix, local, width)
        for offset, out in enumerate(outs):
            value = parts[:, 0]
            for number in range(1, radix):
                value = jnp.where((digit ^ offset) == number, parts[:, number], value)
            out[...] = value.reshape(rows, width).astype(out.dtype)

    shapes = [shape_of((rows, width), f32)] + [shape_of((rows, width), sent_type)] * (radix - 1)
    return call(
        kernel,
        "combine",
        16,
        kept.size,
        12 * kept.size,
        tuple(shapes),
        [SMEM] + [VMEM] * (1 + len(received)),
        (VMEM,) * radix,
        [],
        (position, kept) + tuple(received),
    )


def load_weights(layer, first_in, second_in, first, second, sems):
    loads = [
        pltpu.make_async_copy(first_in.at[layer], first, sems.at[0]),
        pltpu.make_async_copy(second_in.at[layer], second, sems.at[1]),
    ]
    for load in loads:
        load.start()
    return loads


def hub_network_kernel(layer, rows_in, *refs):
    parts, (first_in, second_in, out, first, second, sems) = refs[:-6], refs[-6:]
    loads = load_weights(layer, first_in, second_in, first, second, sems)
    u = rows_in[...].astype(f32)
    for part in parts:
        u = u + part[...].astype(f32)
    for load in loads:
        load.wait()
    out[...] = network(u, first, second, first.shape[-1])


def hub_network(layer, rows_in, parts, first, second):
    return call(
        functools.partial(hub_network_kernel, layer),
        "hub_network",
        24,
        4 * rows_in.size * first.shape[-1],
        2 * first.size,
        shape_of(rows_in.shape, bf16),
        [VMEM] * (1 + len(parts)) + [ANY] * 2,
        VMEM,
        [
            pltpu.VMEM(first.shape[1:], bf16),
            pltpu.VMEM(second.shape[1:], bf16),
            pltpu.SemaphoreType.DMA((2,)),
        ],
        (rows_in,) + tuple(parts) + (first, second),
    )


def before_kernel(
    layer, rows, cols, count, hubs_in, own_in, tiles_in, first_in, second_in, base, out,
    hubs, own, tiles, first, second, u, result, picked, marks, fed, free, sems, block_sems, sem,
):
    own_count = own.shape[0]
    hub_count = hubs.shape[0]
    begin = rows.shape[0] - cols.shape[0]
    load_own = pltpu.make_async_copy(own_in, own, sem.at[0])
    load_hubs = pltpu.make_async_copy(hubs_in, hubs, sem.at[1])
    load_own.start()
    load_hubs.start()
    found = list_slots(rows, count, picked, begin, hub_count, False)
    start_tiles(picked, found, tiles_in, tiles, sems)
    n_fed, n_free = list_blocks(rows, begin, own_count, hub_count, marks, fed, free)
    load_own.wait()
    u[:own_count] = own[...].astype(f32)
    load_hubs.wait()
    wait_tiles(picked, found, tiles_in, tiles, sems)
    loads = load_weights(layer, first_in, second_in, first, second, sem.at[pl.ds(2, 2)])
    add_products(rows, cols, picked, found, begin, tiles, hubs, own, u, hub_count, own_count)
    for load in loads:
        load.wait()

    def save(block):
        return pltpu.make_async_copy(u.at[block], base.at[block], block_sems.at[block])

    def finish(block):
        return pltpu.make_async_copy(result.at[block], out.at[block], block_sems.at[block])

    each_block(fed, n_fed, save, start)
    network_blocks(free, n_free, lambda block: u[block], first, second, result, finish)
    each_block(fed, n_fed, save, wait)
    each_block(free, n_free, finish, wait)


def before(layer, rows, cols, count, hubs, own, tiles, first, second):
    own_count, block_size, width = own.shape
    return call(
        functools.partial(before_kernel, layer),
        "before",
        58,
        4 * own.size * first.shape[-1] // 3,
        18 * MIB,
        (shape_of(own.shape, f32), shape_of(own.shape, bf16)),
        [SMEM] * 3 + [ANY] * 5,
        (ANY, ANY),
        [
            pltpu.VMEM(hubs.shape, bf16),
            pltpu.VMEM(own.shape, bf16),
            pltpu.VMEM((cols.shape[0],) + tiles.shape[1:], bf16),
            pltpu.VMEM(first.shape[1:], bf16),
            pltpu.VMEM(second.shape[1:], bf16),
            pltpu.VMEM((own_count + 1, block_size, width), f32),
            pltpu.VMEM(own.shape, bf16),
            pltpu.SMEM((rows.shape[0],), jnp.int32),
            pltpu.SMEM((own_count,), jnp.int32),
            pltpu.SMEM((own_count,), jnp.int32),
            pltpu.SMEM((own_count,), jnp.int32),
            pltpu.SemaphoreType.DMA((cols.shape[0],)),
            pltpu.SemaphoreType.DMA((own_count,)),
            pltpu.SemaphoreType.DMA((4,)),
        ],
        (rows, cols, count, hubs, own, tiles, first, second),
    )


def after_kernel(
    layer, with_send, hub_count, rows, chosen, base, done, incoming, tiles, first_in, second_in, *refs
):
    out, refs = refs[0], refs[1:]
    if with_send:
        outgoing, refs = refs[0], refs[1:]
    u, extra, inc, adj, first, second, result, marks, fed, free, block_sems, out_sems, sem = refs
    own_count = u.shape[0]
    remote = incoming.shape[0]
    parts = 4
    size = remote // parts
    loads = []
    for part in range(parts):
        cut = pl.ds(part * size, size)
        loads.append(
            (
                pltpu.make_async_copy(tiles.at[cut], adj.at[cut], sem.at[2 + 2 * part]),
                pltpu.make_async_copy(incoming.at[cut], inc.at[cut], sem.at[3 + 2 * part]),
            )
        )
        for load in loads[-1]:
            load.start()

    def load_base(block):
        return pltpu.make_async_copy(base.at[block], u.at[block], block_sems.at[block])

    def load_done(block):
        return pltpu.make_async_copy(done.at[block], result.at[block], block_sems.at[block])

    def finish(block):
        return pltpu.make_async_copy(result.at[block], out.at[block], out_sems.at[block])

    extra[...] = jnp.zeros_like(extra)
    n_fed, n_free = list_blocks(rows, remote, own_count, hub_count, marks, fed, free)
    for part in range(parts):
        for load in loads[part]:
            load.wait()
        if part == 0:
            weights = load_weights(layer, first_in, second_in, first, second, sem.at[pl.ds(0, 2)])
            each_block(fed, n_fed, load_base, start)
            if with_send:
                each_block(free, n_free, load_done, start)
        products = [dot(adj[slot], inc[slot]) for slot in range(part * size, (part + 1) * size)]
        for lane, product in enumerate(products):
            extra[rows[part * size + lane] - hub_count] += product
    each_block(fed, n_fed, load_base, wait)
    for load in weights:
        load.wait()
    network_blocks(
        fed, n_fed, lambda block: u[block] + extra[block], first, second, result, finish
    )
    copies = []
    if with_send:
        each_block(free, n_free, load_done, wait)
        for number in range(remote):
            copy = pltpu.make_async_copy(
                result.at[chosen[0, number]], outgoing.at[number], sem.at[number]
            )
            copy.start()
            copies.append(copy)
    each_block(fed, n_fed, finish, wait)
    for copy in copies:
        copy.wait()


def after(layer, rows, chosen, base, done, incoming, tiles, first, second, hub_count, with_send):
    own_count = base.shape[0]
    remote = incoming.shape[0]
    shapes = [shape_of(base.shape, bf16)]
    if with_send:
        shapes.append(shape_of(incoming.shape, bf16))
    return pl.pallas_call(
        functools.partial(after_kernel, layer, with_send, hub_count),
        out_shape=tuple(shapes),
        in_specs=[SMEM, SMEM] + [ANY] * 6,
        out_specs=(ANY,) * len(shapes),
        scratch_shapes=[
            pltpu.VMEM(base.shape, f32),
            pltpu.VMEM(base.shape, f32),
            pltpu.VMEM(incoming.shape, bf16),
            pltpu.VMEM((remote,) + tiles.shape[1:], bf16),
            pltpu.VMEM(first.shape[1:], bf16),
            pltpu.VMEM(second.shape[1:], bf16),
            pltpu.VMEM(base.shape, bf16),
            pltpu.SMEM((own_count,), jnp.int32),
            pltpu.SMEM((own_count,), jnp.int32),
            pltpu.SMEM((own_count,), jnp.int32),
            pltpu.SemaphoreType.DMA((own_count,)),
            pltpu.SemaphoreType.DMA((own_count,)),
            pltpu.SemaphoreType.DMA((max(10, remote),)),
        ],
        input_output_aliases={3: 0},
        compiler_params=pltpu.CompilerParams(vmem_limit_bytes=58 * MIB),
        cost_estimate=pl.CostEstimate(
            flops=4 * base.size * first.shape[-1], bytes_accessed=16 * MIB, transcendentals=0
        ),
        name="after",
    )(rows, chosen, base, done, incoming, tiles, first, second)


def exchange(x, bit):
    devices = lax.axis_size("dev")
    return lax.ppermute(x, "dev", [(i, i ^ bit) for i in range(devices)])


def all_digits():
    devices = lax.axis_size("dev")
    digits, bit = [(1, 2)], 2
    while bit < devices:
        radix = 4 if 4 * bit <= devices else 2
        digits.append((bit, radix))
        bit *= radix
    return digits


def gather_step(x, bit, radix):
    return [x] + [exchange(x, bit * offset) for offset in range(1, radix)]


def gather_far(x, digits):
    return gather_step(x, *digits[-1])


def gather_near(pieces, digits):
    for digit in digits[-2:0:-1]:
        pieces = gather_step(jnp.concatenate(pieces, axis=0), *digit)
    return pieces


def gather_last(pieces, digits):
    x = jnp.concatenate(pieces, axis=0)
    return x, exchange(x, digits[0][0])


def scatter_near(position, kept, sent, digits, local):
    received = [exchange(sent, digits[0][0])]
    for bit, radix in digits[1:-1]:
        kept, *sent = combine(position, kept, received, bit, radix, local, bf16)
        received = [exchange(part, bit * (1 + number)) for number, part in enumerate(sent)]
    return kept, received


def scatter_far(position, kept, received, digits, local):
    bit, radix = digits[-1]
    kept, *sent = combine(position, kept, received, bit, radix, local, f32)
    return [kept] + [exchange(part, bit * (1 + number)) for number, part in enumerate(sent)]


def body(
    peripheral, hubs, tiles, tile_rows, local_cols, tile_count, send_list, hub_place, w_in, w_out
):
    position = lax.axis_index("dev")
    digits = all_digits()
    block_size = tiles.shape[1]
    width = peripheral.shape[1]
    own_count = peripheral.shape[0] // block_size
    hub_rows = hub_place.shape[0]
    hub_count = hub_rows // block_size
    local = hubs.shape[0]
    rows = jnp.where(tile_rows < hub_count, tile_rows, tile_rows - position * own_count)
    cols = jnp.where(local_cols < hub_count, local_cols, local_cols - position * own_count)
    place_col = hub_place.reshape(hub_rows, 1)
    place_row = hub_place.reshape(1, hub_rows)
    me = position.astype(jnp.int32).reshape(1)
    own = peripheral.reshape(own_count, block_size, width)
    all_to_all = functools.partial(
        lax.all_to_all, axis_name="dev", split_axis=0, concat_axis=0, tiled=True
    )

    outgoing = pack(send_list, own)
    pieces = gather_near(gather_far(hubs, digits), digits)
    outgoing, rows, cols, place_col, *pieces = lax.optimization_barrier(
        (outgoing, rows, cols, place_col, *pieces)
    )
    incoming = all_to_all(outgoing)
    halves = gather_last(pieces, digits)
    hub_table, mine, kept, sent = hub_first(
        digits, rows, cols, tile_count, me, place_col, halves, own, tiles, local
    )
    base, done = before(0, rows, cols, tile_count, hub_table, own, tiles, w_in, w_out)
    kept, received = scatter_near(me, kept, sent, digits, local)
    base, done, *received = lax.optimization_barrier((base, done, *received))
    parts = scatter_far(me, kept, received, digits, local)
    hub_new = hub_network(0, mine, parts, w_in, w_out)
    pieces = gather_far(hub_new, digits)
    base, *pieces = lax.optimization_barrier((base, *pieces))
    own, outgoing = after(
        0, rows, send_list, base, done, incoming, tiles, w_in, w_out, hub_count, True
    )

    pieces = gather_near(pieces, digits)
    outgoing, *pieces = lax.optimization_barrier((outgoing, *pieces))
    incoming = all_to_all(outgoing)
    halves = gather_last(pieces, digits)
    hub_table, mine, kept, sent = hub_second(
        digits, rows, cols, tile_count, me, place_row, halves, own, tiles, local
    )
    base, done = before(1, rows, cols, tile_count, hub_table, own, tiles, w_in, w_out)
    kept, received = scatter_near(me, kept, sent, digits, local)
    base, done, *received = lax.optimization_barrier((base, done, *received))
    parts = scatter_far(me, kept, received, digits, local)
    hub_out = hub_network(1, mine, parts, w_in, w_out)
    (peri_out,) = after(
        1, rows, send_list, base, done, incoming, tiles, w_in, w_out, hub_count, False
    )
    return (peri_out.reshape(peripheral.shape), hub_out)


def solution(mesh):
    in_specs = (
        P("dev", None),
        P("dev", None),
        P("dev", None, None),
        P("dev"),
        P("dev"),
        P("dev"),
        P("dev", None),
        P(),
        P(),
        P(),
    )
    out_specs = (P("dev", None), P("dev", None))
    return jax.shard_map(body, mesh=mesh, in_specs=in_specs, out_specs=out_specs, check_vma=False)
```

```python
import functools

import jax
import jax.numpy as jnp
from jax import lax
from jax.experimental import pallas as pl
from jax.experimental.pallas import tpu as pltpu
from jax.sharding import PartitionSpec as P

epsilon = 1e-06
f32 = jnp.float32
bf16 = jnp.bfloat16
MIB = 1024 * 1024
VMEM = pl.BlockSpec(memory_space=pltpu.VMEM)
SMEM = pl.BlockSpec(memory_space=pltpu.SMEM)
ANY = pl.BlockSpec(memory_space=pl.ANY)
GROUP = 4
SLOTS = 8


def dot(a, b):
    return jnp.dot(a, b, preferred_element_type=f32)


def shape_of(shape, dtype):
    return jax.ShapeDtypeStruct(tuple(shape), dtype)


def call(kernel, name, mib, flops, moved, out_shape, in_specs, out_specs, scratch, args):
    return pl.pallas_call(
        kernel,
        out_shape=out_shape,
        in_specs=in_specs,
        out_specs=out_specs,
        scratch_shapes=scratch,
        compiler_params=pltpu.CompilerParams(vmem_limit_bytes=mib * MIB),
        cost_estimate=pl.CostEstimate(flops=flops, bytes_accessed=moved, transcendentals=0),
        name=name,
    )(*args)


def normalise(u):
    return (u * lax.rsqrt(jnp.mean(u * u, axis=-1, keepdims=True) + epsilon)).astype(bf16)


def network(u, first, second, hidden_step):
    normed = normalise(u)
    total = u
    for start in range(0, first.shape[-1], hidden_step):
        cut = slice(start, start + hidden_step)
        hidden = jnp.maximum(dot(normed, first[:, cut]), 0.0).astype(bf16)
        total = total + dot(hidden, second[cut, :])
    return total.astype(bf16)


def list_slots(rows, count, picked, begin, hub_count, want_hub):
    def step(slot, found):
        picked[found] = slot
        is_hub = (rows[slot] < hub_count).astype(jnp.int32)
        return found + (is_hub if want_hub else 1 - is_hub)

    return lax.fori_loop(begin, count[0], step, jnp.int32(0))


def start_tiles(picked, found, source, tiles, sems):
    def step(place, unused):
        pltpu.make_async_copy(source.at[picked[place]], tiles.at[place], sems.at[place]).start()
        return unused

    lax.fori_loop(0, found, step, 0)


def wait_tiles(picked, found, source, tiles, sems):
    def step(place, unused):
        pltpu.make_async_copy(source.at[picked[place]], tiles.at[place], sems.at[place]).wait()
        return unused

    lax.fori_loop(0, found, step, 0)


def add_products(rows, cols, picked, found, begin, tiles, hubs, own, total, shift, spare):
    hub_count = hubs.shape[0]

    def step(number, unused):
        where, products = [], []
        for lane in range(SLOTS):
            place = number * SLOTS + lane
            live = place < found
            place = jnp.minimum(place, found - 1)
            slot = picked[place]
            where.append(jnp.where(live, rows[slot] - shift, spare))
            col = cols[slot - begin]
            of_hub = hubs[jnp.minimum(col, hub_count - 1)]
            of_own = own[jnp.maximum(col - hub_count, 0)]
            products.append(dot(tiles[place], jnp.where(col < hub_count, of_hub, of_own)))
        for row, product in zip(where, products):
            total[row] += product
        return unused

    lax.fori_loop(0, (found + SLOTS - 1) // SLOTS, step, 0)


def each_block(pick, found, copy_of, act):
    def step(number, unused):
        act(copy_of(pick(number)))
        return unused

    lax.fori_loop(0, found, step, 0)


def start(copy):
    copy.start()


def wait(copy):
    copy.wait()


def list_blocks(rows, remote, own_count, hub_count, chosen, marks, fed, free):
    def clear(block, unused):
        marks[block] = 0 if chosen is not None else 1
        marks[own_count + block] = 0
        return unused

    def mark(slot, unused):
        if chosen is not None:
            marks[chosen[0, slot]] = 1
        marks[own_count + rows[slot] - hub_count] = 1
        return unused

    def take(block, found):
        n_now, n_later, n_free = found
        is_fed, is_now = marks[own_count + block], marks[block]
        now = is_fed * is_now
        later = is_fed * (1 - is_now)
        fed[jnp.where(is_now == 1, n_now, own_count - 1 - n_later)] = block
        free[n_free] = block
        return n_now + now, n_later + later, n_free + 1 - is_fed

    lax.fori_loop(0, own_count, clear, 0)
    lax.fori_loop(0, remote, mark, 0)
    zero = jnp.int32(0)
    return lax.fori_loop(0, own_count, take, (zero, zero, zero))


def network_blocks(pick, found, read, first, second, result, finish):
    size = result.shape[1]

    def step(number, unused):
        blocks = [pick(jnp.minimum(number * GROUP + lane, found - 1)) for lane in range(GROUP)]
        values = jnp.concatenate([read(block) for block in blocks], axis=0)
        values = network(values, first, second, 512)
        for lane, block in enumerate(blocks):
            result[block] = values[lane * size : (lane + 1) * size]
        for lane, block in enumerate(blocks):

            @pl.when(number * GROUP + lane < found)
            def _(block=block):
                finish(block).start()

        return unused

    lax.fori_loop(0, (found + GROUP - 1) // GROUP, step, 0)


def pack_kernel(chosen, blocks, outgoing, held, sems):
    load = pltpu.make_async_copy(blocks, held, sems.at[0])
    load.start()
    load.wait()
    copies = []
    for number in range(outgoing.shape[0]):
        copy = pltpu.make_async_copy(
            held.at[chosen[0, number]], outgoing.at[number], sems.at[number]
        )
        copy.start()
        copies.append(copy)
    for copy in copies:
        copy.wait()


def pack(chosen, blocks):
    devices = chosen.shape[1]
    return call(
        pack_kernel,
        "pack",
        58,
        0,
        2 * blocks.size * 2,
        shape_of((devices,) + blocks.shape[1:], bf16),
        [SMEM, ANY],
        ANY,
        [pltpu.VMEM(blocks.shape, bf16), pltpu.SemaphoreType.DMA((devices,))],
        (chosen, blocks),
    )


def slot_place(slot, digits):
    place, weight = 0, 1
    for bit, radix in digits[:0:-1]:
        place += weight * ((slot // bit) % radix)
        weight *= radix
    return slot % 2, place


def place_shards(me, halves, table, digits, local):
    for slot in range(table.shape[0] // local):
        half, place = slot_place(slot, digits)
        start = pl.multiple_of((me ^ slot) * local, local)
        table[pl.ds(start, local), :] = halves[half][place * local : (place + 1) * local, :]


def split_sums(me, sums, local, kept, sent):
    odd = me % 2
    width = sums.shape[-1]
    pairs = sums.reshape(-1, 2, local, width)
    kept[...] = jnp.where(odd == 1, pairs[:, 1], pairs[:, 0]).reshape(kept.shape).astype(kept.dtype)
    sent[...] = jnp.where(odd == 1, pairs[:, 0], pairs[:, 1]).reshape(sent.shape).astype(sent.dtype)


def hub_first_kernel(
    digits, rows, cols, count, position, place_col, half0, half1, own_hbm, tiles_hbm,
    hubs, mine, kept, sent, own, tiles, table, total, picked, sems,
):
    hub_count, block_size, width = hubs.shape
    hub_rows = hub_count * block_size
    local = mine.shape[0]
    begin = rows.shape[0] - cols.shape[0]
    found = list_slots(rows, count, picked, begin, hub_count, True)
    start_tiles(picked, found, tiles_hbm, tiles, sems)
    load = pltpu.make_async_copy(own_hbm, own, sems.at[cols.shape[0]])
    load.start()
    me = position[0]
    place_shards(me, (half0, half1), table, digits, local)
    total[...] = jnp.zeros_like(total)
    step = 2 * block_size

    def rows_step(number, unused):
        cut = pl.ds(pl.multiple_of(number * step, step), step)
        lanes = lax.broadcasted_iota(jnp.int32, (step, hub_rows), 1)
        unit = jnp.where(place_col[cut, :] == lanes, 1.0, 0.0).astype(bf16)
        placed = dot(unit, table[...]).astype(bf16)
        hubs[pl.ds(number * 2, 2)] = placed.reshape(2, block_size, width)
        return unused

    lax.fori_loop(0, hub_rows // step, rows_step, 0)
    load.wait()
    wait_tiles(picked, found, tiles_hbm, tiles, sems)
    add_products(rows, cols, picked, found, begin, tiles, hubs, own, total, 0, hub_count)
    split_sums(me, total[:hub_count], local, kept, sent)
    flat = hubs.reshape(hub_rows, width)
    mine[...] = flat[pl.ds(pl.multiple_of(me * local, local), local), :]


def hub_first(digits, rows, cols, count, position, place_col, halves, own, tiles, local):
    block_size, width = own.shape[1:]
    hub_rows = place_col.shape[0]
    hub_count = hub_rows // block_size
    half = shape_of((hub_rows // 2, width), f32)
    return call(
        functools.partial(hub_first_kernel, digits),
        "hub_first",
        48,
        2 * hub_rows * hub_rows * width,
        14 * MIB,
        (
            shape_of((hub_count, block_size, width), bf16),
            shape_of((local, width), bf16),
            half,
            half,
        ),
        [SMEM] * 4 + [VMEM] * 3 + [ANY] * 2,
        (VMEM,) * 4,
        [
            pltpu.VMEM(own.shape, bf16),
            pltpu.VMEM((cols.shape[0],) + tiles.shape[1:], bf16),
            pltpu.VMEM((hub_rows, width), bf16),
            pltpu.VMEM((hub_count + 1, block_size, width), f32),
            pltpu.SMEM((rows.shape[0],), jnp.int32),
            pltpu.SemaphoreType.DMA((cols.shape[0] + 1,)),
        ],
        (rows, cols, count, position, place_col) + tuple(halves) + (own, tiles),
    )


def hub_second_kernel(
    digits, rows, cols, count, position, place_row, half0, half1, own_hbm, tiles_hbm,
    hubs, mine, kept, sent, own, tiles, total, placed, picked, sems,
):
    hub_count, block_size, width = hubs.shape
    hub_rows = hub_count * block_size
    local = mine.shape[0]
    begin = rows.shape[0] - cols.shape[0]
    found = list_slots(rows, count, picked, begin, hub_count, True)
    start_tiles(picked, found, tiles_hbm, tiles, sems)
    load = pltpu.make_async_copy(own_hbm, own, sems.at[cols.shape[0]])
    load.start()
    me = position[0]
    flat = hubs.reshape(hub_rows, width)
    place_shards(me, (half0, half1), flat, digits, local)
    total[...] = jnp.zeros_like(total)

    def unit_rows(start, step):
        down = lax.broadcasted_iota(jnp.int32, (step, hub_rows), 0) + start
        return jnp.where(place_row[...] == down, 1.0, 0.0).astype(bf16)

    mine[...] = dot(unit_rows(me * local, local), flat[...]).astype(bf16)
    load.wait()
    wait_tiles(picked, found, tiles_hbm, tiles, sems)
    add_products(rows, cols, picked, found, begin, tiles, hubs, own, total, 0, hub_count)
    sums = total[:hub_count].reshape(hub_rows, width)
    high = sums.astype(bf16)
    low = (sums - high.astype(f32)).astype(bf16)
    step = 2 * block_size

    def rows_step(number, unused):
        start = number * step
        unit = unit_rows(start, step)
        placed[pl.ds(pl.multiple_of(start, step), step), :] = dot(unit, high) + dot(unit, low)
        return unused

    lax.fori_loop(0, hub_rows // step, rows_step, 0)
    split_sums(me, placed[...], local, kept, sent)


def hub_second(digits, rows, cols, count, position, place_row, halves, own, tiles, local):
    block_size, width = own.shape[1:]
    hub_rows = place_row.shape[1]
    hub_count = hub_rows // block_size
    return call(
        functools.partial(hub_second_kernel, digits),
        "hub_second",
        48,
        2 * hub_rows * hub_rows * width,
        14 * MIB,
        (
            shape_of((hub_count, block_size, width), bf16),
            shape_of((local, width), bf16),
            shape_of((hub_rows // 2, width), f32),
            shape_of((hub_rows // 2, width), f32),
        ),
        [SMEM] * 4 + [VMEM] * 3 + [ANY] * 2,
        (VMEM,) * 4,
        [
            pltpu.VMEM(own.shape, bf16),
            pltpu.VMEM((cols.shape[0],) + tiles.shape[1:], bf16),
            pltpu.VMEM((hub_count + 1, block_size, width), f32),
            pltpu.VMEM((hub_rows, width), f32),
            pltpu.SMEM((rows.shape[0],), jnp.int32),
            pltpu.SemaphoreType.DMA((cols.shape[0] + 1,)),
        ],
        (rows, cols, count, position, place_row) + tuple(halves) + (own, tiles),
    )


def combine(position, kept, received, bit, radix, local, sent_type):
    rows = kept.shape[0] // radix
    width = kept.shape[1]

    def kernel(position, kept_in, *refs):
        received, outs = refs[: -radix], refs[-radix:]
        total = kept_in[...].astype(f32)
        for part in received:
            total = total + part[...].astype(f32)
        digit = (position[0] // bit) % radix
        parts = total.reshape(rows // local, radix, local, width)
        for offset, out in enumerate(outs):
            value = parts[:, 0]
            for number in range(1, radix):
                value = jnp.where((digit ^ offset) == number, parts[:, number], value)
            out[...] = value.reshape(rows, width).astype(out.dtype)

    shapes = [shape_of((rows, width), f32)] + [shape_of((rows, width), sent_type)] * (radix - 1)
    return call(
        kernel,
        "combine",
        16,
        kept.size,
        12 * kept.size,
        tuple(shapes),
        [SMEM] + [VMEM] * (1 + len(received)),
        (VMEM,) * radix,
        [],
        (position, kept) + tuple(received),
    )


def load_weights(layer, first_in, second_in, first, second, sems):
    loads = [
        pltpu.make_async_copy(first_in.at[layer], first, sems.at[0]),
        pltpu.make_async_copy(second_in.at[layer], second, sems.at[1]),
    ]
    for load in loads:
        load.start()
    return loads


def hub_network_kernel(layer, rows_in, *refs):
    parts, (first_in, second_in, out, first, second, sems) = refs[:-6], refs[-6:]
    loads = load_weights(layer, first_in, second_in, first, second, sems)
    u = rows_in[...].astype(f32)
    for part in parts:
        u = u + part[...].astype(f32)
    for load in loads:
        load.wait()
    out[...] = network(u, first, second, first.shape[-1])


def hub_network(layer, rows_in, parts, first, second):
    return call(
        functools.partial(hub_network_kernel, layer),
        "hub_network",
        24,
        4 * rows_in.size * first.shape[-1],
        2 * first.size,
        shape_of(rows_in.shape, bf16),
        [VMEM] * (1 + len(parts)) + [ANY] * 2,
        VMEM,
        [
            pltpu.VMEM(first.shape[1:], bf16),
            pltpu.VMEM(second.shape[1:], bf16),
            pltpu.SemaphoreType.DMA((2,)),
        ],
        (rows_in,) + tuple(parts) + (first, second),
    )


def before_kernel(
    layer, rows, cols, count, hubs_in, own_in, tiles_in, first_in, second_in, base, out,
    hubs, own, tiles, first, second, u, result, picked, marks, fed, free, sems, block_sems, sem,
):
    own_count = own.shape[0]
    hub_count = hubs.shape[0]
    begin = rows.shape[0] - cols.shape[0]
    load_own = pltpu.make_async_copy(own_in, own, sem.at[0])
    load_hubs = pltpu.make_async_copy(hubs_in, hubs, sem.at[1])
    load_own.start()
    load_hubs.start()
    found = list_slots(rows, count, picked, begin, hub_count, False)
    start_tiles(picked, found, tiles_in, tiles, sems)
    n_fed, none, n_free = list_blocks(rows, begin, own_count, hub_count, None, marks, fed, free)
    load_own.wait()
    u[:own_count] = own[...].astype(f32)
    load_hubs.wait()
    wait_tiles(picked, found, tiles_in, tiles, sems)
    loads = load_weights(layer, first_in, second_in, first, second, sem.at[pl.ds(2, 2)])
    add_products(rows, cols, picked, found, begin, tiles, hubs, own, u, hub_count, own_count)
    for load in loads:
        load.wait()

    def save(block):
        return pltpu.make_async_copy(u.at[block], base.at[block], block_sems.at[block])

    def finish(block):
        return pltpu.make_async_copy(result.at[block], out.at[block], block_sems.at[block])

    each_block(lambda i: fed[i], n_fed, save, start)
    network_blocks(lambda i: free[i], n_free, lambda block: u[block], first, second, result, finish)
    each_block(lambda i: fed[i], n_fed, save, wait)
    each_block(lambda i: free[i], n_free, finish, wait)


def before(layer, rows, cols, count, hubs, own, tiles, first, second):
    own_count, block_size, width = own.shape
    return call(
        functools.partial(before_kernel, layer),
        "before",
        58,
        4 * own.size * first.shape[-1] // 3,
        18 * MIB,
        (shape_of(own.shape, f32), shape_of(own.shape, bf16)),
        [SMEM] * 3 + [ANY] * 5,
        (ANY, ANY),
        [
            pltpu.VMEM(hubs.shape, bf16),
            pltpu.VMEM(own.shape, bf16),
            pltpu.VMEM((cols.shape[0],) + tiles.shape[1:], bf16),
            pltpu.VMEM(first.shape[1:], bf16),
            pltpu.VMEM(second.shape[1:], bf16),
            pltpu.VMEM((own_count + 1, block_size, width), f32),
            pltpu.VMEM(own.shape, bf16),
            pltpu.SMEM((rows.shape[0],), jnp.int32),
            pltpu.SMEM((2 * own_count,), jnp.int32),
            pltpu.SMEM((own_count,), jnp.int32),
            pltpu.SMEM((own_count,), jnp.int32),
            pltpu.SemaphoreType.DMA((cols.shape[0],)),
            pltpu.SemaphoreType.DMA((own_count,)),
            pltpu.SemaphoreType.DMA((4,)),
        ],
        (rows, cols, count, hubs, own, tiles, first, second),
    )


def after_kernel(
    layer, with_send, hub_count, rows, chosen, base, done, incoming, tiles, first_in, second_in, *refs
):
    out, refs = refs[0], refs[1:]
    if with_send:
        (sums, outgoing), refs = refs[:2], refs[2:]
    u, extra, inc, adj, first, second, result, marks, fed, free, block_sems, out_sems, sem = refs
    own_count = u.shape[0]
    remote = incoming.shape[0]
    parts = 4
    size = remote // parts
    loads = []
    for part in range(parts):
        cut = pl.ds(part * size, size)
        loads.append(
            (
                pltpu.make_async_copy(tiles.at[cut], adj.at[cut], sem.at[2 + 2 * part]),
                pltpu.make_async_copy(incoming.at[cut], inc.at[cut], sem.at[3 + 2 * part]),
            )
        )
        for load in loads[-1]:
            load.start()

    def now(number):
        return fed[number]

    def later(number):
        return fed[own_count - 1 - number]

    def load_base(block):
        return pltpu.make_async_copy(base.at[block], u.at[block], block_sems.at[block])

    def load_done(block):
        return pltpu.make_async_copy(done.at[block], result.at[block], block_sems.at[block])

    def finish(block):
        return pltpu.make_async_copy(result.at[block], out.at[block], out_sems.at[block])

    extra[...] = jnp.zeros_like(extra)
    n_now, n_later, n_free = list_blocks(
        rows, remote, own_count, hub_count, chosen if with_send else None, marks, fed, free
    )
    for part in range(parts):
        for load in loads[part]:
            load.wait()
        if part == 0:
            weights = load_weights(layer, first_in, second_in, first, second, sem.at[pl.ds(0, 2)])
            each_block(now, n_now, load_base, start)
            if with_send:
                each_block(later, n_later, load_base, start)
                each_block(lambda i: free[i], n_free, load_done, start)
        products = [dot(adj[slot], inc[slot]) for slot in range(part * size, (part + 1) * size)]
        for lane, product in enumerate(products):
            extra[rows[part * size + lane] - hub_count] += product
    each_block(now, n_now, load_base, wait)
    for load in weights:
        load.wait()
    network_blocks(
        now, n_now, lambda block: u[block] + extra[block], first, second, result, finish
    )
    copies = []
    if with_send:
        each_block(lambda i: free[i], n_free, load_done, wait)
        for number in range(remote):
            copy = pltpu.make_async_copy(
                result.at[chosen[0, number]], outgoing.at[number], sem.at[number]
            )
            copy.start()
            copies.append(copy)

        def save(block):
            return pltpu.make_async_copy(u.at[block], sums.at[block], block_sems.at[block])

        def keep(number, unused):
            block = later(number)
            load_base(block).wait()
            u[block] += extra[block]
            save(block).start()
            return unused

        lax.fori_loop(0, n_later, keep, 0)
        each_block(later, n_later, save, wait)
    each_block(now, n_now, finish, wait)
    for copy in copies:
        copy.wait()


def after(layer, rows, chosen, base, done, incoming, tiles, first, second, hub_count, with_send):
    own_count = base.shape[0]
    remote = incoming.shape[0]
    shapes = [shape_of(base.shape, bf16)]
    if with_send:
        shapes += [shape_of(base.shape, f32), shape_of(incoming.shape, bf16)]
    return pl.pallas_call(
        functools.partial(after_kernel, layer, with_send, hub_count),
        out_shape=tuple(shapes),
        in_specs=[SMEM, SMEM] + [ANY] * 6,
        out_specs=(ANY,) * len(shapes),
        scratch_shapes=[
            pltpu.VMEM(base.shape, f32),
            pltpu.VMEM(base.shape, f32),
            pltpu.VMEM(incoming.shape, bf16),
            pltpu.VMEM((remote,) + tiles.shape[1:], bf16),
            pltpu.VMEM(first.shape[1:], bf16),
            pltpu.VMEM(second.shape[1:], bf16),
            pltpu.VMEM(base.shape, bf16),
            pltpu.SMEM((2 * own_count,), jnp.int32),
            pltpu.SMEM((own_count,), jnp.int32),
            pltpu.SMEM((own_count,), jnp.int32),
            pltpu.SemaphoreType.DMA((own_count,)),
            pltpu.SemaphoreType.DMA((own_count,)),
            pltpu.SemaphoreType.DMA((max(10, remote),)),
        ],
        input_output_aliases={3: 0, 2: 1} if with_send else {3: 0},
        compiler_params=pltpu.CompilerParams(vmem_limit_bytes=58 * MIB),
        cost_estimate=pl.CostEstimate(
            flops=4 * base.size * first.shape[-1], bytes_accessed=16 * MIB, transcendentals=0
        ),
        name="after",
    )(rows, chosen, base, done, incoming, tiles, first, second)


def late_kernel(
    layer, remote, hub_count, rows, chosen, sums, done, first_in, second_in, out,
    u, first, second, result, marks, fed, free, block_sems, sem,
):
    own_count = u.shape[0]
    weights = load_weights(layer, first_in, second_in, first, second, sem)
    n_later = list_blocks(rows, remote, own_count, hub_count, chosen, marks, fed, free)[1]

    def later(number):
        return fed[own_count - 1 - number]

    def load(block):
        return pltpu.make_async_copy(sums.at[block], u.at[block], block_sems.at[block])

    def finish(block):
        return pltpu.make_async_copy(result.at[block], out.at[block], block_sems.at[block])

    each_block(later, n_later, load, start)
    each_block(later, n_later, load, wait)
    for part in weights:
        part.wait()
    network_blocks(later, n_later, lambda block: u[block], first, second, result, finish)
    each_block(later, n_later, finish, wait)


def late(layer, rows, chosen, sums, done, first, second, hub_count):
    own_count = sums.shape[0]
    return pl.pallas_call(
        functools.partial(late_kernel, layer, chosen.shape[1], hub_count),
        out_shape=shape_of(done.shape, bf16),
        in_specs=[SMEM, SMEM] + [ANY] * 4,
        out_specs=ANY,
        scratch_shapes=[
            pltpu.VMEM(sums.shape, f32),
            pltpu.VMEM(first.shape[1:], bf16),
            pltpu.VMEM(second.shape[1:], bf16),
            pltpu.VMEM(sums.shape, bf16),
            pltpu.SMEM((2 * own_count,), jnp.int32),
            pltpu.SMEM((own_count,), jnp.int32),
            pltpu.SMEM((own_count,), jnp.int32),
            pltpu.SemaphoreType.DMA((own_count,)),
            pltpu.SemaphoreType.DMA((2,)),
        ],
        input_output_aliases={3: 0},
        compiler_params=pltpu.CompilerParams(vmem_limit_bytes=58 * MIB),
        cost_estimate=pl.CostEstimate(
            flops=sums.size * first.shape[-1], bytes_accessed=5 * MIB, transcendentals=0
        ),
        name="late",
    )(rows, chosen, sums, done, first, second)


def exchange(x, bit):
    devices = lax.axis_size("dev")
    return lax.ppermute(x, "dev", [(i, i ^ bit) for i in range(devices)])


def all_digits():
    devices = lax.axis_size("dev")
    digits, bit = [(1, 2)], 2
    while bit < devices:
        radix = 4 if 4 * bit <= devices else 2
        digits.append((bit, radix))
        bit *= radix
    return digits


def gather_step(x, bit, radix):
    return [x] + [exchange(x, bit * offset) for offset in range(1, radix)]


def gather_far(x, digits):
    return gather_step(x, *digits[-1])


def gather_near(pieces, digits):
    for digit in digits[-2:0:-1]:
        pieces = gather_step(jnp.concatenate(pieces, axis=0), *digit)
    return pieces


def gather_last(pieces, digits):
    x = jnp.concatenate(pieces, axis=0)
    return x, exchange(x, digits[0][0])


def scatter_near(position, kept, sent, digits, local):
    received = [exchange(sent, digits[0][0])]
    for bit, radix in digits[1:-1]:
        kept, *sent = combine(position, kept, received, bit, radix, local, bf16)
        received = [exchange(part, bit * (1 + number)) for number, part in enumerate(sent)]
    return kept, received


def scatter_far(position, kept, received, digits, local, sent_type):
    bit, radix = digits[-1]
    kept, *sent = combine(position, kept, received, bit, radix, local, sent_type)
    return [kept] + [exchange(part, bit * (1 + number)) for number, part in enumerate(sent)]


def body(
    peripheral, hubs, tiles, tile_rows, local_cols, tile_count, send_list, hub_place, w_in, w_out
):
    position = lax.axis_index("dev")
    digits = all_digits()
    block_size = tiles.shape[1]
    width = peripheral.shape[1]
    own_count = peripheral.shape[0] // block_size
    hub_rows = hub_place.shape[0]
    hub_count = hub_rows // block_size
    local = hubs.shape[0]
    rows = jnp.where(tile_rows < hub_count, tile_rows, tile_rows - position * own_count)
    cols = jnp.where(local_cols < hub_count, local_cols, local_cols - position * own_count)
    place_col = hub_place.reshape(hub_rows, 1)
    place_row = hub_place.reshape(1, hub_rows)
    me = position.astype(jnp.int32).reshape(1)
    own = peripheral.reshape(own_count, block_size, width)
    all_to_all = functools.partial(
        lax.all_to_all, axis_name="dev", split_axis=0, concat_axis=0, tiled=True
    )

    pieces = gather_far(hubs, digits)
    own, *pieces = lax.optimization_barrier((own, *pieces))
    outgoing = pack(send_list, own)
    pieces = gather_near(pieces, digits)
    outgoing, rows, cols, place_col, *pieces = lax.optimization_barrier(
        (outgoing, rows, cols, place_col, *pieces)
    )
    incoming = all_to_all(outgoing)
    halves = gather_last(pieces, digits)
    hub_table, mine, kept, sent = hub_first(
        digits, rows, cols, tile_count, me, place_col, halves, own, tiles, local
    )
    base, done = before(0, rows, cols, tile_count, hub_table, own, tiles, w_in, w_out)
    kept, received = scatter_near(me, kept, sent, digits, local)
    base, done, *received = lax.optimization_barrier((base, done, *received))
    parts = scatter_far(me, kept, received, digits, local, bf16)
    hub_new = hub_network(0, mine, parts, w_in, w_out)
    pieces = gather_far(hub_new, digits)
    base, *pieces = lax.optimization_barrier((base, *pieces))
    done, sums, outgoing = after(
        0, rows, send_list, base, done, incoming, tiles, w_in, w_out, hub_count, True
    )

    pieces = gather_near(pieces, digits)
    outgoing, *pieces = lax.optimization_barrier((outgoing, *pieces))
    incoming = all_to_all(outgoing)
    own = late(0, rows, send_list, sums, done, w_in, w_out, hub_count)
    halves = gather_last(pieces, digits)
    hub_table, mine, kept, sent = hub_second(
        digits, rows, cols, tile_count, me, place_row, halves, own, tiles, local
    )
    base, done = before(1, rows, cols, tile_count, hub_table, own, tiles, w_in, w_out)
    kept, received = scatter_near(me, kept, sent, digits, local)
    base, done, *received = lax.optimization_barrier((base, done, *received))
    parts = scatter_far(me, kept, received, digits, local, f32)
    (peri_out,) = after(
        1, rows, send_list, base, done, incoming, tiles, w_in, w_out, hub_count, False
    )
    peri_out, *parts = lax.optimization_barrier((peri_out, *parts))
    hub_out = hub_network(1, mine, parts, w_in, w_out)
    return (peri_out.reshape(peripheral.shape), hub_out)


def solution(mesh):
    in_specs = (
        P("dev", None),
        P("dev", None),
        P("dev", None, None),
        P("dev"),
        P("dev"),
        P("dev"),
        P("dev", None),
        P(),
        P(),
        P(),
    )
    out_specs = (P("dev", None), P("dev", None))
    return jax.shard_map(body, mesh=mesh, in_specs=in_specs, out_specs=out_specs, check_vma=False)
```

```python
import functools

import jax
import jax.numpy as jnp
from jax import lax
from jax.experimental import pallas as pl
from jax.experimental.pallas import tpu as pltpu
from jax.sharding import PartitionSpec as P

epsilon = 1e-06
f32 = jnp.float32
bf16 = jnp.bfloat16
MIB = 1024 * 1024
VMEM = pl.BlockSpec(memory_space=pltpu.VMEM)
SMEM = pl.BlockSpec(memory_space=pltpu.SMEM)
ANY = pl.BlockSpec(memory_space=pl.ANY)
GROUP = 4
SLOTS = 8


def dot(a, b):
    return jnp.dot(a, b, preferred_element_type=f32)


def shape_of(shape, dtype):
    return jax.ShapeDtypeStruct(tuple(shape), dtype)


def call(kernel, name, mib, flops, moved, out_shape, in_specs, out_specs, scratch, args):
    return pl.pallas_call(
        kernel,
        out_shape=out_shape,
        in_specs=in_specs,
        out_specs=out_specs,
        scratch_shapes=scratch,
        compiler_params=pltpu.CompilerParams(vmem_limit_bytes=mib * MIB),
        cost_estimate=pl.CostEstimate(flops=flops, bytes_accessed=moved, transcendentals=0),
        name=name,
    )(*args)


def normalise(u):
    return (u * lax.rsqrt(jnp.mean(u * u, axis=-1, keepdims=True) + epsilon)).astype(bf16)


def network(u, first, second, hidden_step):
    normed = normalise(u)
    total = u
    for start in range(0, first.shape[-1], hidden_step):
        cut = slice(start, start + hidden_step)
        hidden = jnp.maximum(dot(normed, first[:, cut]), 0.0).astype(bf16)
        total = total + dot(hidden, second[cut, :])
    return total.astype(bf16)


def list_slots(rows, count, picked, begin, hub_count, want_hub):
    def step(slot, found):
        picked[found] = slot
        is_hub = (rows[slot] < hub_count).astype(jnp.int32)
        return found + (is_hub if want_hub else 1 - is_hub)

    return lax.fori_loop(begin, count[0], step, jnp.int32(0))


def start_tiles(picked, found, source, tiles, sems):
    def step(place, unused):
        pltpu.make_async_copy(source.at[picked[place]], tiles.at[place], sems.at[place]).start()
        return unused

    lax.fori_loop(0, found, step, 0)


def wait_tiles(picked, found, source, tiles, sems):
    def step(place, unused):
        pltpu.make_async_copy(source.at[picked[place]], tiles.at[place], sems.at[place]).wait()
        return unused

    lax.fori_loop(0, found, step, 0)


def add_products(rows, cols, picked, found, begin, tiles, hubs, own, total, shift, spare):
    hub_count = hubs.shape[0]

    def step(number, unused):
        where, products = [], []
        for lane in range(SLOTS):
            place = number * SLOTS + lane
            live = place < found
            place = jnp.minimum(place, found - 1)
            slot = picked[place]
            where.append(jnp.where(live, rows[slot] - shift, spare))
            col = cols[slot - begin]
            of_hub = hubs[jnp.minimum(col, hub_count - 1)]
            of_own = own[jnp.maximum(col - hub_count, 0)]
            products.append(dot(tiles[place], jnp.where(col < hub_count, of_hub, of_own)))
        for row, product in zip(where, products):
            total[row] += product
        return unused

    lax.fori_loop(0, (found + SLOTS - 1) // SLOTS, step, 0)


def each_block(pick, found, copy_of, act):
    def step(number, unused):
        act(copy_of(pick(number)))
        return unused

    lax.fori_loop(0, found, step, 0)


def start(copy):
    copy.start()


def wait(copy):
    copy.wait()


def list_blocks(rows, remote, own_count, hub_count, chosen, marks, fed, free):
    def clear(block, unused):
        marks[block] = 0 if chosen is not None else 1
        marks[own_count + block] = 0
        return unused

    def mark(slot, unused):
        if chosen is not None:
            marks[chosen[0, slot]] = 1
        marks[own_count + rows[slot] - hub_count] = 1
        return unused

    def take(block, found):
        n_now, n_later, n_free = found
        is_fed, is_now = marks[own_count + block], marks[block]
        now = is_fed * is_now
        later = is_fed * (1 - is_now)
        fed[jnp.where(is_now == 1, n_now, own_count - 1 - n_later)] = block
        free[n_free] = block
        return n_now + now, n_later + later, n_free + 1 - is_fed

    lax.fori_loop(0, own_count, clear, 0)
    lax.fori_loop(0, remote, mark, 0)
    zero = jnp.int32(0)
    return lax.fori_loop(0, own_count, take, (zero, zero, zero))


def network_blocks(pick, found, read, first, second, result, finish):
    size = result.shape[1]

    def step(number, unused):
        blocks = [pick(jnp.minimum(number * GROUP + lane, found - 1)) for lane in range(GROUP)]
        values = jnp.concatenate([read(block) for block in blocks], axis=0)
        values = network(values, first, second, 512)
        for lane, block in enumerate(blocks):
            result[block] = values[lane * size : (lane + 1) * size]
        for lane, block in enumerate(blocks):

            @pl.when(number * GROUP + lane < found)
            def _(block=block):
                finish(block).start()

        return unused

    lax.fori_loop(0, (found + GROUP - 1) // GROUP, step, 0)


def pack_kernel(chosen, blocks, outgoing, held, sems):
    load = pltpu.make_async_copy(blocks, held, sems.at[0])
    load.start()
    load.wait()
    copies = []
    for number in range(outgoing.shape[0]):
        copy = pltpu.make_async_copy(
            held.at[chosen[0, number]], outgoing.at[number], sems.at[number]
        )
        copy.start()
        copies.append(copy)
    for copy in copies:
        copy.wait()


def pack(chosen, blocks):
    devices = chosen.shape[1]
    return call(
        pack_kernel,
        "pack",
        58,
        0,
        2 * blocks.size * 2,
        shape_of((devices,) + blocks.shape[1:], bf16),
        [SMEM, ANY],
        ANY,
        [pltpu.VMEM(blocks.shape, bf16), pltpu.SemaphoreType.DMA((devices,))],
        (chosen, blocks),
    )


def slot_place(slot, digits):
    place, weight = 0, 1
    for bit, radix in digits[:0:-1]:
        place += weight * ((slot // bit) % radix)
        weight *= radix
    return slot % 2, place


def place_shards(me, halves, table, digits, local):
    for slot in range(table.shape[0] // local):
        half, place = slot_place(slot, digits)
        start = pl.multiple_of((me ^ slot) * local, local)
        table[pl.ds(start, local), :] = halves[half][place * local : (place + 1) * local, :]


def split_sums(me, sums, local, kept, sent):
    odd = me % 2
    width = sums.shape[-1]
    pairs = sums.reshape(-1, 2, local, width)
    kept[...] = jnp.where(odd == 1, pairs[:, 1], pairs[:, 0]).reshape(kept.shape).astype(kept.dtype)
    sent[...] = jnp.where(odd == 1, pairs[:, 0], pairs[:, 1]).reshape(sent.shape).astype(sent.dtype)


def hub_first_kernel(
    digits, rows, cols, count, position, place_col, half0, half1, own_hbm, tiles_hbm,
    hubs, mine, kept, sent, own, tiles, table, total, picked, sems,
):
    hub_count, block_size, width = hubs.shape
    hub_rows = hub_count * block_size
    local = mine.shape[0] // digits[-1][1]
    begin = rows.shape[0] - cols.shape[0]
    found = list_slots(rows, count, picked, begin, hub_count, True)
    start_tiles(picked, found, tiles_hbm, tiles, sems)
    load = pltpu.make_async_copy(own_hbm, own, sems.at[cols.shape[0]])
    load.start()
    me = position[0]
    place_shards(me, (half0, half1), table, digits, local)
    total[...] = jnp.zeros_like(total)
    step = 2 * block_size

    def rows_step(number, unused):
        cut = pl.ds(pl.multiple_of(number * step, step), step)
        lanes = lax.broadcasted_iota(jnp.int32, (step, hub_rows), 1)
        unit = jnp.where(place_col[cut, :] == lanes, 1.0, 0.0).astype(bf16)
        placed = dot(unit, table[...]).astype(bf16)
        hubs[pl.ds(number * 2, 2)] = placed.reshape(2, block_size, width)
        return unused

    lax.fori_loop(0, hub_rows // step, rows_step, 0)
    load.wait()
    wait_tiles(picked, found, tiles_hbm, tiles, sems)
    add_products(rows, cols, picked, found, begin, tiles, hubs, own, total, 0, hub_count)
    split_sums(me, total[:hub_count], local, kept, sent)
    flat = hubs.reshape(hub_rows, width)
    bit, radix = digits[-1]
    for offset in range(radix):
        first_row = pl.multiple_of((me ^ (bit * offset)) * local, local)
        mine[offset * local : (offset + 1) * local, :] = flat[pl.ds(first_row, local), :]


def hub_first(digits, rows, cols, count, position, place_col, halves, own, tiles, local):
    block_size, width = own.shape[1:]
    hub_rows = place_col.shape[0]
    hub_count = hub_rows // block_size
    half = shape_of((hub_rows // 2, width), f32)
    return call(
        functools.partial(hub_first_kernel, digits),
        "hub_first",
        48,
        2 * hub_rows * hub_rows * width,
        14 * MIB,
        (
            shape_of((hub_count, block_size, width), bf16),
            shape_of((digits[-1][1] * local, width), bf16),
            half,
            half,
        ),
        [SMEM] * 4 + [VMEM] * 3 + [ANY] * 2,
        (VMEM,) * 4,
        [
            pltpu.VMEM(own.shape, bf16),
            pltpu.VMEM((cols.shape[0],) + tiles.shape[1:], bf16),
            pltpu.VMEM((hub_rows, width), bf16),
            pltpu.VMEM((hub_count + 1, block_size, width), f32),
            pltpu.SMEM((rows.shape[0],), jnp.int32),
            pltpu.SemaphoreType.DMA((cols.shape[0] + 1,)),
        ],
        (rows, cols, count, position, place_col) + tuple(halves) + (own, tiles),
    )


def hub_second_kernel(
    digits, rows, cols, count, position, place_row, half0, half1, own_hbm, tiles_hbm,
    hubs, mine, kept, sent, own, tiles, total, placed, picked, sems,
):
    hub_count, block_size, width = hubs.shape
    hub_rows = hub_count * block_size
    local = mine.shape[0]
    begin = rows.shape[0] - cols.shape[0]
    found = list_slots(rows, count, picked, begin, hub_count, True)
    start_tiles(picked, found, tiles_hbm, tiles, sems)
    load = pltpu.make_async_copy(own_hbm, own, sems.at[cols.shape[0]])
    load.start()
    me = position[0]
    flat = hubs.reshape(hub_rows, width)
    place_shards(me, (half0, half1), flat, digits, local)
    total[...] = jnp.zeros_like(total)

    def unit_rows(start, step):
        down = lax.broadcasted_iota(jnp.int32, (step, hub_rows), 0) + start
        return jnp.where(place_row[...] == down, 1.0, 0.0).astype(bf16)

    mine[...] = dot(unit_rows(me * local, local), flat[...]).astype(bf16)
    load.wait()
    wait_tiles(picked, found, tiles_hbm, tiles, sems)
    add_products(rows, cols, picked, found, begin, tiles, hubs, own, total, 0, hub_count)
    sums = total[:hub_count].reshape(hub_rows, width)
    high = sums.astype(bf16)
    low = (sums - high.astype(f32)).astype(bf16)
    step = 2 * block_size

    def rows_step(number, unused):
        start = number * step
        unit = unit_rows(start, step)
        placed[pl.ds(pl.multiple_of(start, step), step), :] = dot(unit, high) + dot(unit, low)
        return unused

    lax.fori_loop(0, hub_rows // step, rows_step, 0)
    split_sums(me, placed[...], local, kept, sent)


def hub_second(digits, rows, cols, count, position, place_row, halves, own, tiles, local):
    block_size, width = own.shape[1:]
    hub_rows = place_row.shape[1]
    hub_count = hub_rows // block_size
    return call(
        functools.partial(hub_second_kernel, digits),
        "hub_second",
        48,
        2 * hub_rows * hub_rows * width,
        14 * MIB,
        (
            shape_of((hub_count, block_size, width), bf16),
            shape_of((local, width), bf16),
            shape_of((hub_rows // 2, width), f32),
            shape_of((hub_rows // 2, width), f32),
        ),
        [SMEM] * 4 + [VMEM] * 3 + [ANY] * 2,
        (VMEM,) * 4,
        [
            pltpu.VMEM(own.shape, bf16),
            pltpu.VMEM((cols.shape[0],) + tiles.shape[1:], bf16),
            pltpu.VMEM((hub_count + 1, block_size, width), f32),
            pltpu.VMEM((hub_rows, width), f32),
            pltpu.SMEM((rows.shape[0],), jnp.int32),
            pltpu.SemaphoreType.DMA((cols.shape[0] + 1,)),
        ],
        (rows, cols, count, position, place_row) + tuple(halves) + (own, tiles),
    )


def combine(position, kept, received, bit, radix, local, sent_type, together=False):
    rows = kept.shape[0] // radix
    width = kept.shape[1]
    if together:
        shapes = [shape_of(kept.shape, sent_type)]
    else:
        shapes = [shape_of((rows, width), f32)] + [shape_of((rows, width), sent_type)] * (radix - 1)

    def kernel(position, kept_in, *refs):
        received, outs = refs[: -len(shapes)], refs[-len(shapes) :]
        total = kept_in[...].astype(f32)
        for part in received:
            total = total + part[...].astype(f32)
        digit = (position[0] // bit) % radix
        parts = total.reshape(rows // local, radix, local, width)
        for offset in range(radix):
            value = parts[:, 0]
            for number in range(1, radix):
                value = jnp.where((digit ^ offset) == number, parts[:, number], value)
            value = value.reshape(rows, width)
            if together:
                outs[0][offset * rows : (offset + 1) * rows, :] = value.astype(sent_type)
            else:
                outs[offset][...] = value.astype(outs[offset].dtype)

    return call(
        kernel,
        "combine",
        16,
        kept.size,
        12 * kept.size,
        tuple(shapes),
        [SMEM] + [VMEM] * (1 + len(received)),
        (VMEM,) * len(shapes),
        [],
        (position, kept) + tuple(received),
    )


def load_weights(layer, first_in, second_in, first, second, sems):
    loads = [
        pltpu.make_async_copy(first_in.at[layer], first, sems.at[0]),
        pltpu.make_async_copy(second_in.at[layer], second, sems.at[1]),
    ]
    for load in loads:
        load.start()
    return loads


def hub_network_kernel(layer, local, rows_in, *refs):
    parts, (first_in, second_in, out, first, second, sems) = refs[:-6], refs[-6:]
    loads = load_weights(layer, first_in, second_in, first, second, sems)
    u = rows_in[...].astype(f32)
    for mask, part in enumerate(parts):
        if rows_in.shape[0] == local:
            u = u + part[...].astype(f32)
        else:
            pieces = [part[(offset ^ mask) * local :][:local] for offset in range(len(parts))]
            u = u + jnp.concatenate(pieces, axis=0).astype(f32)
    for load in loads:
        load.wait()
    out[...] = network(u, first, second, 512)


def hub_network(layer, local, rows_in, parts, first, second):
    return call(
        functools.partial(hub_network_kernel, layer, local),
        "hub_network",
        24,
        4 * rows_in.size * first.shape[-1],
        2 * first.size,
        shape_of(rows_in.shape, bf16),
        [VMEM] * (1 + len(parts)) + [ANY] * 2,
        VMEM,
        [
            pltpu.VMEM(first.shape[1:], bf16),
            pltpu.VMEM(second.shape[1:], bf16),
            pltpu.SemaphoreType.DMA((2,)),
        ],
        (rows_in,) + tuple(parts) + (first, second),
    )


def before_kernel(
    layer, rows, cols, count, hubs_in, own_in, tiles_in, first_in, second_in, base, out,
    hubs, own, tiles, first, second, u, result, picked, marks, fed, free, sems, block_sems, sem,
):
    own_count = own.shape[0]
    hub_count = hubs.shape[0]
    begin = rows.shape[0] - cols.shape[0]
    load_own = pltpu.make_async_copy(own_in, own, sem.at[0])
    load_hubs = pltpu.make_async_copy(hubs_in, hubs, sem.at[1])
    load_own.start()
    load_hubs.start()
    found = list_slots(rows, count, picked, begin, hub_count, False)
    start_tiles(picked, found, tiles_in, tiles, sems)
    n_fed, none, n_free = list_blocks(rows, begin, own_count, hub_count, None, marks, fed, free)
    load_own.wait()
    u[:own_count] = own[...].astype(f32)
    load_hubs.wait()
    wait_tiles(picked, found, tiles_in, tiles, sems)
    loads = load_weights(layer, first_in, second_in, first, second, sem.at[pl.ds(2, 2)])
    add_products(rows, cols, picked, found, begin, tiles, hubs, own, u, hub_count, own_count)
    for load in loads:
        load.wait()

    def save(block):
        return pltpu.make_async_copy(u.at[block], base.at[block], block_sems.at[block])

    def finish(block):
        return pltpu.make_async_copy(result.at[block], out.at[block], block_sems.at[block])

    each_block(lambda i: fed[i], n_fed, save, start)
    network_blocks(lambda i: free[i], n_free, lambda block: u[block], first, second, result, finish)
    each_block(lambda i: fed[i], n_fed, save, wait)
    each_block(lambda i: free[i], n_free, finish, wait)


def before(layer, rows, cols, count, hubs, own, tiles, first, second):
    own_count, block_size, width = own.shape
    return call(
        functools.partial(before_kernel, layer),
        "before",
        58,
        4 * own.size * first.shape[-1] // 3,
        18 * MIB,
        (shape_of(own.shape, f32), shape_of(own.shape, bf16)),
        [SMEM] * 3 + [ANY] * 5,
        (ANY, ANY),
        [
            pltpu.VMEM(hubs.shape, bf16),
            pltpu.VMEM(own.shape, bf16),
            pltpu.VMEM((cols.shape[0],) + tiles.shape[1:], bf16),
            pltpu.VMEM(first.shape[1:], bf16),
            pltpu.VMEM(second.shape[1:], bf16),
            pltpu.VMEM((own_count + 1, block_size, width), f32),
            pltpu.VMEM(own.shape, bf16),
            pltpu.SMEM((rows.shape[0],), jnp.int32),
            pltpu.SMEM((2 * own_count,), jnp.int32),
            pltpu.SMEM((own_count,), jnp.int32),
            pltpu.SMEM((own_count,), jnp.int32),
            pltpu.SemaphoreType.DMA((cols.shape[0],)),
            pltpu.SemaphoreType.DMA((own_count,)),
            pltpu.SemaphoreType.DMA((4,)),
        ],
        (rows, cols, count, hubs, own, tiles, first, second),
    )


def after_kernel(
    layer, with_send, hub_count, rows, chosen, base, done, incoming, tiles, first_in, second_in, *refs
):
    out, refs = refs[0], refs[1:]
    if with_send:
        (sums, outgoing), refs = refs[:2], refs[2:]
    u, extra, inc, adj, first, second, result, marks, fed, free, block_sems, out_sems, sem = refs
    own_count = u.shape[0]
    remote = incoming.shape[0]
    parts = 4
    size = remote // parts
    loads = []
    for part in range(parts):
        cut = pl.ds(part * size, size)
        loads.append(
            (
                pltpu.make_async_copy(tiles.at[cut], adj.at[cut], sem.at[2 + 2 * part]),
                pltpu.make_async_copy(incoming.at[cut], inc.at[cut], sem.at[3 + 2 * part]),
            )
        )
        for load in loads[-1]:
            load.start()

    def now(number):
        return fed[number]

    def later(number):
        return fed[own_count - 1 - number]

    def load_base(block):
        return pltpu.make_async_copy(base.at[block], u.at[block], block_sems.at[block])

    def load_done(block):
        return pltpu.make_async_copy(done.at[block], result.at[block], block_sems.at[block])

    def finish(block):
        return pltpu.make_async_copy(result.at[block], out.at[block], out_sems.at[block])

    extra[...] = jnp.zeros_like(extra)
    n_now, n_later, n_free = list_blocks(
        rows, remote, own_count, hub_count, chosen if with_send else None, marks, fed, free
    )
    for part in range(parts):
        for load in loads[part]:
            load.wait()
        if part == 0:
            weights = load_weights(layer, first_in, second_in, first, second, sem.at[pl.ds(0, 2)])
            each_block(now, n_now, load_base, start)
            if with_send:
                each_block(later, n_later, load_base, start)
                each_block(lambda i: free[i], n_free, load_done, start)
        products = [dot(adj[slot], inc[slot]) for slot in range(part * size, (part + 1) * size)]
        for lane, product in enumerate(products):
            extra[rows[part * size + lane] - hub_count] += product
    each_block(now, n_now, load_base, wait)
    for load in weights:
        load.wait()
    network_blocks(
        now, n_now, lambda block: u[block] + extra[block], first, second, result, finish
    )
    copies = []
    if with_send:
        each_block(lambda i: free[i], n_free, load_done, wait)
        for number in range(remote):
            copy = pltpu.make_async_copy(
                result.at[chosen[0, number]], outgoing.at[number], sem.at[number]
            )
            copy.start()
            copies.append(copy)

        def save(block):
            return pltpu.make_async_copy(u.at[block], sums.at[block], block_sems.at[block])

        def keep(number, unused):
            block = later(number)
            load_base(block).wait()
            u[block] += extra[block]
            save(block).start()
            return unused

        lax.fori_loop(0, n_later, keep, 0)
        each_block(later, n_later, save, wait)
    each_block(now, n_now, finish, wait)
    for copy in copies:
        copy.wait()


def after(layer, rows, chosen, base, done, incoming, tiles, first, second, hub_count, with_send):
    own_count = base.shape[0]
    remote = incoming.shape[0]
    shapes = [shape_of(base.shape, bf16)]
    if with_send:
        shapes += [shape_of(base.shape, f32), shape_of(incoming.shape, bf16)]
    return pl.pallas_call(
        functools.partial(after_kernel, layer, with_send, hub_count),
        out_shape=tuple(shapes),
        in_specs=[SMEM, SMEM] + [ANY] * 6,
        out_specs=(ANY,) * len(shapes),
        scratch_shapes=[
            pltpu.VMEM(base.shape, f32),
            pltpu.VMEM(base.shape, f32),
            pltpu.VMEM(incoming.shape, bf16),
            pltpu.VMEM((remote,) + tiles.shape[1:], bf16),
            pltpu.VMEM(first.shape[1:], bf16),
            pltpu.VMEM(second.shape[1:], bf16),
            pltpu.VMEM(base.shape, bf16),
            pltpu.SMEM((2 * own_count,), jnp.int32),
            pltpu.SMEM((own_count,), jnp.int32),
            pltpu.SMEM((own_count,), jnp.int32),
            pltpu.SemaphoreType.DMA((own_count,)),
            pltpu.SemaphoreType.DMA((own_count,)),
            pltpu.SemaphoreType.DMA((max(10, remote),)),
        ],
        input_output_aliases={3: 0, 2: 1} if with_send else {3: 0},
        compiler_params=pltpu.CompilerParams(vmem_limit_bytes=58 * MIB),
        cost_estimate=pl.CostEstimate(
            flops=4 * base.size * first.shape[-1], bytes_accessed=16 * MIB, transcendentals=0
        ),
        name="after",
    )(rows, chosen, base, done, incoming, tiles, first, second)


def late_kernel(
    layer, remote, hub_count, rows, chosen, sums, done, first_in, second_in, out,
    u, first, second, result, marks, fed, free, block_sems, sem,
):
    own_count = u.shape[0]
    weights = load_weights(layer, first_in, second_in, first, second, sem)
    n_later = list_blocks(rows, remote, own_count, hub_count, chosen, marks, fed, free)[1]

    def later(number):
        return fed[own_count - 1 - number]

    def load(block):
        return pltpu.make_async_copy(sums.at[block], u.at[block], block_sems.at[block])

    def finish(block):
        return pltpu.make_async_copy(result.at[block], out.at[block], block_sems.at[block])

    each_block(later, n_later, load, start)
    each_block(later, n_later, load, wait)
    for part in weights:
        part.wait()
    network_blocks(later, n_later, lambda block: u[block], first, second, result, finish)
    each_block(later, n_later, finish, wait)


def late(layer, rows, chosen, sums, done, first, second, hub_count):
    own_count = sums.shape[0]
    return pl.pallas_call(
        functools.partial(late_kernel, layer, chosen.shape[1], hub_count),
        out_shape=shape_of(done.shape, bf16),
        in_specs=[SMEM, SMEM] + [ANY] * 4,
        out_specs=ANY,
        scratch_shapes=[
            pltpu.VMEM(sums.shape, f32),
            pltpu.VMEM(first.shape[1:], bf16),
            pltpu.VMEM(second.shape[1:], bf16),
            pltpu.VMEM(sums.shape, bf16),
            pltpu.SMEM((2 * own_count,), jnp.int32),
            pltpu.SMEM((own_count,), jnp.int32),
            pltpu.SMEM((own_count,), jnp.int32),
            pltpu.SemaphoreType.DMA((own_count,)),
            pltpu.SemaphoreType.DMA((2,)),
        ],
        input_output_aliases={3: 0},
        compiler_params=pltpu.CompilerParams(vmem_limit_bytes=58 * MIB),
        cost_estimate=pl.CostEstimate(
            flops=sums.size * first.shape[-1], bytes_accessed=5 * MIB, transcendentals=0
        ),
        name="late",
    )(rows, chosen, sums, done, first, second)


def exchange(x, bit):
    devices = lax.axis_size("dev")
    return lax.ppermute(x, "dev", [(i, i ^ bit) for i in range(devices)])


def all_digits():
    devices = lax.axis_size("dev")
    digits, bit = [(1, 2)], 2
    while bit < devices:
        radix = 4 if 4 * bit <= devices else 2
        digits.append((bit, radix))
        bit *= radix
    return digits


def gather_step(x, bit, radix):
    return [x] + [exchange(x, bit * offset) for offset in range(1, radix)]


def gather_far(x, digits):
    return gather_step(x, *digits[-1])


def gather_near(x, digits):
    pieces = [x]
    for digit in digits[-2:0:-1]:
        pieces = gather_step(jnp.concatenate(pieces, axis=0), *digit)
    return pieces


def gather_last(pieces, digits):
    x = jnp.concatenate(pieces, axis=0)
    return x, exchange(x, digits[0][0])


def scatter_near(position, kept, sent, digits, local):
    received = [exchange(sent, digits[0][0])]
    for bit, radix in digits[1:-1]:
        kept, *sent = combine(position, kept, received, bit, radix, local, bf16)
        received = [exchange(part, bit * (1 + number)) for number, part in enumerate(sent)]
    return kept, received


def scatter_far(position, kept, received, digits, local):
    bit, radix = digits[-1]
    kept, *sent = combine(position, kept, received, bit, radix, local, f32)
    return [kept] + [exchange(part, bit * (1 + number)) for number, part in enumerate(sent)]


def share_far(position, kept, received, digits, local):
    bit, radix = digits[-1]
    (own,) = combine(position, kept, received, bit, radix, local, bf16, together=True)
    return gather_step(own, bit, radix)


def body(
    peripheral, hubs, tiles, tile_rows, local_cols, tile_count, send_list, hub_place, w_in, w_out
):
    position = lax.axis_index("dev")
    digits = all_digits()
    block_size = tiles.shape[1]
    width = peripheral.shape[1]
    own_count = peripheral.shape[0] // block_size
    hub_rows = hub_place.shape[0]
    hub_count = hub_rows // block_size
    local = hubs.shape[0]
    rows = jnp.where(tile_rows < hub_count, tile_rows, tile_rows - position * own_count)
    cols = jnp.where(local_cols < hub_count, local_cols, local_cols - position * own_count)
    place_col = hub_place.reshape(hub_rows, 1)
    place_row = hub_place.reshape(1, hub_rows)
    me = position.astype(jnp.int32).reshape(1)
    own = peripheral.reshape(own_count, block_size, width)
    all_to_all = functools.partial(
        lax.all_to_all, axis_name="dev", split_axis=0, concat_axis=0, tiled=True
    )

    pieces = gather_far(hubs, digits)
    own, rows, cols, *pieces = lax.optimization_barrier((own, rows, cols, *pieces))
    outgoing = pack(send_list, own)
    pieces = gather_near(jnp.concatenate(pieces, axis=0), digits)
    outgoing, place_col, *pieces = lax.optimization_barrier((outgoing, place_col, *pieces))
    incoming = all_to_all(outgoing)
    halves = gather_last(pieces, digits)
    hub_table, mine, kept, sent = hub_first(
        digits, rows, cols, tile_count, me, place_col, halves, own, tiles, local
    )
    base, done = before(0, rows, cols, tile_count, hub_table, own, tiles, w_in, w_out)
    kept, received = scatter_near(me, kept, sent, digits, local)
    base, done, *received = lax.optimization_barrier((base, done, *received))
    parts = share_far(me, kept, received, digits, local)
    done, sums, outgoing = after(
        0, rows, send_list, base, done, incoming, tiles, w_in, w_out, hub_count, True
    )
    outgoing, *parts = lax.optimization_barrier((outgoing, *parts))
    hub_new = hub_network(0, local, mine, parts, w_in, w_out)

    pieces = gather_near(hub_new, digits)
    outgoing, *pieces = lax.optimization_barrier((outgoing, *pieces))
    incoming = all_to_all(outgoing)
    own = late(0, rows, send_list, sums, done, w_in, w_out, hub_count)
    halves = gather_last(pieces, digits)
    hub_table, mine, kept, sent = hub_second(
        digits, rows, cols, tile_count, me, place_row, halves, own, tiles, local
    )
    base, done = before(1, rows, cols, tile_count, hub_table, own, tiles, w_in, w_out)
    kept, received = scatter_near(me, kept, sent, digits, local)
    base, done, *received = lax.optimization_barrier((base, done, *received))
    parts = scatter_far(me, kept, received, digits, local)
    (peri_out,) = after(
        1, rows, send_list, base, done, incoming, tiles, w_in, w_out, hub_count, False
    )
    peri_out, *parts = lax.optimization_barrier((peri_out, *parts))
    hub_out = hub_network(1, local, mine, parts, w_in, w_out)
    return (peri_out.reshape(peripheral.shape), hub_out)


def solution(mesh):
    in_specs = (
        P("dev", None),
        P("dev", None),
        P("dev", None, None),
        P("dev"),
        P("dev"),
        P("dev"),
        P("dev", None),
        P(),
        P(),
        P(),
    )
    out_specs = (P("dev", None), P("dev", None))
    return jax.shard_map(body, mesh=mesh, in_specs=in_specs, out_specs=out_specs, check_vma=False)
```

```python
import functools

import jax
import jax.numpy as jnp
from jax import lax
from jax.experimental import pallas as pl
from jax.experimental.pallas import tpu as pltpu
from jax.sharding import PartitionSpec as P

epsilon = 1e-06
f32 = jnp.float32
bf16 = jnp.bfloat16
MIB = 1024 * 1024
VMEM = pl.BlockSpec(memory_space=pltpu.VMEM)
SMEM = pl.BlockSpec(memory_space=pltpu.SMEM)
ANY = pl.BlockSpec(memory_space=pl.ANY)
GROUP = 4
SLOTS = 8


def dot(a, b):
    return jnp.dot(a, b, preferred_element_type=f32)


def shape_of(shape, dtype):
    return jax.ShapeDtypeStruct(tuple(shape), dtype)


def call(kernel, name, mib, flops, moved, out_shape, in_specs, out_specs, scratch, args):
    return pl.pallas_call(
        kernel,
        out_shape=out_shape,
        in_specs=in_specs,
        out_specs=out_specs,
        scratch_shapes=scratch,
        compiler_params=pltpu.CompilerParams(vmem_limit_bytes=mib * MIB),
        cost_estimate=pl.CostEstimate(flops=flops, bytes_accessed=moved, transcendentals=0),
        name=name,
    )(*args)


def normalise(u):
    return (u * lax.rsqrt(jnp.mean(u * u, axis=-1, keepdims=True) + epsilon)).astype(bf16)


def network(u, first, second, hidden_step):
    normed = normalise(u)
    total = u
    for start in range(0, first.shape[-1], hidden_step):
        cut = slice(start, start + hidden_step)
        hidden = jnp.maximum(dot(normed, first[:, cut]), 0.0).astype(bf16)
        total = total + dot(hidden, second[cut, :])
    return total.astype(bf16)


SLOT, ROW, COL, BLOCK, REMOTE, GOING, COUNTS = range(7)
N_HUB, N_OWN, N_NOW, N_FED, N_HELD = range(5)


def ranked(key, size):
    down = lax.broadcasted_iota(jnp.int32, (size, size), 0)
    along = lax.broadcasted_iota(jnp.int32, (size, size), 1)
    wide = jnp.broadcast_to(key, (size, size))
    tall = jnp.sum(jnp.where(down == along, wide, 0), axis=1, keepdims=True)
    ahead = (wide < tall) | ((wide == tall) & (along < down))
    return jnp.sum(ahead.astype(jnp.int32), axis=1, keepdims=True)


def plan_kernel(hub_count, own_count, remote, position, count, rows_in, cols_in, chosen, plan):
    capacity = rows_in.shape[1]
    shift = position[0] * own_count
    rows = jnp.where(rows_in[...] < hub_count, rows_in[...], rows_in[...] - shift)
    cols = jnp.where(cols_in[...] < hub_count, cols_in[...], cols_in[...] - shift)
    plan[...] = jnp.zeros_like(plan)
    slot = lax.broadcasted_iota(jnp.int32, (1, capacity), 1)
    picked = (slot >= remote) & (slot < count[0])
    of_hub = picked & (rows < hub_count)
    of_own = picked & (rows >= hub_count)
    key = jnp.where(of_hub, 0, jnp.where(of_own, 1, 2))
    place = ranked(key, capacity)
    down = lax.broadcasted_iota(jnp.int32, (capacity, capacity), 0)
    along = lax.broadcasted_iota(jnp.int32, (capacity, capacity), 1)
    here = place == along

    def column(row):
        wide = jnp.broadcast_to(row, (capacity, capacity))
        return jnp.sum(jnp.where(down == along, wide, 0), axis=1, keepdims=True)

    def ordered(values):
        return jnp.sum(jnp.where(here, values, 0), axis=0, keepdims=True)

    plan[SLOT : SLOT + 1, :capacity] = ordered(down)
    plan[ROW : ROW + 1, :capacity] = ordered(column(rows))
    plan[COL : COL + 1, :capacity] = ordered(column(cols))

    block = lax.broadcasted_iota(jnp.int32, (own_count, remote), 0)
    target = rows[:, :remote] - hub_count
    fed = jnp.max((block == target).astype(jnp.int32), axis=1, keepdims=True)
    sent = jnp.max((block == chosen[...]).astype(jnp.int32), axis=1, keepdims=True)
    key = 3 - 2 * fed - sent
    down = lax.broadcasted_iota(jnp.int32, (own_count, own_count), 0)
    along = lax.broadcasted_iota(jnp.int32, (own_count, own_count), 1)
    row_key = jnp.sum(jnp.where(down == along, key, 0), axis=0, keepdims=True)
    place = ranked(row_key, own_count)
    plan[BLOCK : BLOCK + 1, :own_count] = jnp.sum(
        jnp.where(place == along, down, 0), axis=0, keepdims=True
    )
    plan[REMOTE : REMOTE + 1, :remote] = jnp.sum(
        jnp.where(block == target, place, 0), axis=0, keepdims=True
    )
    plan[GOING : GOING + 1, :remote] = jnp.sum(
        jnp.where(block == chosen[...], place, 0), axis=0, keepdims=True
    )
    numbers = [
        jnp.sum(of_hub.astype(jnp.int32), axis=1, keepdims=True),
        jnp.sum(of_own.astype(jnp.int32), axis=1, keepdims=True),
        jnp.sum((row_key < 1).astype(jnp.int32), axis=1, keepdims=True),
        jnp.sum((row_key < 2).astype(jnp.int32), axis=1, keepdims=True),
        jnp.sum((row_key < 3).astype(jnp.int32), axis=1, keepdims=True),
    ]
    lane = lax.broadcasted_iota(jnp.int32, (1, plan.shape[1]), 1)
    counts = jnp.zeros((1, plan.shape[1]), jnp.int32)
    for place, number in enumerate(numbers):
        counts = jnp.where(lane == place, number, counts)
    plan[COUNTS : COUNTS + 1, :] = counts


def make_plan(position, count, rows, cols, chosen, hub_count, own_count):
    capacity, remote = rows.shape[0], chosen.shape[1]
    wide = -(-max(capacity, own_count, remote) // 128) * 128
    cols = jnp.concatenate([jnp.zeros((remote,), jnp.int32), cols])
    return call(
        functools.partial(plan_kernel, hub_count, own_count, remote),
        "plan",
        24,
        10**6,
        10**4,
        shape_of((8, wide), jnp.int32),
        [SMEM, SMEM, VMEM, VMEM, VMEM],
        VMEM,
        [],
        (position, count, rows.reshape(1, capacity), cols.reshape(1, capacity), chosen),
    )


def tile_loads(source, tiles, sems):
    remote = source.shape[0] - tiles.shape[0]
    size = tiles.shape[0] // 4
    loads = []
    for part in range(4):
        cut = pl.ds(remote + part * size, size)
        copy = pltpu.make_async_copy(source.at[cut], tiles.at[pl.ds(part * size, size)], sems.at[part])
        loads.append((remote + part * size, copy))
    return loads


def for_live(count, loads, act):
    for first_slot, load in loads:

        @pl.when(count[0] > first_slot)
        def _(load=load):
            act(load)


def add_products(plan, begin, found, remote, tiles, hubs, own, total, shift, spare):
    hub_count = hubs.shape[0]

    def step(number, unused):
        where, products = [], []
        for lane in range(SLOTS):
            place = number * SLOTS + lane
            live = place < found
            place = begin + jnp.minimum(place, found - 1)
            where.append(jnp.where(live, plan[ROW, place] - shift, spare))
            col = plan[COL, place]
            of_hub = hubs[jnp.minimum(col, hub_count - 1)]
            of_own = own[jnp.maximum(col - hub_count, 0)]
            tile = tiles[plan[SLOT, place] - remote]
            products.append(dot(tile, jnp.where(col < hub_count, of_hub, of_own)))
        for row, product in zip(where, products):
            total[row] += product
        return unused

    lax.fori_loop(0, (found + SLOTS - 1) // SLOTS, step, 0)


def each_block(first_place, last_place, copy_of, act):
    def step(place, unused):
        act(copy_of(place))
        return unused

    lax.fori_loop(first_place, last_place, step, 0)


def start(copy):
    copy.start()


def wait(copy):
    copy.wait()


def rounded_up(number):
    return (number + GROUP - 1) // GROUP


def finish_group(first_place, begin, end, finish):
    for lane in range(GROUP):
        place = first_place + lane

        @pl.when((place >= begin) & (place < end))
        def _(place=place):
            finish(place).start()


def pack_kernel(chosen, blocks, outgoing, held, sems):
    load = pltpu.make_async_copy(blocks, held, sems.at[0])
    load.start()
    load.wait()
    copies = []
    for number in range(outgoing.shape[0]):
        copy = pltpu.make_async_copy(
            held.at[chosen[0, number]], outgoing.at[number], sems.at[number]
        )
        copy.start()
        copies.append(copy)
    for copy in copies:
        copy.wait()


def pack(chosen, blocks):
    devices = chosen.shape[1]
    return call(
        pack_kernel,
        "pack",
        58,
        0,
        2 * blocks.size * 2,
        shape_of((devices,) + blocks.shape[1:], bf16),
        [SMEM, ANY],
        ANY,
        [pltpu.VMEM(blocks.shape, bf16), pltpu.SemaphoreType.DMA((devices,))],
        (chosen, blocks),
    )


def slot_place(slot, digits):
    place, weight = 0, 1
    for bit, radix in digits[:0:-1]:
        place += weight * ((slot // bit) % radix)
        weight *= radix
    return slot % 2, place


def place_shards(me, halves, table, digits, local):
    for slot in range(table.shape[0] // local):
        half, place = slot_place(slot, digits)
        start = pl.multiple_of((me ^ slot) * local, local)
        table[pl.ds(start, local), :] = halves[half][place * local : (place + 1) * local, :]


def split_sums(me, sums, local, kept, sent):
    odd = me % 2
    width = sums.shape[-1]
    pairs = sums.reshape(-1, 2, local, width)
    kept[...] = jnp.where(odd == 1, pairs[:, 1], pairs[:, 0]).reshape(kept.shape).astype(kept.dtype)
    sent[...] = jnp.where(odd == 1, pairs[:, 0], pairs[:, 1]).reshape(sent.shape).astype(sent.dtype)


def hub_first_kernel(
    digits, plan, count, position, place_col, half0, half1, own_hbm, tiles_hbm,
    hubs, mine, kept, sent, own, tiles, table, total, sems,
):
    hub_count, block_size, width = hubs.shape
    hub_rows = hub_count * block_size
    local = mine.shape[0]
    remote = tiles_hbm.shape[0] - tiles.shape[0]
    loads = tile_loads(tiles_hbm, tiles, sems)
    load = pltpu.make_async_copy(own_hbm, own, sems.at[4])
    load.start()
    for_live(count, loads, start)
    me = position[0]
    place_shards(me, (half0, half1), table, digits, local)
    total[...] = jnp.zeros_like(total)
    step = 2 * block_size

    def rows_step(number, unused):
        cut = pl.ds(pl.multiple_of(number * step, step), step)
        lanes = lax.broadcasted_iota(jnp.int32, (step, hub_rows), 1)
        unit = jnp.where(place_col[cut, :] == lanes, 1.0, 0.0).astype(bf16)
        placed = dot(unit, table[...]).astype(bf16)
        hubs[pl.ds(number * 2, 2)] = placed.reshape(2, block_size, width)
        return unused

    lax.fori_loop(0, hub_rows // step, rows_step, 0)
    load.wait()
    for_live(count, loads, wait)
    add_products(plan, 0, plan[COUNTS, N_HUB], remote, tiles, hubs, own, total, 0, hub_count)
    split_sums(me, total[:hub_count], local, kept, sent)
    flat = hubs.reshape(hub_rows, width)
    mine[...] = flat[pl.ds(pl.multiple_of(me * local, local), local), :]


def hub_first(digits, plan, count, position, place_col, halves, own, tiles, local, remote):
    block_size, width = own.shape[1:]
    hub_rows = place_col.shape[0]
    hub_count = hub_rows // block_size
    half = shape_of((hub_rows // 2, width), f32)
    return call(
        functools.partial(hub_first_kernel, digits),
        "hub_first",
        48,
        2 * hub_rows * hub_rows * width,
        14 * MIB,
        (
            shape_of((hub_count, block_size, width), bf16),
            shape_of((local, width), bf16),
            half,
            half,
        ),
        [SMEM] * 3 + [VMEM] * 3 + [ANY] * 2,
        (VMEM,) * 4,
        [
            pltpu.VMEM(own.shape, bf16),
            pltpu.VMEM((tiles.shape[0] - remote,) + tiles.shape[1:], bf16),
            pltpu.VMEM((hub_rows, width), bf16),
            pltpu.VMEM((hub_count + 1, block_size, width), f32),
            pltpu.SemaphoreType.DMA((5,)),
        ],
        (plan, count, position, place_col) + tuple(halves) + (own, tiles),
    )


def hub_second_kernel(
    digits, plan, count, position, place_row, half0, half1, own_hbm, tiles_hbm,
    hubs, mine, kept, sent, own, tiles, total, placed, sems,
):
    hub_count, block_size, width = hubs.shape
    hub_rows = hub_count * block_size
    local = mine.shape[0]
    remote = tiles_hbm.shape[0] - tiles.shape[0]
    loads = tile_loads(tiles_hbm, tiles, sems)
    load = pltpu.make_async_copy(own_hbm, own, sems.at[4])
    load.start()
    for_live(count, loads, start)
    me = position[0]
    flat = hubs.reshape(hub_rows, width)
    place_shards(me, (half0, half1), flat, digits, local)
    total[...] = jnp.zeros_like(total)

    def unit_rows(start, step):
        down = lax.broadcasted_iota(jnp.int32, (step, hub_rows), 0) + start
        return jnp.where(place_row[...] == down, 1.0, 0.0).astype(bf16)

    mine[...] = dot(unit_rows(me * local, local), flat[...]).astype(bf16)
    load.wait()
    for_live(count, loads, wait)
    add_products(plan, 0, plan[COUNTS, N_HUB], remote, tiles, hubs, own, total, 0, hub_count)
    sums = total[:hub_count].reshape(hub_rows, width)
    high = sums.astype(bf16)
    low = (sums - high.astype(f32)).astype(bf16)
    step = 2 * block_size

    def rows_step(number, unused):
        start = number * step
        unit = unit_rows(start, step)
        placed[pl.ds(pl.multiple_of(start, step), step), :] = dot(unit, high) + dot(unit, low)
        return unused

    lax.fori_loop(0, hub_rows // step, rows_step, 0)
    split_sums(me, placed[...], local, kept, sent)


def hub_second(digits, plan, count, position, place_row, halves, own, tiles, local, remote):
    block_size, width = own.shape[1:]
    hub_rows = place_row.shape[1]
    hub_count = hub_rows // block_size
    return call(
        functools.partial(hub_second_kernel, digits),
        "hub_second",
        48,
        2 * hub_rows * hub_rows * width,
        14 * MIB,
        (
            shape_of((hub_count, block_size, width), bf16),
            shape_of((local, width), bf16),
            shape_of((hub_rows // 2, width), f32),
            shape_of((hub_rows // 2, width), f32),
        ),
        [SMEM] * 3 + [VMEM] * 3 + [ANY] * 2,
        (VMEM,) * 4,
        [
            pltpu.VMEM(own.shape, bf16),
            pltpu.VMEM((tiles.shape[0] - remote,) + tiles.shape[1:], bf16),
            pltpu.VMEM((hub_count + 1, block_size, width), f32),
            pltpu.VMEM((hub_rows, width), f32),
            pltpu.SemaphoreType.DMA((5,)),
        ],
        (plan, count, position, place_row) + tuple(halves) + (own, tiles),
    )


def combine(position, kept, received, bit, radix, local, sent_type):
    rows = kept.shape[0] // radix
    width = kept.shape[1]

    def kernel(position, kept_in, *refs):
        received, outs = refs[: -radix], refs[-radix:]
        total = kept_in[...].astype(f32)
        for part in received:
            total = total + part[...].astype(f32)
        digit = (position[0] // bit) % radix
        parts = total.reshape(rows // local, radix, local, width)
        for offset, out in enumerate(outs):
            value = parts[:, 0]
            for number in range(1, radix):
                value = jnp.where((digit ^ offset) == number, parts[:, number], value)
            out[...] = value.reshape(rows, width).astype(out.dtype)

    shapes = [shape_of((rows, width), f32)] + [shape_of((rows, width), sent_type)] * (radix - 1)
    return call(
        kernel,
        "combine",
        16,
        kept.size,
        12 * kept.size,
        tuple(shapes),
        [SMEM] + [VMEM] * (1 + len(received)),
        (VMEM,) * radix,
        [],
        (position, kept) + tuple(received),
    )


def load_weights(layer, first_in, second_in, first, second, sems):
    loads = [
        pltpu.make_async_copy(first_in.at[layer], first, sems.at[0]),
        pltpu.make_async_copy(second_in.at[layer], second, sems.at[1]),
    ]
    for load in loads:
        load.start()
    return loads


def hub_network_kernel(layer, rows_in, *refs):
    parts, (first_in, second_in, out, first, second, sems) = refs[:-6], refs[-6:]
    loads = load_weights(layer, first_in, second_in, first, second, sems)
    u = rows_in[...].astype(f32)
    for part in parts:
        u = u + part[...].astype(f32)
    for load in loads:
        load.wait()
    out[...] = network(u, first, second, first.shape[-1])


def hub_network(layer, rows_in, parts, first, second):
    return call(
        functools.partial(hub_network_kernel, layer),
        "hub_network",
        24,
        4 * rows_in.size * first.shape[-1],
        2 * first.size,
        shape_of(rows_in.shape, bf16),
        [VMEM] * (1 + len(parts)) + [ANY] * 2,
        VMEM,
        [
            pltpu.VMEM(first.shape[1:], bf16),
            pltpu.VMEM(second.shape[1:], bf16),
            pltpu.SemaphoreType.DMA((2,)),
        ],
        (rows_in,) + tuple(parts) + (first, second),
    )


def before_kernel(
    layer, plan, count, hubs_in, own_in, tiles_in, first_in, second_in, base, out,
    hubs, own, tiles, first, second, u, result, tile_sems, block_sems, sem,
):
    own_count = own.shape[0]
    hub_count = hubs.shape[0]
    remote = tiles_in.shape[0] - tiles.shape[0]
    load_own = pltpu.make_async_copy(own_in, own, sem.at[0])
    load_hubs = pltpu.make_async_copy(hubs_in, hubs, sem.at[1])
    loads = tile_loads(tiles_in, tiles, tile_sems)
    load_own.start()
    load_hubs.start()
    for_live(count, loads, start)
    load_own.wait()
    u[:own_count] = own[...].astype(f32)
    load_hubs.wait()
    for_live(count, loads, wait)
    weights = load_weights(layer, first_in, second_in, first, second, sem.at[pl.ds(2, 2)])
    n_fed = plan[COUNTS, N_FED]
    add_products(
        plan, plan[COUNTS, N_HUB], plan[COUNTS, N_OWN], remote, tiles, hubs, own, u, hub_count, own_count
    )

    def save(place):
        return pltpu.make_async_copy(u.at[plan[BLOCK, place]], base.at[place], block_sems.at[place])

    def finish(place):
        block = plan[BLOCK, place]
        return pltpu.make_async_copy(result.at[place], out.at[block], block_sems.at[place])

    each_block(0, n_fed, save, start)
    for load in weights:
        load.wait()

    def step(number, unused):
        first_place = number * GROUP
        places = [first_place + lane for lane in range(GROUP)]
        values = jnp.concatenate([u[plan[BLOCK, place]] for place in places], axis=0)
        values = network(values, first, second, 512)
        result[pl.ds(first_place, GROUP)] = values.reshape((GROUP,) + result.shape[1:])
        finish_group(first_place, n_fed, own_count, finish)
        return unused

    lax.fori_loop(n_fed // GROUP, own_count // GROUP, step, 0)
    each_block(0, n_fed, save, wait)
    each_block(n_fed, own_count, finish, wait)


def before(layer, plan, count, hubs, own, tiles, first, second, remote):
    own_count, block_size, width = own.shape
    return call(
        functools.partial(before_kernel, layer),
        "before",
        58,
        4 * own.size * first.shape[-1] // 3,
        18 * MIB,
        (shape_of(own.shape, f32), shape_of(own.shape, bf16)),
        [SMEM] * 2 + [ANY] * 5,
        (ANY, ANY),
        [
            pltpu.VMEM(hubs.shape, bf16),
            pltpu.VMEM(own.shape, bf16),
            pltpu.VMEM((tiles.shape[0] - remote,) + tiles.shape[1:], bf16),
            pltpu.VMEM(first.shape[1:], bf16),
            pltpu.VMEM(second.shape[1:], bf16),
            pltpu.VMEM((own_count + 1, block_size, width), f32),
            pltpu.VMEM(own.shape, bf16),
            pltpu.SemaphoreType.DMA((4,)),
            pltpu.SemaphoreType.DMA((own_count,)),
            pltpu.SemaphoreType.DMA((4,)),
        ],
        (plan, count, hubs, own, tiles, first, second),
    )


def after_kernel(
    layer, with_send, plan, base, done, incoming, tiles, first_in, second_in, *refs
):
    out, refs = refs[0], refs[1:]
    if with_send:
        (sums, outgoing), refs = refs[:2], refs[2:]
    u, extra, inc, adj, first, second, result, base_sems, block_sems, sem = refs
    own_count = u.shape[0]
    remote = incoming.shape[0]
    parts = 4
    size = remote // parts
    loads = []
    for part in range(parts):
        cut = pl.ds(part * size, size)
        loads.append(
            (
                pltpu.make_async_copy(tiles.at[cut], adj.at[cut], sem.at[2 + 2 * part]),
                pltpu.make_async_copy(incoming.at[cut], inc.at[cut], sem.at[3 + 2 * part]),
            )
        )
        for load in loads[-1]:
            load.start()
    n_fed, n_held = plan[COUNTS, N_FED], plan[COUNTS, N_HELD]
    groups = rounded_up(n_fed)
    groups_now = rounded_up(plan[COUNTS, N_NOW]) if with_send else groups
    apart = jnp.minimum(groups * GROUP, n_held)

    def cut_of(group):
        return pl.ds(group * GROUP, GROUP)

    def load_base(group):
        cut = cut_of(group)
        return pltpu.make_async_copy(base.at[cut], u.at[cut], base_sems.at[group])

    def load_done(place):
        block = plan[BLOCK, place]
        return pltpu.make_async_copy(done.at[block], result.at[place], block_sems.at[place])

    def finish(place):
        block = plan[BLOCK, place]
        return pltpu.make_async_copy(result.at[place], out.at[block], block_sems.at[place])

    extra[...] = jnp.zeros_like(extra)
    for part in range(parts):
        for load in loads[part]:
            load.wait()
        if part == 0:
            weights = load_weights(layer, first_in, second_in, first, second, sem.at[pl.ds(0, 2)])
            each_block(0, groups, load_base, start)
            if with_send:
                each_block(apart, n_held, load_done, start)
        products = [dot(adj[slot], inc[slot]) for slot in range(part * size, (part + 1) * size)]
        for lane, product in enumerate(products):
            extra[plan[REMOTE, part * size + lane]] += product
    for load in weights:
        load.wait()
    n_now = jnp.minimum(groups_now * GROUP, n_fed)

    def step(group, unused):
        load_base(group).wait()
        cut = cut_of(group)
        values = (u[cut] + extra[cut]).reshape(GROUP * u.shape[1], u.shape[2])
        values = network(values, first, second, 512)
        result[cut] = values.reshape((GROUP,) + result.shape[1:])
        finish_group(group * GROUP, 0, n_now, finish)
        return unused

    lax.fori_loop(0, groups_now, step, 0)
    copies = []
    if with_send:
        each_block(n_fed, apart, load_done, start)
        each_block(n_fed, n_held, load_done, wait)
        for number in range(remote):
            copy = pltpu.make_async_copy(
                result.at[plan[GOING, number]], outgoing.at[number], sem.at[number]
            )
            copy.start()
            copies.append(copy)

        def save(group):
            cut = cut_of(group)
            return pltpu.make_async_copy(u.at[cut], sums.at[cut], base_sems.at[group])

        def keep(group, unused):
            load_base(group).wait()
            cut = cut_of(group)
            u[cut] += extra[cut]
            save(group).start()
            return unused

        lax.fori_loop(groups_now, groups, keep, 0)
        each_block(groups_now, groups, save, wait)
    each_block(0, n_now, finish, wait)
    for copy in copies:
        copy.wait()


def after(layer, plan, base, done, incoming, tiles, first, second, with_send):
    own_count = base.shape[0]
    remote = incoming.shape[0]
    shapes = [shape_of(base.shape, bf16)]
    if with_send:
        shapes += [shape_of(base.shape, f32), shape_of(incoming.shape, bf16)]
    return pl.pallas_call(
        functools.partial(after_kernel, layer, with_send),
        out_shape=tuple(shapes),
        in_specs=[SMEM] + [ANY] * 6,
        out_specs=(ANY,) * len(shapes),
        scratch_shapes=[
            pltpu.VMEM(base.shape, f32),
            pltpu.VMEM(base.shape, f32),
            pltpu.VMEM(incoming.shape, bf16),
            pltpu.VMEM((remote,) + tiles.shape[1:], bf16),
            pltpu.VMEM(first.shape[1:], bf16),
            pltpu.VMEM(second.shape[1:], bf16),
            pltpu.VMEM(base.shape, bf16),
            pltpu.SemaphoreType.DMA((own_count // GROUP,)),
            pltpu.SemaphoreType.DMA((own_count,)),
            pltpu.SemaphoreType.DMA((max(10, remote),)),
        ],
        input_output_aliases={2: 0, 1: 1} if with_send else {2: 0},
        compiler_params=pltpu.CompilerParams(vmem_limit_bytes=58 * MIB),
        cost_estimate=pl.CostEstimate(
            flops=4 * base.size * first.shape[-1], bytes_accessed=16 * MIB, transcendentals=0
        ),
        name="after",
    )(plan, base, done, incoming, tiles, first, second)


def late_kernel(
    layer, plan, sums, done, first_in, second_in, out, u, first, second, result, base_sems, block_sems, sem
):
    weights = load_weights(layer, first_in, second_in, first, second, sem)
    n_fed = plan[COUNTS, N_FED]
    groups = rounded_up(n_fed)
    groups_now = rounded_up(plan[COUNTS, N_NOW])

    def load(group):
        cut = pl.ds(group * GROUP, GROUP)
        return pltpu.make_async_copy(sums.at[cut], u.at[cut], base_sems.at[group])

    def finish(place):
        block = plan[BLOCK, place]
        return pltpu.make_async_copy(result.at[place], out.at[block], block_sems.at[place])

    each_block(groups_now, groups, load, start)
    for part in weights:
        part.wait()

    def step(group, unused):
        load(group).wait()
        cut = pl.ds(group * GROUP, GROUP)
        values = network(u[cut].reshape(GROUP * u.shape[1], u.shape[2]), first, second, 512)
        result[cut] = values.reshape((GROUP,) + result.shape[1:])
        finish_group(group * GROUP, 0, n_fed, finish)
        return unused

    lax.fori_loop(groups_now, groups, step, 0)
    each_block(jnp.minimum(groups_now * GROUP, n_fed), n_fed, finish, wait)


def late(layer, plan, sums, done, first, second):
    own_count = sums.shape[0]
    return pl.pallas_call(
        functools.partial(late_kernel, layer),
        out_shape=shape_of(done.shape, bf16),
        in_specs=[SMEM] + [ANY] * 4,
        out_specs=ANY,
        scratch_shapes=[
            pltpu.VMEM(sums.shape, f32),
            pltpu.VMEM(first.shape[1:], bf16),
            pltpu.VMEM(second.shape[1:], bf16),
            pltpu.VMEM(sums.shape, bf16),
            pltpu.SemaphoreType.DMA((own_count // GROUP,)),
            pltpu.SemaphoreType.DMA((own_count,)),
            pltpu.SemaphoreType.DMA((2,)),
        ],
        input_output_aliases={2: 0},
        compiler_params=pltpu.CompilerParams(vmem_limit_bytes=58 * MIB),
        cost_estimate=pl.CostEstimate(
            flops=sums.size * first.shape[-1], bytes_accessed=5 * MIB, transcendentals=0
        ),
        name="late",
    )(plan, sums, done, first, second)


def exchange(x, bit):
    devices = lax.axis_size("dev")
    return lax.ppermute(x, "dev", [(i, i ^ bit) for i in range(devices)])


def all_digits():
    devices = lax.axis_size("dev")
    digits, bit = [(1, 2)], 2
    while bit < devices:
        radix = 4 if 4 * bit <= devices else 2
        digits.append((bit, radix))
        bit *= radix
    return digits


def gather_step(x, bit, radix):
    return [x] + [exchange(x, bit * offset) for offset in range(1, radix)]


def gather_far(x, digits):
    return gather_step(x, *digits[-1])


def gather_near(pieces, digits):
    for digit in digits[-2:0:-1]:
        pieces = gather_step(jnp.concatenate(pieces, axis=0), *digit)
    return pieces


def gather_last(pieces, digits):
    x = jnp.concatenate(pieces, axis=0)
    return x, exchange(x, digits[0][0])


def scatter_near(position, kept, sent, digits, local):
    received = [exchange(sent, digits[0][0])]
    for bit, radix in digits[1:-1]:
        kept, *sent = combine(position, kept, received, bit, radix, local, bf16)
        received = [exchange(part, bit * (1 + number)) for number, part in enumerate(sent)]
    return kept, received


def scatter_far(position, kept, received, digits, local, sent_type):
    bit, radix = digits[-1]
    kept, *sent = combine(position, kept, received, bit, radix, local, sent_type)
    return [kept] + [exchange(part, bit * (1 + number)) for number, part in enumerate(sent)]


def body(
    peripheral, hubs, tiles, tile_rows, local_cols, tile_count, send_list, hub_place, w_in, w_out
):
    position = lax.axis_index("dev")
    digits = all_digits()
    block_size = tiles.shape[1]
    width = peripheral.shape[1]
    own_count = peripheral.shape[0] // block_size
    hub_rows = hub_place.shape[0]
    hub_count = hub_rows // block_size
    local = hubs.shape[0]
    remote = send_list.shape[1]
    place_col = hub_place.reshape(hub_rows, 1)
    place_row = hub_place.reshape(1, hub_rows)
    me = position.astype(jnp.int32).reshape(1)
    own = peripheral.reshape(own_count, block_size, width)
    all_to_all = functools.partial(
        lax.all_to_all, axis_name="dev", split_axis=0, concat_axis=0, tiled=True
    )

    pieces = gather_far(hubs, digits)
    plan = make_plan(me, tile_count, tile_rows, local_cols, send_list, hub_count, own_count)
    own, plan, *pieces = lax.optimization_barrier((own, plan, *pieces))
    outgoing = pack(send_list, own)
    pieces = gather_near(pieces, digits)
    outgoing, place_col, *pieces = lax.optimization_barrier((outgoing, place_col, *pieces))
    incoming = all_to_all(outgoing)
    halves = gather_last(pieces, digits)
    hub_table, mine, kept, sent = hub_first(
        digits, plan, tile_count, me, place_col, halves, own, tiles, local, remote
    )
    base, done = before(0, plan, tile_count, hub_table, own, tiles, w_in, w_out, remote)
    kept, received = scatter_near(me, kept, sent, digits, local)
    base, done, *received = lax.optimization_barrier((base, done, *received))
    parts = scatter_far(me, kept, received, digits, local, bf16)
    hub_new = hub_network(0, mine, parts, w_in, w_out)
    pieces = gather_far(hub_new, digits)
    base, *pieces = lax.optimization_barrier((base, *pieces))
    done, sums, outgoing = after(0, plan, base, done, incoming, tiles, w_in, w_out, True)

    pieces = gather_near(pieces, digits)
    outgoing, *pieces = lax.optimization_barrier((outgoing, *pieces))
    incoming = all_to_all(outgoing)
    own = late(0, plan, sums, done, w_in, w_out)
    halves = gather_last(pieces, digits)
    hub_table, mine, kept, sent = hub_second(
        digits, plan, tile_count, me, place_row, halves, own, tiles, local, remote
    )
    base, done = before(1, plan, tile_count, hub_table, own, tiles, w_in, w_out, remote)
    kept, received = scatter_near(me, kept, sent, digits, local)
    base, done, *received = lax.optimization_barrier((base, done, *received))
    parts = scatter_far(me, kept, received, digits, local, f32)
    (peri_out,) = after(1, plan, base, done, incoming, tiles, w_in, w_out, False)
    peri_out, *parts = lax.optimization_barrier((peri_out, *parts))
    hub_out = hub_network(1, mine, parts, w_in, w_out)
    return (peri_out.reshape(peripheral.shape), hub_out)


def solution(mesh):
    in_specs = (
        P("dev", None),
        P("dev", None),
        P("dev", None, None),
        P("dev"),
        P("dev"),
        P("dev"),
        P("dev", None),
        P(),
        P(),
        P(),
    )
    out_specs = (P("dev", None), P("dev", None))
    return jax.shard_map(body, mesh=mesh, in_specs=in_specs, out_specs=out_specs, check_vma=False)
```

```python
import functools

import jax
import jax.numpy as jnp
from jax import lax
from jax.experimental import pallas as pl
from jax.experimental.pallas import tpu as pltpu
from jax.sharding import PartitionSpec as P

epsilon = 1e-06
f32 = jnp.float32
bf16 = jnp.bfloat16
MIB = 1024 * 1024
VMEM = pl.BlockSpec(memory_space=pltpu.VMEM)
SMEM = pl.BlockSpec(memory_space=pltpu.SMEM)
ANY = pl.BlockSpec(memory_space=pl.ANY)
GROUP = 4
SLOTS = 8


def dot(a, b):
    return jnp.dot(a, b, preferred_element_type=f32)


def shape_of(shape, dtype):
    return jax.ShapeDtypeStruct(tuple(shape), dtype)


def call(kernel, name, mib, flops, moved, out_shape, in_specs, out_specs, scratch, args):
    return pl.pallas_call(
        kernel,
        out_shape=out_shape,
        in_specs=in_specs,
        out_specs=out_specs,
        scratch_shapes=scratch,
        compiler_params=pltpu.CompilerParams(vmem_limit_bytes=mib * MIB),
        cost_estimate=pl.CostEstimate(flops=flops, bytes_accessed=moved, transcendentals=0),
        name=name,
    )(*args)


def normalise(u):
    return (u * lax.rsqrt(jnp.mean(u * u, axis=-1, keepdims=True) + epsilon)).astype(bf16)


def network(u, first, second, hidden_step):
    normed = normalise(u)
    total = u
    for start in range(0, first.shape[-1], hidden_step):
        cut = slice(start, start + hidden_step)
        hidden = jnp.maximum(dot(normed, first[:, cut]), 0.0).astype(bf16)
        total = total + dot(hidden, second[cut, :])
    return total.astype(bf16)


SLOT, ROW, COL, BLOCK, REMOTE, GOING, COUNTS = range(7)
N_HUB, N_OWN, N_NOW, N_FED, N_HELD = range(5)


def ranked(key, size):
    down = lax.broadcasted_iota(jnp.int32, (size, size), 0)
    along = lax.broadcasted_iota(jnp.int32, (size, size), 1)
    wide = jnp.broadcast_to(key, (size, size))
    tall = jnp.sum(jnp.where(down == along, wide, 0), axis=1, keepdims=True)
    ahead = (wide < tall) | ((wide == tall) & (along < down))
    return jnp.sum(ahead.astype(jnp.int32), axis=1, keepdims=True)


def plan_kernel(hub_count, own_count, remote, position, count, rows_in, cols_in, chosen, plan):
    capacity = rows_in.shape[1]
    shift = position[0] * own_count
    rows = jnp.where(rows_in[...] < hub_count, rows_in[...], rows_in[...] - shift)
    cols = jnp.where(cols_in[...] < hub_count, cols_in[...], cols_in[...] - shift)
    plan[...] = jnp.zeros_like(plan)
    slot = lax.broadcasted_iota(jnp.int32, (1, capacity), 1)
    picked = (slot >= remote) & (slot < count[0])
    of_hub = picked & (rows < hub_count)
    of_own = picked & (rows >= hub_count)
    key = jnp.where(of_hub, 0, jnp.where(of_own, 1, 2))
    place = ranked(key, capacity)
    down = lax.broadcasted_iota(jnp.int32, (capacity, capacity), 0)
    along = lax.broadcasted_iota(jnp.int32, (capacity, capacity), 1)
    here = place == along

    def column(row):
        wide = jnp.broadcast_to(row, (capacity, capacity))
        return jnp.sum(jnp.where(down == along, wide, 0), axis=1, keepdims=True)

    def ordered(values):
        return jnp.sum(jnp.where(here, values, 0), axis=0, keepdims=True)

    plan[SLOT : SLOT + 1, :capacity] = ordered(down)
    plan[ROW : ROW + 1, :capacity] = ordered(column(rows))
    plan[COL : COL + 1, :capacity] = ordered(column(cols))

    block = lax.broadcasted_iota(jnp.int32, (own_count, remote), 0)
    target = rows[:, :remote] - hub_count
    fed = jnp.max((block == target).astype(jnp.int32), axis=1, keepdims=True)
    sent = jnp.max((block == chosen[...]).astype(jnp.int32), axis=1, keepdims=True)
    key = 3 - 2 * fed - sent
    down = lax.broadcasted_iota(jnp.int32, (own_count, own_count), 0)
    along = lax.broadcasted_iota(jnp.int32, (own_count, own_count), 1)
    row_key = jnp.sum(jnp.where(down == along, key, 0), axis=0, keepdims=True)
    place = ranked(row_key, own_count)
    plan[BLOCK : BLOCK + 1, :own_count] = jnp.sum(
        jnp.where(place == along, down, 0), axis=0, keepdims=True
    )
    plan[REMOTE : REMOTE + 1, :remote] = jnp.sum(
        jnp.where(block == target, place, 0), axis=0, keepdims=True
    )
    plan[GOING : GOING + 1, :remote] = jnp.sum(
        jnp.where(block == chosen[...], place, 0), axis=0, keepdims=True
    )
    numbers = [
        jnp.sum(of_hub.astype(jnp.int32), axis=1, keepdims=True),
        jnp.sum(of_own.astype(jnp.int32), axis=1, keepdims=True),
        jnp.sum((row_key < 1).astype(jnp.int32), axis=1, keepdims=True),
        jnp.sum((row_key < 2).astype(jnp.int32), axis=1, keepdims=True),
        jnp.sum((row_key < 3).astype(jnp.int32), axis=1, keepdims=True),
    ]
    lane = lax.broadcasted_iota(jnp.int32, (1, plan.shape[1]), 1)
    counts = jnp.zeros((1, plan.shape[1]), jnp.int32)
    for place, number in enumerate(numbers):
        counts = jnp.where(lane == place, number, counts)
    plan[COUNTS : COUNTS + 1, :] = counts


def make_plan(position, count, rows, cols, chosen, hub_count, own_count):
    capacity, remote = rows.shape[0], chosen.shape[1]
    wide = -(-max(capacity, own_count, remote) // 128) * 128
    cols = jnp.concatenate([jnp.zeros((remote,), jnp.int32), cols])
    return call(
        functools.partial(plan_kernel, hub_count, own_count, remote),
        "plan",
        24,
        10**6,
        10**4,
        shape_of((8, wide), jnp.int32),
        [SMEM, SMEM, VMEM, VMEM, VMEM],
        VMEM,
        [],
        (position, count, rows.reshape(1, capacity), cols.reshape(1, capacity), chosen),
    )


def tile_loads(source, tiles, sems):
    remote = source.shape[0] - tiles.shape[0]
    size = tiles.shape[0] // 4
    loads = []
    for part in range(4):
        cut = pl.ds(remote + part * size, size)
        copy = pltpu.make_async_copy(source.at[cut], tiles.at[pl.ds(part * size, size)], sems.at[part])
        loads.append((remote + part * size, copy))
    return loads


def for_live(count, loads, act):
    for first_slot, load in loads:

        @pl.when(count[0] > first_slot)
        def _(load=load):
            act(load)


def add_products(plan, begin, found, remote, tiles, hubs, own, total, shift, spare):
    hub_count = hubs.shape[0]

    def step(number, unused):
        where, products = [], []
        for lane in range(SLOTS):
            place = number * SLOTS + lane
            live = place < found
            place = begin + jnp.minimum(place, found - 1)
            where.append(jnp.where(live, plan[ROW, place] - shift, spare))
            col = plan[COL, place]
            of_hub = hubs[jnp.minimum(col, hub_count - 1)]
            of_own = own[jnp.maximum(col - hub_count, 0)]
            tile = tiles[plan[SLOT, place] - remote]
            products.append(dot(tile, jnp.where(col < hub_count, of_hub, of_own)))
        for row, product in zip(where, products):
            total[row] += product
        return unused

    lax.fori_loop(0, (found + SLOTS - 1) // SLOTS, step, 0)


def each_block(first_place, last_place, copy_of, act):
    def step(place, unused):
        act(copy_of(place))
        return unused

    lax.fori_loop(first_place, last_place, step, 0)


def start(copy):
    copy.start()


def wait(copy):
    copy.wait()


def run_groups(begin, end, step):
    def pair(number, unused):
        step(begin + 2 * number, 2)
        return unused

    lax.fori_loop(0, (end - begin) // 2, pair, 0)

    @pl.when((end - begin) % 2 == 1)
    def _():
        step(end - 1, 1)


def rounded_up(number):
    return (number + GROUP - 1) // GROUP


def finish_group(first_place, number, begin, end, finish):
    for lane in range(number):
        place = first_place + lane

        @pl.when((place >= begin) & (place < end))
        def _(place=place):
            finish(place).start()


def pack_kernel(chosen, blocks, outgoing, held, sems):
    load = pltpu.make_async_copy(blocks, held, sems.at[0])
    load.start()
    load.wait()
    copies = []
    for number in range(outgoing.shape[0]):
        copy = pltpu.make_async_copy(
            held.at[chosen[0, number]], outgoing.at[number], sems.at[number]
        )
        copy.start()
        copies.append(copy)
    for copy in copies:
        copy.wait()


def pack(chosen, blocks):
    devices = chosen.shape[1]
    return call(
        pack_kernel,
        "pack",
        58,
        0,
        2 * blocks.size * 2,
        shape_of((devices,) + blocks.shape[1:], bf16),
        [SMEM, ANY],
        ANY,
        [pltpu.VMEM(blocks.shape, bf16), pltpu.SemaphoreType.DMA((devices,))],
        (chosen, blocks),
    )


def slot_place(slot, digits):
    place, weight = 0, 1
    for bit, radix in digits[:0:-1]:
        place += weight * ((slot // bit) % radix)
        weight *= radix
    return slot % 2, place


def place_shards(me, halves, table, digits, local):
    for slot in range(table.shape[0] // local):
        half, place = slot_place(slot, digits)
        start = pl.multiple_of((me ^ slot) * local, local)
        table[pl.ds(start, local), :] = halves[half][place * local : (place + 1) * local, :]


def split_sums(me, sums, local, kept, sent):
    odd = me % 2
    width = sums.shape[-1]
    pairs = sums.reshape(-1, 2, local, width)
    kept[...] = jnp.where(odd == 1, pairs[:, 1], pairs[:, 0]).reshape(kept.shape).astype(kept.dtype)
    sent[...] = jnp.where(odd == 1, pairs[:, 0], pairs[:, 1]).reshape(sent.shape).astype(sent.dtype)


def hub_first_kernel(
    digits, plan, count, position, place_col, half0, half1, own_hbm, tiles_hbm,
    hubs, mine, kept, sent, own, tiles, table, total, sems,
):
    hub_count, block_size, width = hubs.shape
    hub_rows = hub_count * block_size
    local = mine.shape[0]
    remote = tiles_hbm.shape[0] - tiles.shape[0]
    loads = tile_loads(tiles_hbm, tiles, sems)
    load = pltpu.make_async_copy(own_hbm, own, sems.at[4])
    load.start()
    for_live(count, loads, start)
    me = position[0]
    place_shards(me, (half0, half1), table, digits, local)
    total[...] = jnp.zeros_like(total)
    step = 2 * block_size

    def rows_step(number, unused):
        cut = pl.ds(pl.multiple_of(number * step, step), step)
        lanes = lax.broadcasted_iota(jnp.int32, (step, hub_rows), 1)
        unit = jnp.where(place_col[cut, :] == lanes, 1.0, 0.0).astype(bf16)
        placed = dot(unit, table[...]).astype(bf16)
        hubs[pl.ds(number * 2, 2)] = placed.reshape(2, block_size, width)
        return unused

    lax.fori_loop(0, hub_rows // step, rows_step, 0)
    load.wait()
    for_live(count, loads, wait)
    add_products(plan, 0, plan[COUNTS, N_HUB], remote, tiles, hubs, own, total, 0, hub_count)
    split_sums(me, total[:hub_count], local, kept, sent)
    flat = hubs.reshape(hub_rows, width)
    mine[...] = flat[pl.ds(pl.multiple_of(me * local, local), local), :]


def hub_first(digits, plan, count, position, place_col, halves, own, tiles, local, remote):
    block_size, width = own.shape[1:]
    hub_rows = place_col.shape[0]
    hub_count = hub_rows // block_size
    half = shape_of((hub_rows // 2, width), f32)
    return call(
        functools.partial(hub_first_kernel, digits),
        "hub_first",
        48,
        2 * hub_rows * hub_rows * width,
        14 * MIB,
        (
            shape_of((hub_count, block_size, width), bf16),
            shape_of((local, width), bf16),
            half,
            half,
        ),
        [SMEM] * 3 + [VMEM] * 3 + [ANY] * 2,
        (VMEM,) * 4,
        [
            pltpu.VMEM(own.shape, bf16),
            pltpu.VMEM((tiles.shape[0] - remote,) + tiles.shape[1:], bf16),
            pltpu.VMEM((hub_rows, width), bf16),
            pltpu.VMEM((hub_count + 1, block_size, width), f32),
            pltpu.SemaphoreType.DMA((5,)),
        ],
        (plan, count, position, place_col) + tuple(halves) + (own, tiles),
    )


def hub_second_kernel(
    digits, plan, count, position, place_row, half0, half1, own_hbm, tiles_hbm,
    hubs, mine, kept, sent, own, tiles, total, placed, sems,
):
    hub_count, block_size, width = hubs.shape
    hub_rows = hub_count * block_size
    local = mine.shape[0]
    remote = tiles_hbm.shape[0] - tiles.shape[0]
    loads = tile_loads(tiles_hbm, tiles, sems)
    load = pltpu.make_async_copy(own_hbm, own, sems.at[4])
    load.start()
    for_live(count, loads, start)
    me = position[0]
    flat = hubs.reshape(hub_rows, width)
    place_shards(me, (half0, half1), flat, digits, local)
    total[...] = jnp.zeros_like(total)

    def unit_rows(start, step):
        down = lax.broadcasted_iota(jnp.int32, (step, hub_rows), 0) + start
        return jnp.where(place_row[...] == down, 1.0, 0.0).astype(bf16)

    mine[...] = dot(unit_rows(me * local, local), flat[...]).astype(bf16)
    load.wait()
    for_live(count, loads, wait)
    add_products(plan, 0, plan[COUNTS, N_HUB], remote, tiles, hubs, own, total, 0, hub_count)
    sums = total[:hub_count].reshape(hub_rows, width)
    high = sums.astype(bf16)
    low = (sums - high.astype(f32)).astype(bf16)
    step = 2 * block_size

    def rows_step(number, unused):
        start = number * step
        unit = unit_rows(start, step)
        placed[pl.ds(pl.multiple_of(start, step), step), :] = dot(unit, high) + dot(unit, low)
        return unused

    lax.fori_loop(0, hub_rows // step, rows_step, 0)
    split_sums(me, placed[...], local, kept, sent)


def hub_second(digits, plan, count, position, place_row, halves, own, tiles, local, remote):
    block_size, width = own.shape[1:]
    hub_rows = place_row.shape[1]
    hub_count = hub_rows // block_size
    return call(
        functools.partial(hub_second_kernel, digits),
        "hub_second",
        48,
        2 * hub_rows * hub_rows * width,
        14 * MIB,
        (
            shape_of((hub_count, block_size, width), bf16),
            shape_of((local, width), bf16),
            shape_of((hub_rows // 2, width), f32),
            shape_of((hub_rows // 2, width), f32),
        ),
        [SMEM] * 3 + [VMEM] * 3 + [ANY] * 2,
        (VMEM,) * 4,
        [
            pltpu.VMEM(own.shape, bf16),
            pltpu.VMEM((tiles.shape[0] - remote,) + tiles.shape[1:], bf16),
            pltpu.VMEM((hub_count + 1, block_size, width), f32),
            pltpu.VMEM((hub_rows, width), f32),
            pltpu.SemaphoreType.DMA((5,)),
        ],
        (plan, count, position, place_row) + tuple(halves) + (own, tiles),
    )


def combine(position, kept, received, bit, radix, local, sent_type):
    rows = kept.shape[0] // radix
    width = kept.shape[1]

    def kernel(position, kept_in, *refs):
        received, outs = refs[: -radix], refs[-radix:]
        total = kept_in[...].astype(f32)
        for part in received:
            total = total + part[...].astype(f32)
        digit = (position[0] // bit) % radix
        parts = total.reshape(rows // local, radix, local, width)
        for offset, out in enumerate(outs):
            value = parts[:, 0]
            for number in range(1, radix):
                value = jnp.where((digit ^ offset) == number, parts[:, number], value)
            out[...] = value.reshape(rows, width).astype(out.dtype)

    shapes = [shape_of((rows, width), f32)] + [shape_of((rows, width), sent_type)] * (radix - 1)
    return call(
        kernel,
        "combine",
        16,
        kept.size,
        12 * kept.size,
        tuple(shapes),
        [SMEM] + [VMEM] * (1 + len(received)),
        (VMEM,) * radix,
        [],
        (position, kept) + tuple(received),
    )


def load_weights(layer, first_in, second_in, first, second, sems):
    loads = [
        pltpu.make_async_copy(first_in.at[layer], first, sems.at[0]),
        pltpu.make_async_copy(second_in.at[layer], second, sems.at[1]),
    ]
    for load in loads:
        load.start()
    return loads


def hub_network_kernel(layer, rows_in, *refs):
    parts, (first_in, second_in, out, first, second, sems) = refs[:-6], refs[-6:]
    loads = load_weights(layer, first_in, second_in, first, second, sems)
    u = rows_in[...].astype(f32)
    for part in parts:
        u = u + part[...].astype(f32)
    for load in loads:
        load.wait()
    out[...] = network(u, first, second, first.shape[-1])


def hub_network(layer, rows_in, parts, first, second):
    return call(
        functools.partial(hub_network_kernel, layer),
        "hub_network",
        24,
        4 * rows_in.size * first.shape[-1],
        2 * first.size,
        shape_of(rows_in.shape, bf16),
        [VMEM] * (1 + len(parts)) + [ANY] * 2,
        VMEM,
        [
            pltpu.VMEM(first.shape[1:], bf16),
            pltpu.VMEM(second.shape[1:], bf16),
            pltpu.SemaphoreType.DMA((2,)),
        ],
        (rows_in,) + tuple(parts) + (first, second),
    )


def before_kernel(
    layer, plan, count, hubs_in, own_in, tiles_in, first_in, second_in, base, out,
    hubs, own, tiles, first, second, u, result, tile_sems, block_sems, sem,
):
    own_count = own.shape[0]
    hub_count = hubs.shape[0]
    remote = tiles_in.shape[0] - tiles.shape[0]
    load_own = pltpu.make_async_copy(own_in, own, sem.at[0])
    load_hubs = pltpu.make_async_copy(hubs_in, hubs, sem.at[1])
    loads = tile_loads(tiles_in, tiles, tile_sems)
    load_own.start()
    load_hubs.start()
    for_live(count, loads, start)
    load_own.wait()
    u[:own_count] = own[...].astype(f32)
    load_hubs.wait()
    for_live(count, loads, wait)
    weights = load_weights(layer, first_in, second_in, first, second, sem.at[pl.ds(2, 2)])
    n_fed = plan[COUNTS, N_FED]
    add_products(
        plan, plan[COUNTS, N_HUB], plan[COUNTS, N_OWN], remote, tiles, hubs, own, u, hub_count, own_count
    )

    def save(place):
        return pltpu.make_async_copy(u.at[plan[BLOCK, place]], base.at[place], block_sems.at[place])

    def finish(place):
        block = plan[BLOCK, place]
        return pltpu.make_async_copy(result.at[place], out.at[block], block_sems.at[place])

    each_block(0, n_fed, save, start)
    for load in weights:
        load.wait()

    def step(group, many):
        first_place, number = group * GROUP, many * GROUP
        places = [first_place + lane for lane in range(number)]
        values = jnp.concatenate([u[plan[BLOCK, place]] for place in places], axis=0)
        values = network(values, first, second, 512)
        result[pl.ds(first_place, number)] = values.reshape((number,) + result.shape[1:])
        finish_group(first_place, number, n_fed, own_count, finish)

    run_groups(n_fed // GROUP, own_count // GROUP, step)
    each_block(0, n_fed, save, wait)
    each_block(n_fed, own_count, finish, wait)


def before(layer, plan, count, hubs, own, tiles, first, second, remote):
    own_count, block_size, width = own.shape
    return call(
        functools.partial(before_kernel, layer),
        "before",
        58,
        4 * own.size * first.shape[-1] // 3,
        18 * MIB,
        (shape_of(own.shape, f32), shape_of(own.shape, bf16)),
        [SMEM] * 2 + [ANY] * 5,
        (ANY, ANY),
        [
            pltpu.VMEM(hubs.shape, bf16),
            pltpu.VMEM(own.shape, bf16),
            pltpu.VMEM((tiles.shape[0] - remote,) + tiles.shape[1:], bf16),
            pltpu.VMEM(first.shape[1:], bf16),
            pltpu.VMEM(second.shape[1:], bf16),
            pltpu.VMEM((own_count + 1, block_size, width), f32),
            pltpu.VMEM(own.shape, bf16),
            pltpu.SemaphoreType.DMA((4,)),
            pltpu.SemaphoreType.DMA((own_count,)),
            pltpu.SemaphoreType.DMA((4,)),
        ],
        (plan, count, hubs, own, tiles, first, second),
    )


def after_kernel(
    layer, with_send, plan, base, done, incoming, tiles, first_in, second_in, *refs
):
    out, refs = refs[0], refs[1:]
    if with_send:
        (sums, outgoing), refs = refs[:2], refs[2:]
    u, extra, inc, adj, first, second, result, base_sems, block_sems, sem = refs
    own_count = u.shape[0]
    remote = incoming.shape[0]
    parts = 4
    size = remote // parts
    loads = []
    for part in range(parts):
        cut = pl.ds(part * size, size)
        loads.append(
            (
                pltpu.make_async_copy(tiles.at[cut], adj.at[cut], sem.at[2 + 2 * part]),
                pltpu.make_async_copy(incoming.at[cut], inc.at[cut], sem.at[3 + 2 * part]),
            )
        )
        for load in loads[-1]:
            load.start()
    n_fed, n_held = plan[COUNTS, N_FED], plan[COUNTS, N_HELD]
    groups = rounded_up(n_fed)
    groups_now = rounded_up(plan[COUNTS, N_NOW]) if with_send else groups
    apart = jnp.minimum(groups * GROUP, n_held)
    early = jnp.minimum(groups, 2)

    def cut_of(group):
        return pl.ds(group * GROUP, GROUP)

    def load_base(group):
        cut = cut_of(group)
        return pltpu.make_async_copy(base.at[cut], u.at[cut], base_sems.at[group])

    def load_done(place):
        block = plan[BLOCK, place]
        return pltpu.make_async_copy(done.at[block], result.at[place], block_sems.at[place])

    def finish(place):
        block = plan[BLOCK, place]
        return pltpu.make_async_copy(result.at[place], out.at[block], block_sems.at[place])

    extra[...] = jnp.zeros_like(extra)
    for part in range(parts):
        for load in loads[part]:
            load.wait()
        if part == 0:
            weights = load_weights(layer, first_in, second_in, first, second, sem.at[pl.ds(0, 2)])
            each_block(0, early, load_base, start)
        if part == 2:
            each_block(early, groups, load_base, start)
            if with_send:
                each_block(apart, n_held, load_done, start)
        products = [dot(adj[slot], inc[slot]) for slot in range(part * size, (part + 1) * size)]
        for lane, product in enumerate(products):
            extra[plan[REMOTE, part * size + lane]] += product
    for load in weights:
        load.wait()
    n_now = jnp.minimum(groups_now * GROUP, n_fed)

    def step(group, many):
        for offset in range(many):
            load_base(group + offset).wait()
        cut = pl.ds(group * GROUP, many * GROUP)
        values = (u[cut] + extra[cut]).reshape(many * GROUP * u.shape[1], u.shape[2])
        values = network(values, first, second, 512)
        result[cut] = values.reshape((many * GROUP,) + result.shape[1:])
        finish_group(group * GROUP, many * GROUP, 0, n_now, finish)

    run_groups(0, groups_now, step)
    copies = []
    if with_send:
        each_block(n_fed, apart, load_done, start)
        each_block(n_fed, n_held, load_done, wait)
        for number in range(remote):
            copy = pltpu.make_async_copy(
                result.at[plan[GOING, number]], outgoing.at[number], sem.at[number]
            )
            copy.start()
            copies.append(copy)

        def save(group):
            cut = cut_of(group)
            return pltpu.make_async_copy(u.at[cut], sums.at[cut], base_sems.at[group])

        def keep(group, unused):
            load_base(group).wait()
            cut = cut_of(group)
            u[cut] += extra[cut]
            save(group).start()
            return unused

        lax.fori_loop(groups_now, groups, keep, 0)
        each_block(groups_now, groups, save, wait)
    each_block(0, n_now, finish, wait)
    for copy in copies:
        copy.wait()


def after(layer, plan, base, done, incoming, tiles, first, second, with_send):
    own_count = base.shape[0]
    remote = incoming.shape[0]
    shapes = [shape_of(base.shape, bf16)]
    if with_send:
        shapes += [shape_of(base.shape, f32), shape_of(incoming.shape, bf16)]
    return pl.pallas_call(
        functools.partial(after_kernel, layer, with_send),
        out_shape=tuple(shapes),
        in_specs=[SMEM] + [ANY] * 6,
        out_specs=(ANY,) * len(shapes),
        scratch_shapes=[
            pltpu.VMEM(base.shape, f32),
            pltpu.VMEM(base.shape, f32),
            pltpu.VMEM(incoming.shape, bf16),
            pltpu.VMEM((remote,) + tiles.shape[1:], bf16),
            pltpu.VMEM(first.shape[1:], bf16),
            pltpu.VMEM(second.shape[1:], bf16),
            pltpu.VMEM(base.shape, bf16),
            pltpu.SemaphoreType.DMA((own_count // GROUP,)),
            pltpu.SemaphoreType.DMA((own_count,)),
            pltpu.SemaphoreType.DMA((max(10, remote),)),
        ],
        input_output_aliases={2: 0, 1: 1} if with_send else {2: 0},
        compiler_params=pltpu.CompilerParams(vmem_limit_bytes=58 * MIB),
        cost_estimate=pl.CostEstimate(
            flops=4 * base.size * first.shape[-1], bytes_accessed=16 * MIB, transcendentals=0
        ),
        name="after",
    )(plan, base, done, incoming, tiles, first, second)


def late_kernel(
    layer, plan, sums, done, first_in, second_in, out, u, first, second, result, base_sems, block_sems, sem
):
    weights = load_weights(layer, first_in, second_in, first, second, sem)
    n_fed = plan[COUNTS, N_FED]
    groups = rounded_up(n_fed)
    groups_now = rounded_up(plan[COUNTS, N_NOW])

    def load(group):
        cut = pl.ds(group * GROUP, GROUP)
        return pltpu.make_async_copy(sums.at[cut], u.at[cut], base_sems.at[group])

    def finish(place):
        block = plan[BLOCK, place]
        return pltpu.make_async_copy(result.at[place], out.at[block], block_sems.at[place])

    each_block(groups_now, groups, load, start)
    for part in weights:
        part.wait()

    def step(group, many):
        for offset in range(many):
            load(group + offset).wait()
        cut = pl.ds(group * GROUP, many * GROUP)
        values = network(
            u[cut].reshape(many * GROUP * u.shape[1], u.shape[2]), first, second, 512
        )
        result[cut] = values.reshape((many * GROUP,) + result.shape[1:])
        finish_group(group * GROUP, many * GROUP, 0, n_fed, finish)

    run_groups(groups_now, groups, step)
    each_block(jnp.minimum(groups_now * GROUP, n_fed), n_fed, finish, wait)


def late(layer, plan, sums, done, first, second):
    own_count = sums.shape[0]
    return pl.pallas_call(
        functools.partial(late_kernel, layer),
        out_shape=shape_of(done.shape, bf16),
        in_specs=[SMEM] + [ANY] * 4,
        out_specs=ANY,
        scratch_shapes=[
            pltpu.VMEM(sums.shape, f32),
            pltpu.VMEM(first.shape[1:], bf16),
            pltpu.VMEM(second.shape[1:], bf16),
            pltpu.VMEM(sums.shape, bf16),
            pltpu.SemaphoreType.DMA((own_count // GROUP,)),
            pltpu.SemaphoreType.DMA((own_count,)),
            pltpu.SemaphoreType.DMA((2,)),
        ],
        input_output_aliases={2: 0},
        compiler_params=pltpu.CompilerParams(vmem_limit_bytes=58 * MIB),
        cost_estimate=pl.CostEstimate(
            flops=sums.size * first.shape[-1], bytes_accessed=5 * MIB, transcendentals=0
        ),
        name="late",
    )(plan, sums, done, first, second)


def exchange(x, bit):
    devices = lax.axis_size("dev")
    return lax.ppermute(x, "dev", [(i, i ^ bit) for i in range(devices)])


def all_digits():
    devices = lax.axis_size("dev")
    digits, bit = [(1, 2)], 2
    while bit < devices:
        radix = 4 if 4 * bit <= devices else 2
        digits.append((bit, radix))
        bit *= radix
    return digits


def gather_step(x, bit, radix):
    return [x] + [exchange(x, bit * offset) for offset in range(1, radix)]


def gather_far(x, digits):
    return gather_step(x, *digits[-1])


def gather_near(pieces, digits):
    for digit in digits[-2:0:-1]:
        pieces = gather_step(jnp.concatenate(pieces, axis=0), *digit)
    return pieces


def gather_last(pieces, digits):
    x = jnp.concatenate(pieces, axis=0)
    return x, exchange(x, digits[0][0])


def scatter_near(position, kept, sent, digits, local):
    received = [exchange(sent, digits[0][0])]
    for bit, radix in digits[1:-1]:
        kept, *sent = combine(position, kept, received, bit, radix, local, f32)
        received = [exchange(part, bit * (1 + number)) for number, part in enumerate(sent)]
    return kept, received


def scatter_far(position, kept, received, digits, local, sent_type):
    bit, radix = digits[-1]
    kept, *sent = combine(position, kept, received, bit, radix, local, sent_type)
    return [kept] + [exchange(part, bit * (1 + number)) for number, part in enumerate(sent)]


def body(
    peripheral, hubs, tiles, tile_rows, local_cols, tile_count, send_list, hub_place, w_in, w_out
):
    position = lax.axis_index("dev")
    digits = all_digits()
    block_size = tiles.shape[1]
    width = peripheral.shape[1]
    own_count = peripheral.shape[0] // block_size
    hub_rows = hub_place.shape[0]
    hub_count = hub_rows // block_size
    local = hubs.shape[0]
    remote = send_list.shape[1]
    place_col = hub_place.reshape(hub_rows, 1)
    place_row = hub_place.reshape(1, hub_rows)
    me = position.astype(jnp.int32).reshape(1)
    own = peripheral.reshape(own_count, block_size, width)
    all_to_all = functools.partial(
        lax.all_to_all, axis_name="dev", split_axis=0, concat_axis=0, tiled=True
    )

    pieces = gather_far(hubs, digits)
    plan = make_plan(me, tile_count, tile_rows, local_cols, send_list, hub_count, own_count)
    outgoing = pack(send_list, own)
    plan, outgoing, *pieces = lax.optimization_barrier((plan, outgoing, *pieces))
    pieces = gather_near(pieces, digits)
    outgoing, place_col, *pieces = lax.optimization_barrier((outgoing, place_col, *pieces))
    incoming = all_to_all(outgoing)
    halves = gather_last(pieces, digits)
    hub_table, mine, kept, sent = hub_first(
        digits, plan, tile_count, me, place_col, halves, own, tiles, local, remote
    )
    base, done = before(0, plan, tile_count, hub_table, own, tiles, w_in, w_out, remote)
    kept, received = scatter_near(me, kept, sent, digits, local)
    base, done, *received = lax.optimization_barrier((base, done, *received))
    parts = scatter_far(me, kept, received, digits, local, bf16)
    hub_new = hub_network(0, mine, parts, w_in, w_out)
    pieces = gather_far(hub_new, digits)
    base, *pieces = lax.optimization_barrier((base, *pieces))
    done, sums, outgoing = after(0, plan, base, done, incoming, tiles, w_in, w_out, True)

    pieces = gather_near(pieces, digits)
    outgoing, *pieces = lax.optimization_barrier((outgoing, *pieces))
    incoming = all_to_all(outgoing)
    own = late(0, plan, sums, done, w_in, w_out)
    halves = gather_last(pieces, digits)
    hub_table, mine, kept, sent = hub_second(
        digits, plan, tile_count, me, place_row, halves, own, tiles, local, remote
    )
    base, done = before(1, plan, tile_count, hub_table, own, tiles, w_in, w_out, remote)
    kept, received = scatter_near(me, kept, sent, digits, local)
    base, done, *received = lax.optimization_barrier((base, done, *received))
    parts = scatter_far(me, kept, received, digits, local, bf16)
    (peri_out,) = after(1, plan, base, done, incoming, tiles, w_in, w_out, False)
    peri_out, *parts = lax.optimization_barrier((peri_out, *parts))
    hub_out = hub_network(1, mine, parts, w_in, w_out)
    return (peri_out.reshape(peripheral.shape), hub_out)


def solution(mesh):
    in_specs = (
        P("dev", None),
        P("dev", None),
        P("dev", None, None),
        P("dev"),
        P("dev"),
        P("dev"),
        P("dev", None),
        P(),
        P(),
        P(),
    )
    out_specs = (P("dev", None), P("dev", None))
    return jax.shard_map(body, mesh=mesh, in_specs=in_specs, out_specs=out_specs, check_vma=False)
```

```python
import functools

import jax
import jax.numpy as jnp
from jax import lax
from jax.experimental import pallas as pl
from jax.experimental.pallas import tpu as pltpu
from jax.sharding import PartitionSpec as P

epsilon = 1e-06
f32 = jnp.float32
bf16 = jnp.bfloat16
MIB = 1024 * 1024
VMEM = pl.BlockSpec(memory_space=pltpu.VMEM)
SMEM = pl.BlockSpec(memory_space=pltpu.SMEM)
ANY = pl.BlockSpec(memory_space=pl.ANY)
GROUP = 4
SLOTS = 8


def dot(a, b):
    return jnp.dot(a, b, preferred_element_type=f32)


def shape_of(shape, dtype):
    return jax.ShapeDtypeStruct(tuple(shape), dtype)


def call(kernel, name, mib, flops, moved, out_shape, in_specs, out_specs, scratch, args):
    return pl.pallas_call(
        kernel,
        out_shape=out_shape,
        in_specs=in_specs,
        out_specs=out_specs,
        scratch_shapes=scratch,
        compiler_params=pltpu.CompilerParams(vmem_limit_bytes=mib * MIB),
        cost_estimate=pl.CostEstimate(flops=flops, bytes_accessed=moved, transcendentals=0),
        name=name,
    )(*args)


def normalise(u):
    return (u * lax.rsqrt(jnp.mean(u * u, axis=-1, keepdims=True) + epsilon)).astype(bf16)


def network(u, first, second, hidden_step):
    normed = normalise(u)
    total = u
    for start in range(0, first.shape[-1], hidden_step):
        cut = slice(start, start + hidden_step)
        hidden = jnp.maximum(dot(normed, first[:, cut]), 0.0).astype(bf16)
        total = total + dot(hidden, second[cut, :])
    return total.astype(bf16)


SLOT, ROW, COL, BLOCK, REMOTE, GOING, COUNTS = range(7)
N_HUB, N_OWN, N_NOW, N_FED, N_HELD = range(5)


def ranked(key, size):
    down = lax.broadcasted_iota(jnp.int32, (size, size), 0)
    along = lax.broadcasted_iota(jnp.int32, (size, size), 1)
    wide = jnp.broadcast_to(key, (size, size))
    tall = jnp.sum(jnp.where(down == along, wide, 0), axis=1, keepdims=True)
    ahead = (wide < tall) | ((wide == tall) & (along < down))
    return jnp.sum(ahead.astype(jnp.int32), axis=1, keepdims=True)


def plan_kernel(hub_count, own_count, remote, position, count, rows_in, cols_in, chosen, plan):
    capacity = rows_in.shape[1]
    shift = position[0] * own_count
    rows = jnp.where(rows_in[...] < hub_count, rows_in[...], rows_in[...] - shift)
    cols = jnp.where(cols_in[...] < hub_count, cols_in[...], cols_in[...] - shift)
    plan[...] = jnp.zeros_like(plan)
    slot = lax.broadcasted_iota(jnp.int32, (1, capacity), 1)
    picked = (slot >= remote) & (slot < count[0])
    of_hub = picked & (rows < hub_count)
    of_own = picked & (rows >= hub_count)
    key = jnp.where(of_hub, 0, jnp.where(of_own, 1, 2))
    place = ranked(key, capacity)
    down = lax.broadcasted_iota(jnp.int32, (capacity, capacity), 0)
    along = lax.broadcasted_iota(jnp.int32, (capacity, capacity), 1)
    here = place == along

    def column(row):
        wide = jnp.broadcast_to(row, (capacity, capacity))
        return jnp.sum(jnp.where(down == along, wide, 0), axis=1, keepdims=True)

    def ordered(values):
        return jnp.sum(jnp.where(here, values, 0), axis=0, keepdims=True)

    plan[SLOT : SLOT + 1, :capacity] = ordered(down)
    plan[ROW : ROW + 1, :capacity] = ordered(column(rows))
    plan[COL : COL + 1, :capacity] = ordered(column(cols))

    block = lax.broadcasted_iota(jnp.int32, (own_count, remote), 0)
    target = rows[:, :remote] - hub_count
    fed = jnp.max((block == target).astype(jnp.int32), axis=1, keepdims=True)
    sent = jnp.max((block == chosen[...]).astype(jnp.int32), axis=1, keepdims=True)
    key = 3 - 2 * fed - sent
    down = lax.broadcasted_iota(jnp.int32, (own_count, own_count), 0)
    along = lax.broadcasted_iota(jnp.int32, (own_count, own_count), 1)
    row_key = jnp.sum(jnp.where(down == along, key, 0), axis=0, keepdims=True)
    place = ranked(row_key, own_count)
    plan[BLOCK : BLOCK + 1, :own_count] = jnp.sum(
        jnp.where(place == along, down, 0), axis=0, keepdims=True
    )
    plan[REMOTE : REMOTE + 1, :remote] = jnp.sum(
        jnp.where(block == target, place, 0), axis=0, keepdims=True
    )
    plan[GOING : GOING + 1, :remote] = jnp.sum(
        jnp.where(block == chosen[...], place, 0), axis=0, keepdims=True
    )
    numbers = [
        jnp.sum(of_hub.astype(jnp.int32), axis=1, keepdims=True),
        jnp.sum(of_own.astype(jnp.int32), axis=1, keepdims=True),
        jnp.sum((row_key < 1).astype(jnp.int32), axis=1, keepdims=True),
        jnp.sum((row_key < 2).astype(jnp.int32), axis=1, keepdims=True),
        jnp.sum((row_key < 3).astype(jnp.int32), axis=1, keepdims=True),
    ]
    lane = lax.broadcasted_iota(jnp.int32, (1, plan.shape[1]), 1)
    counts = jnp.zeros((1, plan.shape[1]), jnp.int32)
    for place, number in enumerate(numbers):
        counts = jnp.where(lane == place, number, counts)
    plan[COUNTS : COUNTS + 1, :] = counts


def make_plan(position, count, rows, cols, chosen, hub_count, own_count):
    capacity, remote = rows.shape[0], chosen.shape[1]
    wide = -(-max(capacity, own_count, remote) // 128) * 128
    cols = jnp.concatenate([jnp.zeros((remote,), jnp.int32), cols])
    return call(
        functools.partial(plan_kernel, hub_count, own_count, remote),
        "plan",
        24,
        10**6,
        10**4,
        shape_of((8, wide), jnp.int32),
        [SMEM, SMEM, VMEM, VMEM, VMEM],
        VMEM,
        [],
        (position, count, rows.reshape(1, capacity), cols.reshape(1, capacity), chosen),
    )


def tile_loads(source, tiles, sems):
    remote = source.shape[0] - tiles.shape[0]
    size = tiles.shape[0] // 4
    loads = []
    for part in range(4):
        cut = pl.ds(remote + part * size, size)
        copy = pltpu.make_async_copy(source.at[cut], tiles.at[pl.ds(part * size, size)], sems.at[part])
        loads.append((remote + part * size, copy))
    return loads


def for_live(count, loads, act):
    for first_slot, load in loads:

        @pl.when(count[0] > first_slot)
        def _(load=load):
            act(load)


def add_products(plan, begin, found, remote, tiles, hubs, own, total, shift, spare):
    hub_count = hubs.shape[0]

    def step(number, unused):
        where, products = [], []
        for lane in range(SLOTS):
            place = number * SLOTS + lane
            live = place < found
            place = begin + jnp.minimum(place, found - 1)
            where.append(jnp.where(live, plan[ROW, place] - shift, spare))
            col = plan[COL, place]
            of_hub = hubs[jnp.minimum(col, hub_count - 1)]
            of_own = own[jnp.maximum(col - hub_count, 0)]
            tile = tiles[plan[SLOT, place] - remote]
            products.append(dot(tile, jnp.where(col < hub_count, of_hub, of_own)))
        for row, product in zip(where, products):
            total[row] += product
        return unused

    lax.fori_loop(0, (found + SLOTS - 1) // SLOTS, step, 0)


def each_block(first_place, last_place, copy_of, act):
    def step(place, unused):
        act(copy_of(place))
        return unused

    lax.fori_loop(first_place, last_place, step, 0)


def start(copy):
    copy.start()


def wait(copy):
    copy.wait()


def run_groups(begin, end, step):
    def pair(number, unused):
        step(begin + 2 * number, 2)
        return unused

    lax.fori_loop(0, (end - begin) // 2, pair, 0)

    @pl.when((end - begin) % 2 == 1)
    def _():
        step(end - 1, 1)


def rounded_up(number):
    return (number + GROUP - 1) // GROUP


def finish_group(first_place, number, begin, end, finish):
    for lane in range(number):
        place = first_place + lane

        @pl.when((place >= begin) & (place < end))
        def _(place=place):
            finish(place).start()


def pack_kernel(chosen, blocks, outgoing, held, sems):
    load = pltpu.make_async_copy(blocks, held, sems.at[0])
    load.start()
    load.wait()
    copies = []
    for number in range(outgoing.shape[0]):
        copy = pltpu.make_async_copy(
            held.at[chosen[0, number]], outgoing.at[number], sems.at[number]
        )
        copy.start()
        copies.append(copy)
    for copy in copies:
        copy.wait()


def pack(chosen, blocks):
    devices = chosen.shape[1]
    return call(
        pack_kernel,
        "pack",
        58,
        0,
        2 * blocks.size * 2,
        shape_of((devices,) + blocks.shape[1:], bf16),
        [SMEM, ANY],
        ANY,
        [pltpu.VMEM(blocks.shape, bf16), pltpu.SemaphoreType.DMA((devices,))],
        (chosen, blocks),
    )


def slot_place(slot, digits):
    place, weight = 0, 1
    for bit, radix in digits[:0:-1]:
        place += weight * ((slot // bit) % radix)
        weight *= radix
    return slot % 2, place


def place_shards(me, halves, table, digits, local, in_order):
    bit = digits[-1][0]
    for slot in range(table.shape[0] // local):
        half, place = slot_place(slot, digits)
        device = slot // bit * bit + (lax.rem(me, bit) ^ (slot % bit)) if in_order else me ^ slot
        first_row = pl.multiple_of(device * local, local)
        table[pl.ds(first_row, local), :] = halves[half][place * local : (place + 1) * local, :]


def split_sums(me, sums, local, kept, sent):
    odd = me % 2
    width = sums.shape[-1]
    pairs = sums.reshape(-1, 2, local, width)
    kept[...] = jnp.where(odd == 1, pairs[:, 1], pairs[:, 0]).reshape(kept.shape).astype(kept.dtype)
    sent[...] = jnp.where(odd == 1, pairs[:, 0], pairs[:, 1]).reshape(sent.shape).astype(sent.dtype)


def hub_first_kernel(
    digits, plan, count, position, place_col, half0, half1, own_hbm, tiles_hbm,
    hubs, mine, kept, sent, own, tiles, table, total, sems,
):
    hub_count, block_size, width = hubs.shape
    hub_rows = hub_count * block_size
    local = mine.shape[0] // digits[-1][1]
    remote = tiles_hbm.shape[0] - tiles.shape[0]
    loads = tile_loads(tiles_hbm, tiles, sems)
    load = pltpu.make_async_copy(own_hbm, own, sems.at[4])
    load.start()
    for_live(count, loads, start)
    me = position[0]
    place_shards(me, (half0, half1), table, digits, local, False)
    total[...] = jnp.zeros_like(total)
    step = 2 * block_size

    def rows_step(number, unused):
        cut = pl.ds(pl.multiple_of(number * step, step), step)
        lanes = lax.broadcasted_iota(jnp.int32, (step, hub_rows), 1)
        unit = jnp.where(place_col[cut, :] == lanes, 1.0, 0.0).astype(bf16)
        placed = dot(unit, table[...]).astype(bf16)
        hubs[pl.ds(number * 2, 2)] = placed.reshape(2, block_size, width)
        return unused

    lax.fori_loop(0, hub_rows // step, rows_step, 0)
    load.wait()
    for_live(count, loads, wait)
    add_products(plan, 0, plan[COUNTS, N_HUB], remote, tiles, hubs, own, total, 0, hub_count)
    split_sums(me, total[:hub_count], local, kept, sent)
    flat = hubs.reshape(hub_rows, width)
    bit, radix = digits[-1]
    for digit in range(radix):
        first_row = pl.multiple_of((digit * bit + lax.rem(me, bit)) * local, local)
        mine[digit * local : (digit + 1) * local, :] = flat[pl.ds(first_row, local), :]


def hub_first(digits, plan, count, position, place_col, halves, own, tiles, local, remote):
    block_size, width = own.shape[1:]
    hub_rows = place_col.shape[0]
    hub_count = hub_rows // block_size
    half = shape_of((hub_rows // 2, width), f32)
    return call(
        functools.partial(hub_first_kernel, digits),
        "hub_first",
        48,
        2 * hub_rows * hub_rows * width,
        14 * MIB,
        (
            shape_of((hub_count, block_size, width), bf16),
            shape_of((digits[-1][1] * local, width), bf16),
            half,
            half,
        ),
        [SMEM] * 3 + [VMEM] * 3 + [ANY] * 2,
        (VMEM,) * 4,
        [
            pltpu.VMEM(own.shape, bf16),
            pltpu.VMEM((tiles.shape[0] - remote,) + tiles.shape[1:], bf16),
            pltpu.VMEM((hub_rows, width), bf16),
            pltpu.VMEM((hub_count + 1, block_size, width), f32),
            pltpu.SemaphoreType.DMA((5,)),
        ],
        (plan, count, position, place_col) + tuple(halves) + (own, tiles),
    )


def hub_second_kernel(
    digits, plan, count, position, place_row, half0, half1, own_hbm, tiles_hbm,
    hubs, mine, kept, sent, own, tiles, total, placed, sems,
):
    hub_count, block_size, width = hubs.shape
    hub_rows = hub_count * block_size
    local = mine.shape[0]
    remote = tiles_hbm.shape[0] - tiles.shape[0]
    loads = tile_loads(tiles_hbm, tiles, sems)
    load = pltpu.make_async_copy(own_hbm, own, sems.at[4])
    load.start()
    for_live(count, loads, start)
    me = position[0]
    flat = hubs.reshape(hub_rows, width)
    place_shards(me, (half0, half1), flat, digits, local, True)
    total[...] = jnp.zeros_like(total)

    def unit_rows(start, step):
        down = lax.broadcasted_iota(jnp.int32, (step, hub_rows), 0) + start
        return jnp.where(place_row[...] == down, 1.0, 0.0).astype(bf16)

    mine[...] = dot(unit_rows(me * local, local), flat[...]).astype(bf16)
    load.wait()
    for_live(count, loads, wait)
    add_products(plan, 0, plan[COUNTS, N_HUB], remote, tiles, hubs, own, total, 0, hub_count)
    sums = total[:hub_count].reshape(hub_rows, width)
    high = sums.astype(bf16)
    low = (sums - high.astype(f32)).astype(bf16)
    step = 2 * block_size

    def rows_step(number, unused):
        start = number * step
        unit = unit_rows(start, step)
        placed[pl.ds(pl.multiple_of(start, step), step), :] = dot(unit, high) + dot(unit, low)
        return unused

    lax.fori_loop(0, hub_rows // step, rows_step, 0)
    split_sums(me, placed[...], local, kept, sent)


def hub_second(digits, plan, count, position, place_row, halves, own, tiles, local, remote):
    block_size, width = own.shape[1:]
    hub_rows = place_row.shape[1]
    hub_count = hub_rows // block_size
    return call(
        functools.partial(hub_second_kernel, digits),
        "hub_second",
        48,
        2 * hub_rows * hub_rows * width,
        14 * MIB,
        (
            shape_of((hub_count, block_size, width), bf16),
            shape_of((local, width), bf16),
            shape_of((hub_rows // 2, width), f32),
            shape_of((hub_rows // 2, width), f32),
        ),
        [SMEM] * 3 + [VMEM] * 3 + [ANY] * 2,
        (VMEM,) * 4,
        [
            pltpu.VMEM(own.shape, bf16),
            pltpu.VMEM((tiles.shape[0] - remote,) + tiles.shape[1:], bf16),
            pltpu.VMEM((hub_count + 1, block_size, width), f32),
            pltpu.VMEM((hub_rows, width), f32),
            pltpu.SemaphoreType.DMA((5,)),
        ],
        (plan, count, position, place_row) + tuple(halves) + (own, tiles),
    )


def combine(position, kept, received, bit, radix, local, sent_type):
    rows = kept.shape[0] // radix
    width = kept.shape[1]

    def kernel(position, kept_in, *refs):
        received, outs = refs[: -radix], refs[-radix:]
        total = kept_in[...].astype(f32)
        for part in received:
            total = total + part[...].astype(f32)
        digit = (position[0] // bit) % radix
        parts = total.reshape(rows // local, radix, local, width)
        for offset, out in enumerate(outs):
            value = parts[:, 0]
            for number in range(1, radix):
                value = jnp.where((digit ^ offset) == number, parts[:, number], value)
            out[...] = value.reshape(rows, width).astype(out.dtype)

    shapes = [shape_of((rows, width), f32)] + [shape_of((rows, width), sent_type)] * (radix - 1)
    return call(
        kernel,
        "combine",
        16,
        kept.size,
        12 * kept.size,
        tuple(shapes),
        [SMEM] + [VMEM] * (1 + len(received)),
        (VMEM,) * radix,
        [],
        (position, kept) + tuple(received),
    )


def total_kernel(*refs):
    total = refs[0][...].astype(f32)
    for part in refs[1:-1]:
        total = total + part[...].astype(f32)
    refs[-1][...] = total.astype(bf16)


def total(parts):
    return call(
        total_kernel,
        "total",
        16,
        parts[0].size,
        8 * parts[0].size,
        shape_of(parts[0].shape, bf16),
        [VMEM] * len(parts),
        VMEM,
        [],
        tuple(parts),
    )


def load_weights(layer, first_in, second_in, first, second, sems):
    loads = [
        pltpu.make_async_copy(first_in.at[layer], first, sems.at[0]),
        pltpu.make_async_copy(second_in.at[layer], second, sems.at[1]),
    ]
    for load in loads:
        load.start()
    return loads


def hub_network_kernel(layer, rows_in, *refs):
    parts, (first_in, second_in, out, first, second, sems) = refs[:-6], refs[-6:]
    loads = load_weights(layer, first_in, second_in, first, second, sems)
    u = rows_in[...].astype(f32)
    for part in parts:
        u = u + part[...].astype(f32)
    for load in loads:
        load.wait()
    out[...] = network(u, first, second, 512)


def hub_network(layer, rows_in, parts, first, second):
    return call(
        functools.partial(hub_network_kernel, layer),
        "hub_network",
        24,
        4 * rows_in.size * first.shape[-1],
        2 * first.size,
        shape_of(rows_in.shape, bf16),
        [VMEM] * (1 + len(parts)) + [ANY] * 2,
        VMEM,
        [
            pltpu.VMEM(first.shape[1:], bf16),
            pltpu.VMEM(second.shape[1:], bf16),
            pltpu.SemaphoreType.DMA((2,)),
        ],
        (rows_in,) + tuple(parts) + (first, second),
    )


def before_kernel(
    layer, plan, count, hubs_in, own_in, tiles_in, first_in, second_in, base, out,
    hubs, own, tiles, first, second, u, result, tile_sems, block_sems, sem,
):
    own_count = own.shape[0]
    hub_count = hubs.shape[0]
    remote = tiles_in.shape[0] - tiles.shape[0]
    load_own = pltpu.make_async_copy(own_in, own, sem.at[0])
    load_hubs = pltpu.make_async_copy(hubs_in, hubs, sem.at[1])
    loads = tile_loads(tiles_in, tiles, tile_sems)
    load_own.start()
    load_hubs.start()
    for_live(count, loads, start)
    load_own.wait()
    u[:own_count] = own[...].astype(f32)
    load_hubs.wait()
    for_live(count, loads, wait)
    weights = load_weights(layer, first_in, second_in, first, second, sem.at[pl.ds(2, 2)])
    n_fed = plan[COUNTS, N_FED]
    add_products(
        plan, plan[COUNTS, N_HUB], plan[COUNTS, N_OWN], remote, tiles, hubs, own, u, hub_count, own_count
    )

    def save(place):
        return pltpu.make_async_copy(u.at[plan[BLOCK, place]], base.at[place], block_sems.at[place])

    def finish(place):
        block = plan[BLOCK, place]
        return pltpu.make_async_copy(result.at[place], out.at[block], block_sems.at[place])

    each_block(0, n_fed, save, start)
    for load in weights:
        load.wait()

    def step(group, many):
        first_place, number = group * GROUP, many * GROUP
        places = [first_place + lane for lane in range(number)]
        values = jnp.concatenate([u[plan[BLOCK, place]] for place in places], axis=0)
        values = network(values, first, second, 512)
        result[pl.ds(first_place, number)] = values.reshape((number,) + result.shape[1:])
        finish_group(first_place, number, n_fed, own_count, finish)

    run_groups(n_fed // GROUP, own_count // GROUP, step)
    each_block(0, n_fed, save, wait)
    each_block(n_fed, own_count, finish, wait)


def before(layer, plan, count, hubs, own, tiles, first, second, remote):
    own_count, block_size, width = own.shape
    return call(
        functools.partial(before_kernel, layer),
        "before",
        58,
        4 * own.size * first.shape[-1] // 3,
        18 * MIB,
        (shape_of(own.shape, f32), shape_of(own.shape, bf16)),
        [SMEM] * 2 + [ANY] * 5,
        (ANY, ANY),
        [
            pltpu.VMEM(hubs.shape, bf16),
            pltpu.VMEM(own.shape, bf16),
            pltpu.VMEM((tiles.shape[0] - remote,) + tiles.shape[1:], bf16),
            pltpu.VMEM(first.shape[1:], bf16),
            pltpu.VMEM(second.shape[1:], bf16),
            pltpu.VMEM((own_count + 1, block_size, width), f32),
            pltpu.VMEM(own.shape, bf16),
            pltpu.SemaphoreType.DMA((4,)),
            pltpu.SemaphoreType.DMA((own_count,)),
            pltpu.SemaphoreType.DMA((4,)),
        ],
        (plan, count, hubs, own, tiles, first, second),
    )


def after_kernel(
    layer, with_send, plan, base, done, incoming, tiles, first_in, second_in, *refs
):
    out, refs = refs[0], refs[1:]
    if with_send:
        (sums, outgoing), refs = refs[:2], refs[2:]
    u, extra, inc, adj, first, second, result, base_sems, block_sems, sem = refs
    own_count = u.shape[0]
    remote = incoming.shape[0]
    parts = 4
    size = remote // parts
    loads = []
    for part in range(parts):
        cut = pl.ds(part * size, size)
        loads.append(
            (
                pltpu.make_async_copy(tiles.at[cut], adj.at[cut], sem.at[2 + 2 * part]),
                pltpu.make_async_copy(incoming.at[cut], inc.at[cut], sem.at[3 + 2 * part]),
            )
        )
        for load in loads[-1]:
            load.start()
    n_fed, n_held = plan[COUNTS, N_FED], plan[COUNTS, N_HELD]
    groups = rounded_up(n_fed)
    groups_now = rounded_up(plan[COUNTS, N_NOW]) if with_send else groups
    apart = jnp.minimum(groups * GROUP, n_held)
    early = jnp.minimum(groups, 2)

    def cut_of(group):
        return pl.ds(group * GROUP, GROUP)

    def load_base(group):
        cut = cut_of(group)
        return pltpu.make_async_copy(base.at[cut], u.at[cut], base_sems.at[group])

    def load_done(place):
        block = plan[BLOCK, place]
        return pltpu.make_async_copy(done.at[block], result.at[place], block_sems.at[place])

    def finish(place):
        block = plan[BLOCK, place]
        return pltpu.make_async_copy(result.at[place], out.at[block], block_sems.at[place])

    extra[...] = jnp.zeros_like(extra)
    for part in range(parts):
        for load in loads[part]:
            load.wait()
        if part == 0:
            weights = load_weights(layer, first_in, second_in, first, second, sem.at[pl.ds(0, 2)])
            each_block(0, early, load_base, start)
        if part == 2:
            each_block(early, groups, load_base, start)
            if with_send:
                each_block(apart, n_held, load_done, start)
        products = [dot(adj[slot], inc[slot]) for slot in range(part * size, (part + 1) * size)]
        for lane, product in enumerate(products):
            extra[plan[REMOTE, part * size + lane]] += product
    for load in weights:
        load.wait()
    n_now = jnp.minimum(groups_now * GROUP, n_fed)

    def step(group, many):
        for offset in range(many):
            load_base(group + offset).wait()
        cut = pl.ds(group * GROUP, many * GROUP)
        values = (u[cut] + extra[cut]).reshape(many * GROUP * u.shape[1], u.shape[2])
        values = network(values, first, second, 512)
        result[cut] = values.reshape((many * GROUP,) + result.shape[1:])
        finish_group(group * GROUP, many * GROUP, 0, n_now, finish)

    run_groups(0, groups_now, step)
    copies = []
    if with_send:
        each_block(n_fed, apart, load_done, start)
        each_block(n_fed, n_held, load_done, wait)
        for number in range(remote):
            copy = pltpu.make_async_copy(
                result.at[plan[GOING, number]], outgoing.at[number], sem.at[number]
            )
            copy.start()
            copies.append(copy)

        def save(group):
            cut = cut_of(group)
            return pltpu.make_async_copy(u.at[cut], sums.at[cut], base_sems.at[group])

        def keep(group, unused):
            load_base(group).wait()
            cut = cut_of(group)
            u[cut] += extra[cut]
            save(group).start()
            return unused

        lax.fori_loop(groups_now, groups, keep, 0)
        each_block(groups_now, groups, save, wait)
    each_block(0, n_now, finish, wait)
    for copy in copies:
        copy.wait()


def after(layer, plan, base, done, incoming, tiles, first, second, with_send):
    own_count = base.shape[0]
    remote = incoming.shape[0]
    shapes = [shape_of(base.shape, bf16)]
    if with_send:
        shapes += [shape_of(base.shape, f32), shape_of(incoming.shape, bf16)]
    return pl.pallas_call(
        functools.partial(after_kernel, layer, with_send),
        out_shape=tuple(shapes),
        in_specs=[SMEM] + [ANY] * 6,
        out_specs=(ANY,) * len(shapes),
        scratch_shapes=[
            pltpu.VMEM(base.shape, f32),
            pltpu.VMEM(base.shape, f32),
            pltpu.VMEM(incoming.shape, bf16),
            pltpu.VMEM((remote,) + tiles.shape[1:], bf16),
            pltpu.VMEM(first.shape[1:], bf16),
            pltpu.VMEM(second.shape[1:], bf16),
            pltpu.VMEM(base.shape, bf16),
            pltpu.SemaphoreType.DMA((own_count // GROUP,)),
            pltpu.SemaphoreType.DMA((own_count,)),
            pltpu.SemaphoreType.DMA((max(10, remote),)),
        ],
        input_output_aliases={2: 0, 1: 1} if with_send else {2: 0},
        compiler_params=pltpu.CompilerParams(vmem_limit_bytes=58 * MIB),
        cost_estimate=pl.CostEstimate(
            flops=4 * base.size * first.shape[-1], bytes_accessed=16 * MIB, transcendentals=0
        ),
        name="after",
    )(plan, base, done, incoming, tiles, first, second)


def late_kernel(
    layer, plan, sums, done, first_in, second_in, out, u, first, second, result, base_sems, block_sems, sem
):
    weights = load_weights(layer, first_in, second_in, first, second, sem)
    n_fed = plan[COUNTS, N_FED]
    groups = rounded_up(n_fed)
    groups_now = rounded_up(plan[COUNTS, N_NOW])

    def load(group):
        cut = pl.ds(group * GROUP, GROUP)
        return pltpu.make_async_copy(sums.at[cut], u.at[cut], base_sems.at[group])

    def finish(place):
        block = plan[BLOCK, place]
        return pltpu.make_async_copy(result.at[place], out.at[block], block_sems.at[place])

    each_block(groups_now, groups, load, start)
    for part in weights:
        part.wait()

    def step(group, many):
        for offset in range(many):
            load(group + offset).wait()
        cut = pl.ds(group * GROUP, many * GROUP)
        values = network(
            u[cut].reshape(many * GROUP * u.shape[1], u.shape[2]), first, second, 512
        )
        result[cut] = values.reshape((many * GROUP,) + result.shape[1:])
        finish_group(group * GROUP, many * GROUP, 0, n_fed, finish)

    run_groups(groups_now, groups, step)
    each_block(jnp.minimum(groups_now * GROUP, n_fed), n_fed, finish, wait)


def late(layer, plan, sums, done, first, second):
    own_count = sums.shape[0]
    return pl.pallas_call(
        functools.partial(late_kernel, layer),
        out_shape=shape_of(done.shape, bf16),
        in_specs=[SMEM] + [ANY] * 4,
        out_specs=ANY,
        scratch_shapes=[
            pltpu.VMEM(sums.shape, f32),
            pltpu.VMEM(first.shape[1:], bf16),
            pltpu.VMEM(second.shape[1:], bf16),
            pltpu.VMEM(sums.shape, bf16),
            pltpu.SemaphoreType.DMA((own_count // GROUP,)),
            pltpu.SemaphoreType.DMA((own_count,)),
            pltpu.SemaphoreType.DMA((2,)),
        ],
        input_output_aliases={2: 0},
        compiler_params=pltpu.CompilerParams(vmem_limit_bytes=58 * MIB),
        cost_estimate=pl.CostEstimate(
            flops=sums.size * first.shape[-1], bytes_accessed=5 * MIB, transcendentals=0
        ),
        name="late",
    )(plan, sums, done, first, second)


def exchange(x, bit):
    devices = lax.axis_size("dev")
    return lax.ppermute(x, "dev", [(i, i ^ bit) for i in range(devices)])


def all_digits():
    devices = lax.axis_size("dev")
    digits, bit = [(1, 2)], 2
    while bit < devices:
        radix = 4 if 4 * bit <= devices else 2
        digits.append((bit, radix))
        bit *= radix
    return digits


def gather_step(x, bit, radix):
    return [x] + [exchange(x, bit * offset) for offset in range(1, radix)]


def gather_far(x, digits):
    return gather_step(x, *digits[-1])


def gather_near(pieces, digits):
    for digit in digits[-2:0:-1]:
        pieces = gather_step(jnp.concatenate(pieces, axis=0), *digit)
    return pieces


def gather_last(pieces, digits):
    x = jnp.concatenate(pieces, axis=0)
    return x, exchange(x, digits[0][0])


def scatter_near(position, kept, sent, digits, local):
    received = [exchange(sent, digits[0][0])]
    for bit, radix in digits[1:-1]:
        kept, *sent = combine(position, kept, received, bit, radix, local, f32)
        received = [exchange(part, bit * (1 + number)) for number, part in enumerate(sent)]
    return kept, received


def scatter_far(position, kept, received, digits, local, sent_type):
    bit, radix = digits[-1]
    kept, *sent = combine(position, kept, received, bit, radix, local, sent_type)
    return [kept] + [exchange(part, bit * (1 + number)) for number, part in enumerate(sent)]


def share_far(kept, received, digits):
    bit, radix = digits[-1]
    parts = [kept] + received
    while radix > 1:
        mine = total(parts)
        parts = [mine, exchange(mine, bit)]
        bit, radix = 2 * bit, radix // 2
    return parts


def body(
    peripheral, hubs, tiles, tile_rows, local_cols, tile_count, send_list, hub_place, w_in, w_out
):
    position = lax.axis_index("dev")
    digits = all_digits()
    block_size = tiles.shape[1]
    width = peripheral.shape[1]
    own_count = peripheral.shape[0] // block_size
    hub_rows = hub_place.shape[0]
    hub_count = hub_rows // block_size
    local = hubs.shape[0]
    remote = send_list.shape[1]
    place_col = hub_place.reshape(hub_rows, 1)
    place_row = hub_place.reshape(1, hub_rows)
    me = position.astype(jnp.int32).reshape(1)
    own = peripheral.reshape(own_count, block_size, width)
    all_to_all = functools.partial(
        lax.all_to_all, axis_name="dev", split_axis=0, concat_axis=0, tiled=True
    )

    pieces = gather_far(hubs, digits)
    plan = make_plan(me, tile_count, tile_rows, local_cols, send_list, hub_count, own_count)
    outgoing = pack(send_list, own)
    plan, outgoing, *pieces = lax.optimization_barrier((plan, outgoing, *pieces))
    pieces = gather_near(pieces, digits)
    outgoing, place_col, *pieces = lax.optimization_barrier((outgoing, place_col, *pieces))
    incoming = all_to_all(outgoing)
    halves = gather_last(pieces, digits)
    hub_table, mine, kept, sent = hub_first(
        digits, plan, tile_count, me, place_col, halves, own, tiles, local, remote
    )
    base, done = before(0, plan, tile_count, hub_table, own, tiles, w_in, w_out, remote)
    kept, received = scatter_near(me, kept, sent, digits, local)
    base, done, *received = lax.optimization_barrier((base, done, *received))
    parts = share_far(kept, received, digits)
    hub_new = hub_network(0, mine, parts, w_in, w_out)
    base, hub_new = lax.optimization_barrier((base, hub_new))
    done, sums, outgoing = after(0, plan, base, done, incoming, tiles, w_in, w_out, True)

    pieces = gather_near([hub_new], digits)
    outgoing, *pieces = lax.optimization_barrier((outgoing, *pieces))
    incoming = all_to_all(outgoing)
    own = late(0, plan, sums, done, w_in, w_out)
    halves = gather_last(pieces, digits)
    hub_table, mine, kept, sent = hub_second(
        digits, plan, tile_count, me, place_row, halves, own, tiles, local, remote
    )
    base, done = before(1, plan, tile_count, hub_table, own, tiles, w_in, w_out, remote)
    kept, received = scatter_near(me, kept, sent, digits, local)
    base, done, *received = lax.optimization_barrier((base, done, *received))
    parts = scatter_far(me, kept, received, digits, local, bf16)
    (peri_out,) = after(1, plan, base, done, incoming, tiles, w_in, w_out, False)
    peri_out, *parts = lax.optimization_barrier((peri_out, *parts))
    hub_out = hub_network(1, mine, parts, w_in, w_out)
    return (peri_out.reshape(peripheral.shape), hub_out)


def solution(mesh):
    in_specs = (
        P("dev", None),
        P("dev", None),
        P("dev", None, None),
        P("dev"),
        P("dev"),
        P("dev"),
        P("dev", None),
        P(),
        P(),
        P(),
    )
    out_specs = (P("dev", None), P("dev", None))
    return jax.shard_map(body, mesh=mesh, in_specs=in_specs, out_specs=out_specs, check_vma=False)
```

```python
import functools

import jax
import jax.numpy as jnp
from jax import lax
from jax.experimental import pallas as pl
from jax.experimental.pallas import tpu as pltpu
from jax.sharding import PartitionSpec as P

epsilon = 1e-06
f32 = jnp.float32
bf16 = jnp.bfloat16
MIB = 1024 * 1024
VMEM = pl.BlockSpec(memory_space=pltpu.VMEM)
SMEM = pl.BlockSpec(memory_space=pltpu.SMEM)
ANY = pl.BlockSpec(memory_space=pl.ANY)
GROUP = 4
SLOTS = 8


def dot(a, b):
    return jnp.dot(a, b, preferred_element_type=f32)


def shape_of(shape, dtype):
    return jax.ShapeDtypeStruct(tuple(shape), dtype)


def call(kernel, name, mib, flops, moved, out_shape, in_specs, out_specs, scratch, args):
    return pl.pallas_call(
        kernel,
        out_shape=out_shape,
        in_specs=in_specs,
        out_specs=out_specs,
        scratch_shapes=scratch,
        compiler_params=pltpu.CompilerParams(vmem_limit_bytes=mib * MIB),
        cost_estimate=pl.CostEstimate(flops=flops, bytes_accessed=moved, transcendentals=0),
        name=name,
    )(*args)


def normalise(u):
    return (u * lax.rsqrt(jnp.mean(u * u, axis=-1, keepdims=True) + epsilon)).astype(bf16)


def network(u, first, second, hidden_step):
    normed = normalise(u)
    total = u
    for start in range(0, first.shape[-1], hidden_step):
        cut = slice(start, start + hidden_step)
        hidden = jnp.maximum(dot(normed, first[:, cut]), 0.0).astype(bf16)
        total = total + dot(hidden, second[cut, :])
    return total.astype(bf16)


SLOT, ROW, COL, BLOCK, REMOTE, GOING, COUNTS = range(7)
N_HUB, N_OWN, N_NOW, N_FED, N_HELD = range(5)


def ranked(key, size):
    down = lax.broadcasted_iota(jnp.int32, (size, size), 0)
    along = lax.broadcasted_iota(jnp.int32, (size, size), 1)
    wide = jnp.broadcast_to(key, (size, size))
    tall = jnp.sum(jnp.where(down == along, wide, 0), axis=1, keepdims=True)
    ahead = (wide < tall) | ((wide == tall) & (along < down))
    return jnp.sum(ahead.astype(jnp.int32), axis=1, keepdims=True)


def plan_kernel(hub_count, own_count, remote, position, count, rows_in, cols_in, chosen, plan):
    capacity = rows_in.shape[1]
    shift = position[0] * own_count
    rows = jnp.where(rows_in[...] < hub_count, rows_in[...], rows_in[...] - shift)
    cols = jnp.where(cols_in[...] < hub_count, cols_in[...], cols_in[...] - shift)
    plan[...] = jnp.zeros_like(plan)
    slot = lax.broadcasted_iota(jnp.int32, (1, capacity), 1)
    picked = (slot >= remote) & (slot < count[0])
    of_hub = picked & (rows < hub_count)
    of_own = picked & (rows >= hub_count)
    key = jnp.where(of_hub, 0, jnp.where(of_own, 1, 2))
    place = ranked(key, capacity)
    down = lax.broadcasted_iota(jnp.int32, (capacity, capacity), 0)
    along = lax.broadcasted_iota(jnp.int32, (capacity, capacity), 1)
    here = place == along

    def column(row):
        wide = jnp.broadcast_to(row, (capacity, capacity))
        return jnp.sum(jnp.where(down == along, wide, 0), axis=1, keepdims=True)

    def ordered(values):
        return jnp.sum(jnp.where(here, values, 0), axis=0, keepdims=True)

    plan[SLOT : SLOT + 1, :capacity] = ordered(down)
    plan[ROW : ROW + 1, :capacity] = ordered(column(rows))
    plan[COL : COL + 1, :capacity] = ordered(column(cols))

    block = lax.broadcasted_iota(jnp.int32, (own_count, remote), 0)
    target = rows[:, :remote] - hub_count
    fed = jnp.max((block == target).astype(jnp.int32), axis=1, keepdims=True)
    sent = jnp.max((block == chosen[...]).astype(jnp.int32), axis=1, keepdims=True)
    key = 3 - 2 * fed - sent
    down = lax.broadcasted_iota(jnp.int32, (own_count, own_count), 0)
    along = lax.broadcasted_iota(jnp.int32, (own_count, own_count), 1)
    row_key = jnp.sum(jnp.where(down == along, key, 0), axis=0, keepdims=True)
    place = ranked(row_key, own_count)
    plan[BLOCK : BLOCK + 1, :own_count] = jnp.sum(
        jnp.where(place == along, down, 0), axis=0, keepdims=True
    )
    plan[REMOTE : REMOTE + 1, :remote] = jnp.sum(
        jnp.where(block == target, place, 0), axis=0, keepdims=True
    )
    plan[GOING : GOING + 1, :remote] = jnp.sum(
        jnp.where(block == chosen[...], place, 0), axis=0, keepdims=True
    )
    numbers = [
        jnp.sum(of_hub.astype(jnp.int32), axis=1, keepdims=True),
        jnp.sum(of_own.astype(jnp.int32), axis=1, keepdims=True),
        jnp.sum((row_key < 1).astype(jnp.int32), axis=1, keepdims=True),
        jnp.sum((row_key < 2).astype(jnp.int32), axis=1, keepdims=True),
        jnp.sum((row_key < 3).astype(jnp.int32), axis=1, keepdims=True),
    ]
    lane = lax.broadcasted_iota(jnp.int32, (1, plan.shape[1]), 1)
    counts = jnp.zeros((1, plan.shape[1]), jnp.int32)
    for place, number in enumerate(numbers):
        counts = jnp.where(lane == place, number, counts)
    plan[COUNTS : COUNTS + 1, :] = counts


def make_plan(position, count, rows, cols, chosen, hub_count, own_count):
    capacity, remote = rows.shape[0], chosen.shape[1]
    wide = -(-max(capacity, own_count, remote) // 128) * 128
    cols = jnp.concatenate([jnp.zeros((remote,), jnp.int32), cols])
    return call(
        functools.partial(plan_kernel, hub_count, own_count, remote),
        "plan",
        24,
        10**6,
        10**4,
        shape_of((8, wide), jnp.int32),
        [SMEM, SMEM, VMEM, VMEM, VMEM],
        VMEM,
        [],
        (position, count, rows.reshape(1, capacity), cols.reshape(1, capacity), chosen),
    )


def tile_loads(source, tiles, sems):
    remote = source.shape[0] - tiles.shape[0]
    size = tiles.shape[0] // 4
    loads = []
    for part in range(4):
        cut = pl.ds(remote + part * size, size)
        copy = pltpu.make_async_copy(source.at[cut], tiles.at[pl.ds(part * size, size)], sems.at[part])
        loads.append((remote + part * size, copy))
    return loads


def for_live(count, loads, act):
    for first_slot, load in loads:

        @pl.when(count[0] > first_slot)
        def _(load=load):
            act(load)


def add_products(plan, begin, found, remote, tiles, hubs, own, total, shift, spare):
    hub_count = hubs.shape[0]

    def step(number, unused):
        where, products = [], []
        for lane in range(SLOTS):
            place = number * SLOTS + lane
            live = place < found
            place = begin + jnp.minimum(place, found - 1)
            where.append(jnp.where(live, plan[ROW, place] - shift, spare))
            col = plan[COL, place]
            of_hub = hubs[jnp.minimum(col, hub_count - 1)]
            of_own = own[jnp.maximum(col - hub_count, 0)]
            tile = tiles[plan[SLOT, place] - remote]
            products.append(dot(tile, jnp.where(col < hub_count, of_hub, of_own)))
        for row, product in zip(where, products):
            total[row] += product
        return unused

    lax.fori_loop(0, (found + SLOTS - 1) // SLOTS, step, 0)


def each_block(first_place, last_place, copy_of, act):
    def step(place, unused):
        act(copy_of(place))
        return unused

    lax.fori_loop(first_place, last_place, step, 0)


def start(copy):
    copy.start()


def wait(copy):
    copy.wait()


def run_groups(begin, end, step):
    def pair(number, unused):
        step(begin + 2 * number, 2)
        return unused

    lax.fori_loop(0, (end - begin) // 2, pair, 0)

    @pl.when((end - begin) % 2 == 1)
    def _():
        step(end - 1, 1)


def rounded_up(number):
    return (number + GROUP - 1) // GROUP


def finish_group(first_place, number, begin, end, finish):
    for lane in range(number):
        place = first_place + lane

        @pl.when((place >= begin) & (place < end))
        def _(place=place):
            finish(place).start()


def pack_kernel(chosen, blocks, outgoing, held, sems):
    loads, stores = [], []
    for number in range(outgoing.shape[0]):
        here = held.at[number]
        loads.append(pltpu.make_async_copy(blocks.at[chosen[0, number]], here, sems.at[number]))
        stores.append(pltpu.make_async_copy(here, outgoing.at[number], sems.at[number]))
        loads[-1].start()
    for load, store in zip(loads, stores):
        load.wait()
        store.start()
    for store in stores:
        store.wait()


def pack(chosen, blocks):
    devices = chosen.shape[1]
    return call(
        pack_kernel,
        "pack",
        58,
        0,
        2 * blocks.size * 2,
        shape_of((devices,) + blocks.shape[1:], bf16),
        [SMEM, ANY],
        ANY,
        [
            pltpu.VMEM((devices,) + blocks.shape[1:], bf16),
            pltpu.SemaphoreType.DMA((devices,)),
        ],
        (chosen, blocks),
    )


def slot_place(slot, digits):
    place, weight = 0, 1
    for bit, radix in digits[:0:-1]:
        place += weight * ((slot // bit) % radix)
        weight *= radix
    return slot % 2, place


def place_shards(me, halves, table, digits, local, in_order):
    bit = digits[-1][0]
    for slot in range(table.shape[0] // local):
        half, place = slot_place(slot, digits)
        device = slot // bit * bit + (lax.rem(me, bit) ^ (slot % bit)) if in_order else me ^ slot
        first_row = pl.multiple_of(device * local, local)
        table[pl.ds(first_row, local), :] = halves[half][place * local : (place + 1) * local, :]


def split_sums(me, sums, local, kept, sent):
    odd = me % 2
    width = sums.shape[-1]
    pairs = sums.reshape(-1, 2, local, width)
    kept[...] = jnp.where(odd == 1, pairs[:, 1], pairs[:, 0]).reshape(kept.shape).astype(kept.dtype)
    sent[...] = jnp.where(odd == 1, pairs[:, 0], pairs[:, 1]).reshape(sent.shape).astype(sent.dtype)


def hub_first_kernel(
    digits, plan, count, position, place_col, half0, half1, own_hbm, tiles_hbm,
    hubs, mine, kept, sent, own, tiles, table, total, sems,
):
    hub_count, block_size, width = hubs.shape
    hub_rows = hub_count * block_size
    local = mine.shape[0] // digits[-1][1]
    remote = tiles_hbm.shape[0] - tiles.shape[0]
    loads = tile_loads(tiles_hbm, tiles, sems)
    load = pltpu.make_async_copy(own_hbm, own, sems.at[4])
    load.start()
    for_live(count, loads, start)
    me = position[0]
    place_shards(me, (half0, half1), table, digits, local, False)
    total[...] = jnp.zeros_like(total)
    step = 2 * block_size

    def rows_step(number, unused):
        cut = pl.ds(pl.multiple_of(number * step, step), step)
        lanes = lax.broadcasted_iota(jnp.int32, (step, hub_rows), 1)
        unit = jnp.where(place_col[cut, :] == lanes, 1.0, 0.0).astype(bf16)
        placed = dot(unit, table[...]).astype(bf16)
        hubs[pl.ds(number * 2, 2)] = placed.reshape(2, block_size, width)
        return unused

    lax.fori_loop(0, hub_rows // step, rows_step, 0)
    load.wait()
    for_live(count, loads, wait)
    add_products(plan, 0, plan[COUNTS, N_HUB], remote, tiles, hubs, own, total, 0, hub_count)
    split_sums(me, total[:hub_count], local, kept, sent)
    flat = hubs.reshape(hub_rows, width)
    bit, radix = digits[-1]
    for digit in range(radix):
        first_row = pl.multiple_of((digit * bit + lax.rem(me, bit)) * local, local)
        mine[digit * local : (digit + 1) * local, :] = flat[pl.ds(first_row, local), :]


def hub_first(digits, plan, count, position, place_col, halves, own, tiles, local, remote):
    block_size, width = own.shape[1:]
    hub_rows = place_col.shape[0]
    hub_count = hub_rows // block_size
    half = shape_of((hub_rows // 2, width), f32)
    return call(
        functools.partial(hub_first_kernel, digits),
        "hub_first",
        48,
        2 * hub_rows * hub_rows * width,
        14 * MIB,
        (
            shape_of((hub_count, block_size, width), bf16),
            shape_of((digits[-1][1] * local, width), bf16),
            half,
            half,
        ),
        [SMEM] * 3 + [VMEM] * 3 + [ANY] * 2,
        (VMEM,) * 4,
        [
            pltpu.VMEM(own.shape, bf16),
            pltpu.VMEM((tiles.shape[0] - remote,) + tiles.shape[1:], bf16),
            pltpu.VMEM((hub_rows, width), bf16),
            pltpu.VMEM((hub_count + 1, block_size, width), f32),
            pltpu.SemaphoreType.DMA((5,)),
        ],
        (plan, count, position, place_col) + tuple(halves) + (own, tiles),
    )


def hub_second_kernel(
    digits, plan, count, position, place_row, half0, half1, own_hbm, tiles_hbm,
    hubs, mine, kept, sent, own, tiles, total, placed, sems,
):
    hub_count, block_size, width = hubs.shape
    hub_rows = hub_count * block_size
    local = mine.shape[0]
    remote = tiles_hbm.shape[0] - tiles.shape[0]
    loads = tile_loads(tiles_hbm, tiles, sems)
    load = pltpu.make_async_copy(own_hbm, own, sems.at[4])
    load.start()
    for_live(count, loads, start)
    me = position[0]
    flat = hubs.reshape(hub_rows, width)
    place_shards(me, (half0, half1), flat, digits, local, True)
    total[...] = jnp.zeros_like(total)

    def unit_rows(start, step):
        down = lax.broadcasted_iota(jnp.int32, (step, hub_rows), 0) + start
        return jnp.where(place_row[...] == down, 1.0, 0.0).astype(bf16)

    mine[...] = dot(unit_rows(me * local, local), flat[...]).astype(bf16)
    load.wait()
    for_live(count, loads, wait)
    add_products(plan, 0, plan[COUNTS, N_HUB], remote, tiles, hubs, own, total, 0, hub_count)
    sums = total[:hub_count].reshape(hub_rows, width)
    high = sums.astype(bf16)
    low = (sums - high.astype(f32)).astype(bf16)
    step = 2 * block_size

    def rows_step(number, unused):
        start = number * step
        unit = unit_rows(start, step)
        placed[pl.ds(pl.multiple_of(start, step), step), :] = dot(unit, high) + dot(unit, low)
        return unused

    lax.fori_loop(0, hub_rows // step, rows_step, 0)
    split_sums(me, placed[...], local, kept, sent)


def hub_second(digits, plan, count, position, place_row, halves, own, tiles, local, remote):
    block_size, width = own.shape[1:]
    hub_rows = place_row.shape[1]
    hub_count = hub_rows // block_size
    return call(
        functools.partial(hub_second_kernel, digits),
        "hub_second",
        48,
        2 * hub_rows * hub_rows * width,
        14 * MIB,
        (
            shape_of((hub_count, block_size, width), bf16),
            shape_of((local, width), bf16),
            shape_of((hub_rows // 2, width), f32),
            shape_of((hub_rows // 2, width), f32),
        ),
        [SMEM] * 3 + [VMEM] * 3 + [ANY] * 2,
        (VMEM,) * 4,
        [
            pltpu.VMEM(own.shape, bf16),
            pltpu.VMEM((tiles.shape[0] - remote,) + tiles.shape[1:], bf16),
            pltpu.VMEM((hub_count + 1, block_size, width), f32),
            pltpu.VMEM((hub_rows, width), f32),
            pltpu.SemaphoreType.DMA((5,)),
        ],
        (plan, count, position, place_row) + tuple(halves) + (own, tiles),
    )


def combine(position, kept, received, bit, radix, local, sent_type):
    rows = kept.shape[0] // radix
    width = kept.shape[1]

    def kernel(position, kept_in, *refs):
        received, outs = refs[: -radix], refs[-radix:]
        total = kept_in[...].astype(f32)
        for part in received:
            total = total + part[...].astype(f32)
        digit = (position[0] // bit) % radix
        parts = total.reshape(rows // local, radix, local, width)
        for offset, out in enumerate(outs):
            value = parts[:, 0]
            for number in range(1, radix):
                value = jnp.where((digit ^ offset) == number, parts[:, number], value)
            out[...] = value.reshape(rows, width).astype(out.dtype)

    shapes = [shape_of((rows, width), f32)] + [shape_of((rows, width), sent_type)] * (radix - 1)
    return call(
        kernel,
        "combine",
        16,
        kept.size,
        12 * kept.size,
        tuple(shapes),
        [SMEM] + [VMEM] * (1 + len(received)),
        (VMEM,) * radix,
        [],
        (position, kept) + tuple(received),
    )


def total_kernel(*refs):
    total = refs[0][...].astype(f32)
    for part in refs[1:-1]:
        total = total + part[...].astype(f32)
    refs[-1][...] = total.astype(bf16)


def total(parts):
    return call(
        total_kernel,
        "total",
        16,
        parts[0].size,
        8 * parts[0].size,
        shape_of(parts[0].shape, bf16),
        [VMEM] * len(parts),
        VMEM,
        [],
        tuple(parts),
    )


def load_weights(layer, first_in, second_in, first, second, sems):
    loads = [
        pltpu.make_async_copy(first_in.at[layer], first, sems.at[0]),
        pltpu.make_async_copy(second_in.at[layer], second, sems.at[1]),
    ]
    for load in loads:
        load.start()
    return loads


def hub_network_kernel(layer, rows_in, *refs):
    parts, (first_in, second_in, out, first, second, sems) = refs[:-6], refs[-6:]
    loads = load_weights(layer, first_in, second_in, first, second, sems)
    u = rows_in[...].astype(f32)
    for part in parts:
        u = u + part[...].astype(f32)
    for load in loads:
        load.wait()
    out[...] = network(u, first, second, 512)


def hub_network(layer, rows_in, parts, first, second):
    return call(
        functools.partial(hub_network_kernel, layer),
        "hub_network",
        24,
        4 * rows_in.size * first.shape[-1],
        2 * first.size,
        shape_of(rows_in.shape, bf16),
        [VMEM] * (1 + len(parts)) + [ANY] * 2,
        VMEM,
        [
            pltpu.VMEM(first.shape[1:], bf16),
            pltpu.VMEM(second.shape[1:], bf16),
            pltpu.SemaphoreType.DMA((2,)),
        ],
        (rows_in,) + tuple(parts) + (first, second),
    )


def before_kernel(
    layer, plan, count, hubs_in, own_in, tiles_in, first_in, second_in, base, out,
    hubs, own, tiles, first, second, u, result, tile_sems, block_sems, sem,
):
    own_count = own.shape[0]
    hub_count = hubs.shape[0]
    remote = tiles_in.shape[0] - tiles.shape[0]
    load_own = pltpu.make_async_copy(own_in, own, sem.at[0])
    load_hubs = pltpu.make_async_copy(hubs_in, hubs, sem.at[1])
    loads = tile_loads(tiles_in, tiles, tile_sems)
    load_own.start()
    load_hubs.start()
    for_live(count, loads, start)
    load_own.wait()
    u[:own_count] = own[...].astype(f32)
    load_hubs.wait()
    for_live(count, loads, wait)
    weights = load_weights(layer, first_in, second_in, first, second, sem.at[pl.ds(2, 2)])
    n_fed = plan[COUNTS, N_FED]
    add_products(
        plan, plan[COUNTS, N_HUB], plan[COUNTS, N_OWN], remote, tiles, hubs, own, u, hub_count, own_count
    )

    def save(place):
        return pltpu.make_async_copy(u.at[plan[BLOCK, place]], base.at[place], block_sems.at[place])

    def finish(place):
        block = plan[BLOCK, place]
        return pltpu.make_async_copy(result.at[place], out.at[block], block_sems.at[place])

    each_block(0, n_fed, save, start)
    for load in weights:
        load.wait()

    def step(group, many):
        first_place, number = group * GROUP, many * GROUP
        places = [first_place + lane for lane in range(number)]
        values = jnp.concatenate([u[plan[BLOCK, place]] for place in places], axis=0)
        values = network(values, first, second, 512)
        result[pl.ds(first_place, number)] = values.reshape((number,) + result.shape[1:])
        finish_group(first_place, number, n_fed, own_count, finish)

    run_groups(n_fed // GROUP, own_count // GROUP, step)
    each_block(0, n_fed, save, wait)
    each_block(n_fed, own_count, finish, wait)


def before(layer, plan, count, hubs, own, tiles, first, second, remote):
    own_count, block_size, width = own.shape
    return call(
        functools.partial(before_kernel, layer),
        "before",
        58,
        4 * own.size * first.shape[-1] // 3,
        18 * MIB,
        (shape_of(own.shape, f32), shape_of(own.shape, bf16)),
        [SMEM] * 2 + [ANY] * 5,
        (ANY, ANY),
        [
            pltpu.VMEM(hubs.shape, bf16),
            pltpu.VMEM(own.shape, bf16),
            pltpu.VMEM((tiles.shape[0] - remote,) + tiles.shape[1:], bf16),
            pltpu.VMEM(first.shape[1:], bf16),
            pltpu.VMEM(second.shape[1:], bf16),
            pltpu.VMEM((own_count + 1, block_size, width), f32),
            pltpu.VMEM(own.shape, bf16),
            pltpu.SemaphoreType.DMA((4,)),
            pltpu.SemaphoreType.DMA((own_count,)),
            pltpu.SemaphoreType.DMA((4,)),
        ],
        (plan, count, hubs, own, tiles, first, second),
    )


def after_kernel(
    layer, with_send, plan, base, done, incoming, tiles, first_in, second_in, *refs
):
    out, refs = refs[0], refs[1:]
    if with_send:
        (sums, outgoing), refs = refs[:2], refs[2:]
    u, extra, inc, adj, first, second, result, base_sems, block_sems, sem = refs
    own_count = u.shape[0]
    remote = incoming.shape[0]
    parts = 4
    size = remote // parts
    loads = []
    for part in range(parts):
        cut = pl.ds(part * size, size)
        loads.append(
            (
                pltpu.make_async_copy(tiles.at[cut], adj.at[cut], sem.at[2 + 2 * part]),
                pltpu.make_async_copy(incoming.at[cut], inc.at[cut], sem.at[3 + 2 * part]),
            )
        )
        for load in loads[-1]:
            load.start()
    n_fed, n_held = plan[COUNTS, N_FED], plan[COUNTS, N_HELD]
    groups = rounded_up(n_fed)
    groups_now = rounded_up(plan[COUNTS, N_NOW]) if with_send else groups
    apart = jnp.minimum(groups * GROUP, n_held)
    early = jnp.minimum(groups, 2)

    def cut_of(group):
        return pl.ds(group * GROUP, GROUP)

    def load_base(group):
        cut = cut_of(group)
        return pltpu.make_async_copy(base.at[cut], u.at[cut], base_sems.at[group])

    def load_done(place):
        block = plan[BLOCK, place]
        return pltpu.make_async_copy(done.at[block], result.at[place], block_sems.at[place])

    def finish(place):
        block = plan[BLOCK, place]
        return pltpu.make_async_copy(result.at[place], out.at[block], block_sems.at[place])

    extra[...] = jnp.zeros_like(extra)
    for part in range(parts):
        for load in loads[part]:
            load.wait()
        if part == 0:
            weights = load_weights(layer, first_in, second_in, first, second, sem.at[pl.ds(0, 2)])
            each_block(0, early, load_base, start)
        if part == 2:
            each_block(early, groups, load_base, start)
            if with_send:
                each_block(apart, n_held, load_done, start)
        products = [dot(adj[slot], inc[slot]) for slot in range(part * size, (part + 1) * size)]
        for lane, product in enumerate(products):
            extra[plan[REMOTE, part * size + lane]] += product
    for load in weights:
        load.wait()
    n_now = jnp.minimum(groups_now * GROUP, n_fed)

    def step(group, many):
        for offset in range(many):
            load_base(group + offset).wait()
        cut = pl.ds(group * GROUP, many * GROUP)
        values = (u[cut] + extra[cut]).reshape(many * GROUP * u.shape[1], u.shape[2])
        values = network(values, first, second, 512)
        result[cut] = values.reshape((many * GROUP,) + result.shape[1:])
        finish_group(group * GROUP, many * GROUP, 0, n_now, finish)

    run_groups(0, groups_now, step)
    copies = []
    if with_send:
        each_block(n_fed, apart, load_done, start)
        each_block(n_fed, n_held, load_done, wait)
        for number in range(remote):
            copy = pltpu.make_async_copy(
                result.at[plan[GOING, number]], outgoing.at[number], sem.at[number]
            )
            copy.start()
            copies.append(copy)

        def save(group):
            cut = cut_of(group)
            return pltpu.make_async_copy(u.at[cut], sums.at[cut], base_sems.at[group])

        def keep(group, unused):
            load_base(group).wait()
            cut = cut_of(group)
            u[cut] += extra[cut]
            save(group).start()
            return unused

        lax.fori_loop(groups_now, groups, keep, 0)
        each_block(groups_now, groups, save, wait)
    each_block(0, n_now, finish, wait)
    for copy in copies:
        copy.wait()


def after(layer, plan, base, done, incoming, tiles, first, second, with_send):
    own_count = base.shape[0]
    remote = incoming.shape[0]
    shapes = [shape_of(base.shape, bf16)]
    if with_send:
        shapes += [shape_of(base.shape, f32), shape_of(incoming.shape, bf16)]
    return pl.pallas_call(
        functools.partial(after_kernel, layer, with_send),
        out_shape=tuple(shapes),
        in_specs=[SMEM] + [ANY] * 6,
        out_specs=(ANY,) * len(shapes),
        scratch_shapes=[
            pltpu.VMEM(base.shape, f32),
            pltpu.VMEM(base.shape, f32),
            pltpu.VMEM(incoming.shape, bf16),
            pltpu.VMEM((remote,) + tiles.shape[1:], bf16),
            pltpu.VMEM(first.shape[1:], bf16),
            pltpu.VMEM(second.shape[1:], bf16),
            pltpu.VMEM(base.shape, bf16),
            pltpu.SemaphoreType.DMA((own_count // GROUP,)),
            pltpu.SemaphoreType.DMA((own_count,)),
            pltpu.SemaphoreType.DMA((max(10, remote),)),
        ],
        input_output_aliases={2: 0, 1: 1} if with_send else {2: 0},
        compiler_params=pltpu.CompilerParams(vmem_limit_bytes=58 * MIB),
        cost_estimate=pl.CostEstimate(
            flops=4 * base.size * first.shape[-1], bytes_accessed=16 * MIB, transcendentals=0
        ),
        name="after",
    )(plan, base, done, incoming, tiles, first, second)


def late_kernel(
    layer, plan, sums, done, first_in, second_in, out, u, first, second, result, base_sems, block_sems, sem
):
    weights = load_weights(layer, first_in, second_in, first, second, sem)
    n_fed = plan[COUNTS, N_FED]
    groups = rounded_up(n_fed)
    groups_now = rounded_up(plan[COUNTS, N_NOW])

    def load(group):
        cut = pl.ds(group * GROUP, GROUP)
        return pltpu.make_async_copy(sums.at[cut], u.at[cut], base_sems.at[group])

    def finish(place):
        block = plan[BLOCK, place]
        return pltpu.make_async_copy(result.at[place], out.at[block], block_sems.at[place])

    each_block(groups_now, groups, load, start)
    for part in weights:
        part.wait()

    def step(group, many):
        for offset in range(many):
            load(group + offset).wait()
        cut = pl.ds(group * GROUP, many * GROUP)
        values = network(
            u[cut].reshape(many * GROUP * u.shape[1], u.shape[2]), first, second, 512
        )
        result[cut] = values.reshape((many * GROUP,) + result.shape[1:])
        finish_group(group * GROUP, many * GROUP, 0, n_fed, finish)

    run_groups(groups_now, groups, step)
    each_block(jnp.minimum(groups_now * GROUP, n_fed), n_fed, finish, wait)


def late(layer, plan, sums, done, first, second):
    own_count = sums.shape[0]
    return pl.pallas_call(
        functools.partial(late_kernel, layer),
        out_shape=shape_of(done.shape, bf16),
        in_specs=[SMEM] + [ANY] * 4,
        out_specs=ANY,
        scratch_shapes=[
            pltpu.VMEM(sums.shape, f32),
            pltpu.VMEM(first.shape[1:], bf16),
            pltpu.VMEM(second.shape[1:], bf16),
            pltpu.VMEM(sums.shape, bf16),
            pltpu.SemaphoreType.DMA((own_count // GROUP,)),
            pltpu.SemaphoreType.DMA((own_count,)),
            pltpu.SemaphoreType.DMA((2,)),
        ],
        input_output_aliases={2: 0},
        compiler_params=pltpu.CompilerParams(vmem_limit_bytes=58 * MIB),
        cost_estimate=pl.CostEstimate(
            flops=sums.size * first.shape[-1], bytes_accessed=5 * MIB, transcendentals=0
        ),
        name="late",
    )(plan, sums, done, first, second)


def exchange(x, bit):
    devices = lax.axis_size("dev")
    return lax.ppermute(x, "dev", [(i, i ^ bit) for i in range(devices)])


def all_digits():
    devices = lax.axis_size("dev")
    digits, bit = [(1, 2)], 2
    while bit < devices:
        radix = 4 if 4 * bit <= devices else 2
        digits.append((bit, radix))
        bit *= radix
    return digits


def gather_step(x, bit, radix):
    return [x] + [exchange(x, bit * offset) for offset in range(1, radix)]


def gather_far(x, digits):
    return gather_step(x, *digits[-1])


def gather_near(pieces, digits):
    for digit in digits[-2:0:-1]:
        pieces = gather_step(jnp.concatenate(pieces, axis=0), *digit)
    return pieces


def gather_last(pieces, digits):
    x = jnp.concatenate(pieces, axis=0)
    return x, exchange(x, digits[0][0])


def scatter_near(position, kept, sent, digits, local):
    received = [exchange(sent, digits[0][0])]
    for bit, radix in digits[1:-1]:
        kept, *sent = combine(position, kept, received, bit, radix, local, f32)
        received = [exchange(part, bit * (1 + number)) for number, part in enumerate(sent)]
    return kept, received


def scatter_far(position, kept, received, digits, local, sent_type):
    bit, radix = digits[-1]
    kept, *sent = combine(position, kept, received, bit, radix, local, sent_type)
    return [kept] + [exchange(part, bit * (1 + number)) for number, part in enumerate(sent)]


def share_far(kept, received, digits):
    bit, radix = digits[-1]
    parts = [kept] + received
    while radix > 1:
        mine = total(parts)
        parts = [mine, exchange(mine, bit)]
        bit, radix = 2 * bit, radix // 2
    return parts


def body(
    peripheral, hubs, tiles, tile_rows, local_cols, tile_count, send_list, hub_place, w_in, w_out
):
    position = lax.axis_index("dev")
    digits = all_digits()
    block_size = tiles.shape[1]
    width = peripheral.shape[1]
    own_count = peripheral.shape[0] // block_size
    hub_rows = hub_place.shape[0]
    hub_count = hub_rows // block_size
    local = hubs.shape[0]
    remote = send_list.shape[1]
    place_col = hub_place.reshape(hub_rows, 1)
    place_row = hub_place.reshape(1, hub_rows)
    me = position.astype(jnp.int32).reshape(1)
    own = peripheral.reshape(own_count, block_size, width)
    all_to_all = functools.partial(
        lax.all_to_all, axis_name="dev", split_axis=0, concat_axis=0, tiled=True
    )

    pieces = gather_far(hubs, digits)
    outgoing = pack(send_list, own)
    outgoing, *pieces = lax.optimization_barrier((outgoing, *pieces))
    pieces = gather_near(pieces, digits)
    outgoing, place_col, tile_rows, local_cols, *pieces = lax.optimization_barrier(
        (outgoing, place_col, tile_rows, local_cols, *pieces)
    )
    plan = make_plan(me, tile_count, tile_rows, local_cols, send_list, hub_count, own_count)
    incoming = all_to_all(outgoing)
    halves = gather_last(pieces, digits)
    hub_table, mine, kept, sent = hub_first(
        digits, plan, tile_count, me, place_col, halves, own, tiles, local, remote
    )
    base, done = before(0, plan, tile_count, hub_table, own, tiles, w_in, w_out, remote)
    kept, received = scatter_near(me, kept, sent, digits, local)
    base, done, *received = lax.optimization_barrier((base, done, *received))
    parts = share_far(kept, received, digits)
    hub_new = hub_network(0, mine, parts, w_in, w_out)
    base, hub_new = lax.optimization_barrier((base, hub_new))
    done, sums, outgoing = after(0, plan, base, done, incoming, tiles, w_in, w_out, True)

    pieces = gather_near([hub_new], digits)
    outgoing, *pieces = lax.optimization_barrier((outgoing, *pieces))
    incoming = all_to_all(outgoing)
    own = late(0, plan, sums, done, w_in, w_out)
    halves = gather_last(pieces, digits)
    hub_table, mine, kept, sent = hub_second(
        digits, plan, tile_count, me, place_row, halves, own, tiles, local, remote
    )
    base, done = before(1, plan, tile_count, hub_table, own, tiles, w_in, w_out, remote)
    kept, received = scatter_near(me, kept, sent, digits, local)
    base, done, *received = lax.optimization_barrier((base, done, *received))
    parts = scatter_far(me, kept, received, digits, local, bf16)
    (peri_out,) = after(1, plan, base, done, incoming, tiles, w_in, w_out, False)
    peri_out, *parts = lax.optimization_barrier((peri_out, *parts))
    hub_out = hub_network(1, mine, parts, w_in, w_out)
    return (peri_out.reshape(peripheral.shape), hub_out)


def solution(mesh):
    in_specs = (
        P("dev", None),
        P("dev", None),
        P("dev", None, None),
        P("dev"),
        P("dev"),
        P("dev"),
        P("dev", None),
        P(),
        P(),
        P(),
    )
    out_specs = (P("dev", None), P("dev", None))
    return jax.shard_map(body, mesh=mesh, in_specs=in_specs, out_specs=out_specs, check_vma=False)
```

```python
import functools

import jax
import jax.numpy as jnp
from jax import lax
from jax.experimental import pallas as pl
from jax.experimental.pallas import tpu as pltpu
from jax.sharding import PartitionSpec as P

epsilon = 1e-06
f32 = jnp.float32
bf16 = jnp.bfloat16
MIB = 1024 * 1024
VMEM = pl.BlockSpec(memory_space=pltpu.VMEM)
SMEM = pl.BlockSpec(memory_space=pltpu.SMEM)
ANY = pl.BlockSpec(memory_space=pl.ANY)
GROUP = 2
SLOTS = 8


def dot(a, b):
    return jnp.dot(a, b, preferred_element_type=f32)


def shape_of(shape, dtype):
    return jax.ShapeDtypeStruct(tuple(shape), dtype)


def call(kernel, name, mib, flops, moved, out_shape, in_specs, out_specs, scratch, args):
    return pl.pallas_call(
        kernel,
        out_shape=out_shape,
        in_specs=in_specs,
        out_specs=out_specs,
        scratch_shapes=scratch,
        compiler_params=pltpu.CompilerParams(vmem_limit_bytes=mib * MIB),
        cost_estimate=pl.CostEstimate(flops=flops, bytes_accessed=moved, transcendentals=0),
        name=name,
    )(*args)


def normalise(u):
    return (u * lax.rsqrt(jnp.mean(u * u, axis=-1, keepdims=True) + epsilon)).astype(bf16)


def network(u, first, second, hidden_step):
    normed = normalise(u)
    total = u
    for start in range(0, first.shape[-1], hidden_step):
        cut = slice(start, start + hidden_step)
        hidden = jnp.maximum(dot(normed, first[:, cut]), 0.0).astype(bf16)
        total = total + dot(hidden, second[cut, :])
    return total.astype(bf16)


SLOT, ROW, COL, BLOCK, REMOTE, GOING, COUNTS = range(7)
N_HUB, N_OWN, N_NOW, N_FED, N_HELD = range(5)


def ranked(key, size):
    down = lax.broadcasted_iota(jnp.int32, (size, size), 0)
    along = lax.broadcasted_iota(jnp.int32, (size, size), 1)
    wide = jnp.broadcast_to(key, (size, size))
    tall = jnp.sum(jnp.where(down == along, wide, 0), axis=1, keepdims=True)
    ahead = (wide < tall) | ((wide == tall) & (along < down))
    return jnp.sum(ahead.astype(jnp.int32), axis=1, keepdims=True)


def plan_kernel(hub_count, own_count, remote, position, count, rows_in, cols_in, chosen, plan):
    capacity = rows_in.shape[1]
    shift = position[0] * own_count
    rows = jnp.where(rows_in[...] < hub_count, rows_in[...], rows_in[...] - shift)
    cols = jnp.where(cols_in[...] < hub_count, cols_in[...], cols_in[...] - shift)
    plan[...] = jnp.zeros_like(plan)
    slot = lax.broadcasted_iota(jnp.int32, (1, capacity), 1)
    picked = (slot >= remote) & (slot < count[0])
    of_hub = picked & (rows < hub_count)
    of_own = picked & (rows >= hub_count)
    key = jnp.where(of_hub, 0, jnp.where(of_own, 1, 2))
    place = ranked(key, capacity)
    down = lax.broadcasted_iota(jnp.int32, (capacity, capacity), 0)
    along = lax.broadcasted_iota(jnp.int32, (capacity, capacity), 1)
    here = place == along

    def column(row):
        wide = jnp.broadcast_to(row, (capacity, capacity))
        return jnp.sum(jnp.where(down == along, wide, 0), axis=1, keepdims=True)

    def ordered(values):
        return jnp.sum(jnp.where(here, values, 0), axis=0, keepdims=True)

    plan[SLOT : SLOT + 1, :capacity] = ordered(down)
    plan[ROW : ROW + 1, :capacity] = ordered(column(rows))
    plan[COL : COL + 1, :capacity] = ordered(column(cols))

    block = lax.broadcasted_iota(jnp.int32, (own_count, remote), 0)
    target = rows[:, :remote] - hub_count
    fed = jnp.max((block == target).astype(jnp.int32), axis=1, keepdims=True)
    sent = jnp.max((block == chosen[...]).astype(jnp.int32), axis=1, keepdims=True)
    key = 3 - 2 * fed - sent
    down = lax.broadcasted_iota(jnp.int32, (own_count, own_count), 0)
    along = lax.broadcasted_iota(jnp.int32, (own_count, own_count), 1)
    row_key = jnp.sum(jnp.where(down == along, key, 0), axis=0, keepdims=True)
    place = ranked(row_key, own_count)
    plan[BLOCK : BLOCK + 1, :own_count] = jnp.sum(
        jnp.where(place == along, down, 0), axis=0, keepdims=True
    )
    plan[REMOTE : REMOTE + 1, :remote] = jnp.sum(
        jnp.where(block == target, place, 0), axis=0, keepdims=True
    )
    plan[GOING : GOING + 1, :remote] = jnp.sum(
        jnp.where(block == chosen[...], place, 0), axis=0, keepdims=True
    )
    numbers = [
        jnp.sum(of_hub.astype(jnp.int32), axis=1, keepdims=True),
        jnp.sum(of_own.astype(jnp.int32), axis=1, keepdims=True),
        jnp.sum((row_key < 1).astype(jnp.int32), axis=1, keepdims=True),
        jnp.sum((row_key < 2).astype(jnp.int32), axis=1, keepdims=True),
        jnp.sum((row_key < 3).astype(jnp.int32), axis=1, keepdims=True),
    ]
    lane = lax.broadcasted_iota(jnp.int32, (1, plan.shape[1]), 1)
    counts = jnp.zeros((1, plan.shape[1]), jnp.int32)
    for place, number in enumerate(numbers):
        counts = jnp.where(lane == place, number, counts)
    plan[COUNTS : COUNTS + 1, :] = counts


def make_plan(position, count, rows, cols, chosen, hub_count, own_count):
    capacity, remote = rows.shape[0], chosen.shape[1]
    wide = -(-max(capacity, own_count, remote) // 128) * 128
    cols = jnp.concatenate([jnp.zeros((remote,), jnp.int32), cols])
    return call(
        functools.partial(plan_kernel, hub_count, own_count, remote),
        "plan",
        24,
        10**6,
        10**4,
        shape_of((8, wide), jnp.int32),
        [SMEM, SMEM, VMEM, VMEM, VMEM],
        VMEM,
        [],
        (position, count, rows.reshape(1, capacity), cols.reshape(1, capacity), chosen),
    )


def tile_loads(source, tiles, sems):
    remote = source.shape[0] - tiles.shape[0]
    size = tiles.shape[0] // 4
    loads = []
    for part in range(4):
        cut = pl.ds(remote + part * size, size)
        copy = pltpu.make_async_copy(source.at[cut], tiles.at[pl.ds(part * size, size)], sems.at[part])
        loads.append((remote + part * size, copy))
    return loads


def for_live(count, loads, act):
    for first_slot, load in loads:

        @pl.when(count[0] > first_slot)
        def _(load=load):
            act(load)


def add_products(plan, begin, found, remote, tiles, hubs, own, total, shift, spare):
    hub_count = hubs.shape[0]

    def step(number, unused):
        where, products = [], []
        for lane in range(SLOTS):
            place = number * SLOTS + lane
            live = place < found
            place = begin + jnp.minimum(place, found - 1)
            where.append(jnp.where(live, plan[ROW, place] - shift, spare))
            col = plan[COL, place]
            of_hub = hubs[jnp.minimum(col, hub_count - 1)]
            of_own = own[jnp.maximum(col - hub_count, 0)]
            tile = tiles[plan[SLOT, place] - remote]
            products.append(dot(tile, jnp.where(col < hub_count, of_hub, of_own)))
        for row, product in zip(where, products):
            total[row] += product
        return unused

    lax.fori_loop(0, (found + SLOTS - 1) // SLOTS, step, 0)


def each_block(first_place, last_place, copy_of, act):
    def step(place, unused):
        act(copy_of(place))
        return unused

    lax.fori_loop(first_place, last_place, step, 0)


def start(copy):
    copy.start()


def wait(copy):
    copy.wait()


def run_groups(begin, end, step):
    def four(number, unused):
        step(begin + 4 * number, 4)
        return unused

    lax.fori_loop(0, (end - begin) // 4, four, 0)
    rest = (end - begin) % 4

    @pl.when(rest >= 2)
    def _():
        step(end - rest, 2)

    @pl.when(rest % 2 == 1)
    def _():
        step(end - 1, 1)


def rounded_up(number):
    return (number + GROUP - 1) // GROUP


def finish_group(first_place, number, begin, end, finish):
    for lane in range(number):
        place = first_place + lane

        @pl.when((place >= begin) & (place < end))
        def _(place=place):
            finish(place).start()


def pack_kernel(chosen, blocks, outgoing, held, sems):
    loads, stores = [], []
    for number in range(outgoing.shape[0]):
        here = held.at[number]
        loads.append(pltpu.make_async_copy(blocks.at[chosen[0, number]], here, sems.at[number]))
        stores.append(pltpu.make_async_copy(here, outgoing.at[number], sems.at[number]))
        loads[-1].start()
    for load, store in zip(loads, stores):
        load.wait()
        store.start()
    for store in stores:
        store.wait()


def pack(chosen, blocks):
    devices = chosen.shape[1]
    return call(
        pack_kernel,
        "pack",
        58,
        0,
        2 * blocks.size * 2,
        shape_of((devices,) + blocks.shape[1:], bf16),
        [SMEM, ANY],
        ANY,
        [
            pltpu.VMEM((devices,) + blocks.shape[1:], bf16),
            pltpu.SemaphoreType.DMA((devices,)),
        ],
        (chosen, blocks),
    )


def slot_place(slot, digits):
    place, weight = 0, 1
    for bit, radix in digits[:0:-1]:
        place += weight * ((slot // bit) % radix)
        weight *= radix
    return slot % 2, place


def place_shards(me, halves, table, digits, local, in_order):
    bit = digits[-1][0]
    for slot in range(table.shape[0] // local):
        half, place = slot_place(slot, digits)
        device = slot // bit * bit + (lax.rem(me, bit) ^ (slot % bit)) if in_order else me ^ slot
        first_row = pl.multiple_of(device * local, local)
        table[pl.ds(first_row, local), :] = halves[half][place * local : (place + 1) * local, :]


def split_sums(me, sums, local, kept, sent):
    odd = me % 2
    width = sums.shape[-1]
    pairs = sums.reshape(-1, 2, local, width)
    kept[...] = jnp.where(odd == 1, pairs[:, 1], pairs[:, 0]).reshape(kept.shape).astype(kept.dtype)
    sent[...] = jnp.where(odd == 1, pairs[:, 0], pairs[:, 1]).reshape(sent.shape).astype(sent.dtype)


def hub_first_kernel(
    digits, plan, count, position, place_col, half0, half1, own_hbm, tiles_hbm,
    hubs, mine, kept, sent, own, tiles, table, total, sems,
):
    hub_count, block_size, width = hubs.shape
    hub_rows = hub_count * block_size
    local = mine.shape[0] // digits[-1][1]
    remote = tiles_hbm.shape[0] - tiles.shape[0]
    loads = tile_loads(tiles_hbm, tiles, sems)
    load = pltpu.make_async_copy(own_hbm, own, sems.at[4])
    load.start()
    for_live(count, loads, start)
    me = position[0]
    place_shards(me, (half0, half1), table, digits, local, False)
    total[...] = jnp.zeros_like(total)
    step = 2 * block_size

    def rows_step(number, unused):
        cut = pl.ds(pl.multiple_of(number * step, step), step)
        lanes = lax.broadcasted_iota(jnp.int32, (step, hub_rows), 1)
        unit = jnp.where(place_col[cut, :] == lanes, 1.0, 0.0).astype(bf16)
        placed = dot(unit, table[...]).astype(bf16)
        hubs[pl.ds(number * 2, 2)] = placed.reshape(2, block_size, width)
        return unused

    lax.fori_loop(0, hub_rows // step, rows_step, 0)
    load.wait()
    for_live(count, loads, wait)
    add_products(plan, 0, plan[COUNTS, N_HUB], remote, tiles, hubs, own, total, 0, hub_count)
    split_sums(me, total[:hub_count], local, kept, sent)
    flat = hubs.reshape(hub_rows, width)
    bit, radix = digits[-1]
    for digit in range(radix):
        first_row = pl.multiple_of((digit * bit + lax.rem(me, bit)) * local, local)
        mine[digit * local : (digit + 1) * local, :] = flat[pl.ds(first_row, local), :]


def hub_first(digits, plan, count, position, place_col, halves, own, tiles, local, remote):
    block_size, width = own.shape[1:]
    hub_rows = place_col.shape[0]
    hub_count = hub_rows // block_size
    half = shape_of((hub_rows // 2, width), f32)
    return call(
        functools.partial(hub_first_kernel, digits),
        "hub_first",
        48,
        2 * hub_rows * hub_rows * width,
        14 * MIB,
        (
            shape_of((hub_count, block_size, width), bf16),
            shape_of((digits[-1][1] * local, width), bf16),
            half,
            half,
        ),
        [SMEM] * 3 + [VMEM] * 3 + [ANY] * 2,
        (VMEM,) * 4,
        [
            pltpu.VMEM(own.shape, bf16),
            pltpu.VMEM((tiles.shape[0] - remote,) + tiles.shape[1:], bf16),
            pltpu.VMEM((hub_rows, width), bf16),
            pltpu.VMEM((hub_count + 1, block_size, width), f32),
            pltpu.SemaphoreType.DMA((5,)),
        ],
        (plan, count, position, place_col) + tuple(halves) + (own, tiles),
    )


def hub_second_kernel(
    digits, plan, count, position, place_row, half0, half1, own_hbm, tiles_hbm,
    hubs, mine, kept, sent, own, tiles, total, placed, sems,
):
    hub_count, block_size, width = hubs.shape
    hub_rows = hub_count * block_size
    local = mine.shape[0]
    remote = tiles_hbm.shape[0] - tiles.shape[0]
    loads = tile_loads(tiles_hbm, tiles, sems)
    load = pltpu.make_async_copy(own_hbm, own, sems.at[4])
    load.start()
    for_live(count, loads, start)
    me = position[0]
    flat = hubs.reshape(hub_rows, width)
    place_shards(me, (half0, half1), flat, digits, local, True)
    total[...] = jnp.zeros_like(total)

    def unit_rows(start, step):
        down = lax.broadcasted_iota(jnp.int32, (step, hub_rows), 0) + start
        return jnp.where(place_row[...] == down, 1.0, 0.0).astype(bf16)

    mine[...] = dot(unit_rows(me * local, local), flat[...]).astype(bf16)
    load.wait()
    for_live(count, loads, wait)
    add_products(plan, 0, plan[COUNTS, N_HUB], remote, tiles, hubs, own, total, 0, hub_count)
    sums = total[:hub_count].reshape(hub_rows, width)
    high = sums.astype(bf16)
    low = (sums - high.astype(f32)).astype(bf16)
    step = 2 * block_size

    def rows_step(number, unused):
        start = number * step
        unit = unit_rows(start, step)
        placed[pl.ds(pl.multiple_of(start, step), step), :] = dot(unit, high) + dot(unit, low)
        return unused

    lax.fori_loop(0, hub_rows // step, rows_step, 0)
    split_sums(me, placed[...], local, kept, sent)


def hub_second(digits, plan, count, position, place_row, halves, own, tiles, local, remote):
    block_size, width = own.shape[1:]
    hub_rows = place_row.shape[1]
    hub_count = hub_rows // block_size
    return call(
        functools.partial(hub_second_kernel, digits),
        "hub_second",
        48,
        2 * hub_rows * hub_rows * width,
        14 * MIB,
        (
            shape_of((hub_count, block_size, width), bf16),
            shape_of((local, width), bf16),
            shape_of((hub_rows // 2, width), f32),
            shape_of((hub_rows // 2, width), f32),
        ),
        [SMEM] * 3 + [VMEM] * 3 + [ANY] * 2,
        (VMEM,) * 4,
        [
            pltpu.VMEM(own.shape, bf16),
            pltpu.VMEM((tiles.shape[0] - remote,) + tiles.shape[1:], bf16),
            pltpu.VMEM((hub_count + 1, block_size, width), f32),
            pltpu.VMEM((hub_rows, width), f32),
            pltpu.SemaphoreType.DMA((5,)),
        ],
        (plan, count, position, place_row) + tuple(halves) + (own, tiles),
    )


def combine(position, kept, received, bit, radix, local, sent_type):
    rows = kept.shape[0] // radix
    width = kept.shape[1]

    def kernel(position, kept_in, *refs):
        received, outs = refs[: -radix], refs[-radix:]
        total = kept_in[...].astype(f32)
        for part in received:
            total = total + part[...].astype(f32)
        digit = (position[0] // bit) % radix
        parts = total.reshape(rows // local, radix, local, width)
        for offset, out in enumerate(outs):
            value = parts[:, 0]
            for number in range(1, radix):
                value = jnp.where((digit ^ offset) == number, parts[:, number], value)
            out[...] = value.reshape(rows, width).astype(out.dtype)

    shapes = [shape_of((rows, width), f32)] + [shape_of((rows, width), sent_type)] * (radix - 1)
    return call(
        kernel,
        "combine",
        16,
        kept.size,
        12 * kept.size,
        tuple(shapes),
        [SMEM] + [VMEM] * (1 + len(received)),
        (VMEM,) * radix,
        [],
        (position, kept) + tuple(received),
    )


def total_kernel(*refs):
    total = refs[0][...].astype(f32)
    for part in refs[1:-1]:
        total = total + part[...].astype(f32)
    refs[-1][...] = total.astype(bf16)


def total(parts):
    return call(
        total_kernel,
        "total",
        16,
        parts[0].size,
        8 * parts[0].size,
        shape_of(parts[0].shape, bf16),
        [VMEM] * len(parts),
        VMEM,
        [],
        tuple(parts),
    )


def load_weights(layer, first_in, second_in, first, second, sems):
    loads = [
        pltpu.make_async_copy(first_in.at[layer], first, sems.at[0]),
        pltpu.make_async_copy(second_in.at[layer], second, sems.at[1]),
    ]
    for load in loads:
        load.start()
    return loads


def hub_network_kernel(layer, rows_in, *refs):
    parts, (first_in, second_in, out, first, second, sems) = refs[:-6], refs[-6:]
    loads = load_weights(layer, first_in, second_in, first, second, sems)
    u = rows_in[...].astype(f32)
    for part in parts:
        u = u + part[...].astype(f32)
    for load in loads:
        load.wait()
    out[...] = network(u, first, second, 512)


def hub_network(layer, rows_in, parts, first, second):
    return call(
        functools.partial(hub_network_kernel, layer),
        "hub_network",
        24,
        4 * rows_in.size * first.shape[-1],
        2 * first.size,
        shape_of(rows_in.shape, bf16),
        [VMEM] * (1 + len(parts)) + [ANY] * 2,
        VMEM,
        [
            pltpu.VMEM(first.shape[1:], bf16),
            pltpu.VMEM(second.shape[1:], bf16),
            pltpu.SemaphoreType.DMA((2,)),
        ],
        (rows_in,) + tuple(parts) + (first, second),
    )


def before_kernel(
    layer, plan, count, hubs_in, own_in, tiles_in, first_in, second_in, base, out,
    hubs, own, tiles, first, second, u, result, tile_sems, block_sems, sem,
):
    own_count = own.shape[0]
    hub_count = hubs.shape[0]
    remote = tiles_in.shape[0] - tiles.shape[0]
    load_own = pltpu.make_async_copy(own_in, own, sem.at[0])
    load_hubs = pltpu.make_async_copy(hubs_in, hubs, sem.at[1])
    loads = tile_loads(tiles_in, tiles, tile_sems)
    load_own.start()
    load_hubs.start()
    for_live(count, loads, start)
    load_own.wait()
    u[:own_count] = own[...].astype(f32)
    load_hubs.wait()
    for_live(count, loads, wait)
    weights = load_weights(layer, first_in, second_in, first, second, sem.at[pl.ds(2, 2)])
    n_fed = plan[COUNTS, N_FED]
    add_products(
        plan, plan[COUNTS, N_HUB], plan[COUNTS, N_OWN], remote, tiles, hubs, own, u, hub_count, own_count
    )

    def save(place):
        return pltpu.make_async_copy(u.at[plan[BLOCK, place]], base.at[place], block_sems.at[place])

    def finish(place):
        block = plan[BLOCK, place]
        return pltpu.make_async_copy(result.at[place], out.at[block], block_sems.at[place])

    each_block(0, n_fed, save, start)
    for load in weights:
        load.wait()

    def step(group, many):
        first_place, number = group * GROUP, many * GROUP
        places = [first_place + lane for lane in range(number)]
        values = jnp.concatenate([u[plan[BLOCK, place]] for place in places], axis=0)
        values = network(values, first, second, 512)
        result[pl.ds(first_place, number)] = values.reshape((number,) + result.shape[1:])
        finish_group(first_place, number, n_fed, own_count, finish)

    run_groups(n_fed // GROUP, own_count // GROUP, step)
    each_block(0, n_fed, save, wait)
    each_block(n_fed, own_count, finish, wait)


def before(layer, plan, count, hubs, own, tiles, first, second, remote):
    own_count, block_size, width = own.shape
    return call(
        functools.partial(before_kernel, layer),
        "before",
        58,
        4 * own.size * first.shape[-1] // 3,
        18 * MIB,
        (shape_of(own.shape, f32), shape_of(own.shape, bf16)),
        [SMEM] * 2 + [ANY] * 5,
        (ANY, ANY),
        [
            pltpu.VMEM(hubs.shape, bf16),
            pltpu.VMEM(own.shape, bf16),
            pltpu.VMEM((tiles.shape[0] - remote,) + tiles.shape[1:], bf16),
            pltpu.VMEM(first.shape[1:], bf16),
            pltpu.VMEM(second.shape[1:], bf16),
            pltpu.VMEM((own_count + 1, block_size, width), f32),
            pltpu.VMEM(own.shape, bf16),
            pltpu.SemaphoreType.DMA((4,)),
            pltpu.SemaphoreType.DMA((own_count,)),
            pltpu.SemaphoreType.DMA((4,)),
        ],
        (plan, count, hubs, own, tiles, first, second),
    )


def after_kernel(
    layer, with_send, plan, base, done, incoming, tiles, first_in, second_in, *refs
):
    out, refs = refs[0], refs[1:]
    if with_send:
        (sums, outgoing), refs = refs[:2], refs[2:]
    u, extra, inc, adj, first, second, result, base_sems, block_sems, sem = refs
    own_count = u.shape[0]
    remote = incoming.shape[0]
    parts = 4
    size = remote // parts
    loads = []
    for part in range(parts):
        cut = pl.ds(part * size, size)
        loads.append(
            (
                pltpu.make_async_copy(tiles.at[cut], adj.at[cut], sem.at[2 + 2 * part]),
                pltpu.make_async_copy(incoming.at[cut], inc.at[cut], sem.at[3 + 2 * part]),
            )
        )
        for load in loads[-1]:
            load.start()
    n_fed, n_held = plan[COUNTS, N_FED], plan[COUNTS, N_HELD]
    groups = rounded_up(n_fed)
    groups_now = rounded_up(plan[COUNTS, N_NOW]) if with_send else groups
    apart = jnp.minimum(groups * GROUP, n_held)
    early = jnp.minimum(groups, 4)

    def cut_of(group):
        return pl.ds(group * GROUP, GROUP)

    def load_base(group):
        cut = cut_of(group)
        return pltpu.make_async_copy(base.at[cut], u.at[cut], base_sems.at[group])

    def load_done(place):
        block = plan[BLOCK, place]
        return pltpu.make_async_copy(done.at[block], result.at[place], block_sems.at[place])

    def finish(place):
        block = plan[BLOCK, place]
        return pltpu.make_async_copy(result.at[place], out.at[block], block_sems.at[place])

    extra[...] = jnp.zeros_like(extra)
    for part in range(parts):
        for load in loads[part]:
            load.wait()
        if part == 0:
            weights = load_weights(layer, first_in, second_in, first, second, sem.at[pl.ds(0, 2)])
            each_block(0, early, load_base, start)
        if part == 2:
            each_block(early, groups, load_base, start)
            if with_send:
                each_block(apart, n_held, load_done, start)
        products = [dot(adj[slot], inc[slot]) for slot in range(part * size, (part + 1) * size)]
        for lane, product in enumerate(products):
            extra[plan[REMOTE, part * size + lane]] += product
    for load in weights:
        load.wait()
    n_now = jnp.minimum(groups_now * GROUP, n_fed)

    def step(group, many):
        for offset in range(many):
            load_base(group + offset).wait()
        cut = pl.ds(group * GROUP, many * GROUP)
        values = (u[cut] + extra[cut]).reshape(many * GROUP * u.shape[1], u.shape[2])
        values = network(values, first, second, 512)
        result[cut] = values.reshape((many * GROUP,) + result.shape[1:])
        finish_group(group * GROUP, many * GROUP, 0, n_now, finish)

    run_groups(0, groups_now, step)
    copies = []
    if with_send:
        each_block(n_fed, apart, load_done, start)
        each_block(n_fed, n_held, load_done, wait)
        for number in range(remote):
            copy = pltpu.make_async_copy(
                result.at[plan[GOING, number]], outgoing.at[number], sem.at[number]
            )
            copy.start()
            copies.append(copy)

        def save(group):
            cut = cut_of(group)
            return pltpu.make_async_copy(u.at[cut], sums.at[cut], base_sems.at[group])

        def keep(group, unused):
            load_base(group).wait()
            cut = cut_of(group)
            u[cut] += extra[cut]
            save(group).start()
            return unused

        lax.fori_loop(groups_now, groups, keep, 0)
        each_block(groups_now, groups, save, wait)
    each_block(0, n_now, finish, wait)
    for copy in copies:
        copy.wait()


def after(layer, plan, base, done, incoming, tiles, first, second, with_send):
    own_count = base.shape[0]
    remote = incoming.shape[0]
    shapes = [shape_of(base.shape, bf16)]
    if with_send:
        shapes += [shape_of(base.shape, f32), shape_of(incoming.shape, bf16)]
    return pl.pallas_call(
        functools.partial(after_kernel, layer, with_send),
        out_shape=tuple(shapes),
        in_specs=[SMEM] + [ANY] * 6,
        out_specs=(ANY,) * len(shapes),
        scratch_shapes=[
            pltpu.VMEM(base.shape, f32),
            pltpu.VMEM(base.shape, f32),
            pltpu.VMEM(incoming.shape, bf16),
            pltpu.VMEM((remote,) + tiles.shape[1:], bf16),
            pltpu.VMEM(first.shape[1:], bf16),
            pltpu.VMEM(second.shape[1:], bf16),
            pltpu.VMEM(base.shape, bf16),
            pltpu.SemaphoreType.DMA((own_count // GROUP,)),
            pltpu.SemaphoreType.DMA((own_count,)),
            pltpu.SemaphoreType.DMA((max(10, remote),)),
        ],
        input_output_aliases={2: 0, 1: 1} if with_send else {2: 0},
        compiler_params=pltpu.CompilerParams(vmem_limit_bytes=58 * MIB),
        cost_estimate=pl.CostEstimate(
            flops=4 * base.size * first.shape[-1], bytes_accessed=16 * MIB, transcendentals=0
        ),
        name="after",
    )(plan, base, done, incoming, tiles, first, second)


def late_kernel(
    layer, plan, sums, done, first_in, second_in, out, u, first, second, result, base_sems, block_sems, sem
):
    weights = load_weights(layer, first_in, second_in, first, second, sem)
    n_fed = plan[COUNTS, N_FED]
    groups = rounded_up(n_fed)
    groups_now = rounded_up(plan[COUNTS, N_NOW])

    def load(group):
        cut = pl.ds(group * GROUP, GROUP)
        return pltpu.make_async_copy(sums.at[cut], u.at[cut], base_sems.at[group])

    def finish(place):
        block = plan[BLOCK, place]
        return pltpu.make_async_copy(result.at[place], out.at[block], block_sems.at[place])

    each_block(groups_now, groups, load, start)
    for part in weights:
        part.wait()

    def step(group, many):
        for offset in range(many):
            load(group + offset).wait()
        cut = pl.ds(group * GROUP, many * GROUP)
        values = network(
            u[cut].reshape(many * GROUP * u.shape[1], u.shape[2]), first, second, 512
        )
        result[cut] = values.reshape((many * GROUP,) + result.shape[1:])
        finish_group(group * GROUP, many * GROUP, 0, n_fed, finish)

    run_groups(groups_now, groups, step)
    each_block(jnp.minimum(groups_now * GROUP, n_fed), n_fed, finish, wait)


def late(layer, plan, sums, done, first, second):
    own_count = sums.shape[0]
    return pl.pallas_call(
        functools.partial(late_kernel, layer),
        out_shape=shape_of(done.shape, bf16),
        in_specs=[SMEM] + [ANY] * 4,
        out_specs=ANY,
        scratch_shapes=[
            pltpu.VMEM(sums.shape, f32),
            pltpu.VMEM(first.shape[1:], bf16),
            pltpu.VMEM(second.shape[1:], bf16),
            pltpu.VMEM(sums.shape, bf16),
            pltpu.SemaphoreType.DMA((own_count // GROUP,)),
            pltpu.SemaphoreType.DMA((own_count,)),
            pltpu.SemaphoreType.DMA((2,)),
        ],
        input_output_aliases={2: 0},
        compiler_params=pltpu.CompilerParams(vmem_limit_bytes=58 * MIB),
        cost_estimate=pl.CostEstimate(
            flops=sums.size * first.shape[-1], bytes_accessed=5 * MIB, transcendentals=0
        ),
        name="late",
    )(plan, sums, done, first, second)


def exchange(x, bit):
    devices = lax.axis_size("dev")
    return lax.ppermute(x, "dev", [(i, i ^ bit) for i in range(devices)])


def all_digits():
    devices = lax.axis_size("dev")
    digits, bit = [(1, 2)], 2
    while bit < devices:
        radix = 4 if 4 * bit <= devices else 2
        digits.append((bit, radix))
        bit *= radix
    return digits


def gather_step(x, bit, radix):
    return [x] + [exchange(x, bit * offset) for offset in range(1, radix)]


def gather_far(x, digits):
    return gather_step(x, *digits[-1])


def gather_near(pieces, digits):
    for digit in digits[-2:0:-1]:
        pieces = gather_step(jnp.concatenate(pieces, axis=0), *digit)
    return pieces


def gather_last(pieces, digits):
    x = jnp.concatenate(pieces, axis=0)
    return x, exchange(x, digits[0][0])


def scatter_near(position, kept, sent, digits, local):
    received = [exchange(sent, digits[0][0])]
    for bit, radix in digits[1:-1]:
        kept, *sent = combine(position, kept, received, bit, radix, local, f32)
        received = [exchange(part, bit * (1 + number)) for number, part in enumerate(sent)]
    return kept, received


def scatter_far(position, kept, received, digits, local, sent_type):
    bit, radix = digits[-1]
    kept, *sent = combine(position, kept, received, bit, radix, local, sent_type)
    return [kept] + [exchange(part, bit * (1 + number)) for number, part in enumerate(sent)]


def share_far(kept, received, digits):
    bit, radix = digits[-1]
    parts = [kept] + received
    while radix > 1:
        mine = total(parts)
        parts = [mine, exchange(mine, bit)]
        bit, radix = 2 * bit, radix // 2
    return parts


def body(
    peripheral, hubs, tiles, tile_rows, local_cols, tile_count, send_list, hub_place, w_in, w_out
):
    position = lax.axis_index("dev")
    digits = all_digits()
    block_size = tiles.shape[1]
    width = peripheral.shape[1]
    own_count = peripheral.shape[0] // block_size
    hub_rows = hub_place.shape[0]
    hub_count = hub_rows // block_size
    local = hubs.shape[0]
    remote = send_list.shape[1]
    place_col = hub_place.reshape(hub_rows, 1)
    place_row = hub_place.reshape(1, hub_rows)
    me = position.astype(jnp.int32).reshape(1)
    own = peripheral.reshape(own_count, block_size, width)
    all_to_all = functools.partial(
        lax.all_to_all, axis_name="dev", split_axis=0, concat_axis=0, tiled=True
    )

    pieces = gather_far(hubs, digits)
    outgoing = pack(send_list, own)
    outgoing, *pieces = lax.optimization_barrier((outgoing, *pieces))
    pieces = gather_near(pieces, digits)
    outgoing, place_col, tile_rows, local_cols, *pieces = lax.optimization_barrier(
        (outgoing, place_col, tile_rows, local_cols, *pieces)
    )
    plan = make_plan(me, tile_count, tile_rows, local_cols, send_list, hub_count, own_count)
    incoming = all_to_all(outgoing)
    halves = gather_last(pieces, digits)
    hub_table, mine, kept, sent = hub_first(
        digits, plan, tile_count, me, place_col, halves, own, tiles, local, remote
    )
    base, done = before(0, plan, tile_count, hub_table, own, tiles, w_in, w_out, remote)
    kept, received = scatter_near(me, kept, sent, digits, local)
    base, done, *received = lax.optimization_barrier((base, done, *received))
    parts = share_far(kept, received, digits)
    hub_new = hub_network(0, mine, parts, w_in, w_out)
    base, hub_new = lax.optimization_barrier((base, hub_new))
    done, sums, outgoing = after(0, plan, base, done, incoming, tiles, w_in, w_out, True)

    pieces = gather_near([hub_new], digits)
    outgoing, *pieces = lax.optimization_barrier((outgoing, *pieces))
    incoming = all_to_all(outgoing)
    own = late(0, plan, sums, done, w_in, w_out)
    halves = gather_last(pieces, digits)
    hub_table, mine, kept, sent = hub_second(
        digits, plan, tile_count, me, place_row, halves, own, tiles, local, remote
    )
    base, done = before(1, plan, tile_count, hub_table, own, tiles, w_in, w_out, remote)
    kept, received = scatter_near(me, kept, sent, digits, local)
    base, done, *received = lax.optimization_barrier((base, done, *received))
    parts = scatter_far(me, kept, received, digits, local, bf16)
    (peri_out,) = after(1, plan, base, done, incoming, tiles, w_in, w_out, False)
    peri_out, *parts = lax.optimization_barrier((peri_out, *parts))
    hub_out = hub_network(1, mine, parts, w_in, w_out)
    return (peri_out.reshape(peripheral.shape), hub_out)


def solution(mesh):
    in_specs = (
        P("dev", None),
        P("dev", None),
        P("dev", None, None),
        P("dev"),
        P("dev"),
        P("dev"),
        P("dev", None),
        P(),
        P(),
        P(),
    )
    out_specs = (P("dev", None), P("dev", None))
    return jax.shard_map(body, mesh=mesh, in_specs=in_specs, out_specs=out_specs, check_vma=False)
```

```python
import functools

import jax
import jax.numpy as jnp
from jax import lax
from jax.experimental import pallas as pl
from jax.experimental.pallas import tpu as pltpu
from jax.sharding import PartitionSpec as P

epsilon = 1e-06
f32 = jnp.float32
bf16 = jnp.bfloat16
MIB = 1024 * 1024
VMEM = pl.BlockSpec(memory_space=pltpu.VMEM)
SMEM = pl.BlockSpec(memory_space=pltpu.SMEM)
ANY = pl.BlockSpec(memory_space=pl.ANY)
GROUP = 2
SLOTS = 16


def dot(a, b):
    return jnp.dot(a, b, preferred_element_type=f32)


def shape_of(shape, dtype):
    return jax.ShapeDtypeStruct(tuple(shape), dtype)


def call(kernel, name, mib, flops, moved, out_shape, in_specs, out_specs, scratch, args):
    return pl.pallas_call(
        kernel,
        out_shape=out_shape,
        in_specs=in_specs,
        out_specs=out_specs,
        scratch_shapes=scratch,
        compiler_params=pltpu.CompilerParams(vmem_limit_bytes=mib * MIB),
        cost_estimate=pl.CostEstimate(flops=flops, bytes_accessed=moved, transcendentals=0),
        name=name,
    )(*args)


def normalise(u):
    return (u * lax.rsqrt(jnp.mean(u * u, axis=-1, keepdims=True) + epsilon)).astype(bf16)


def network(u, first, second, hidden_step):
    normed = normalise(u)
    total = u
    for start in range(0, first.shape[-1], hidden_step):
        cut = slice(start, start + hidden_step)
        hidden = jnp.maximum(dot(normed, first[:, cut]), 0.0).astype(bf16)
        total = total + dot(hidden, second[cut, :])
    return total.astype(bf16)


SLOT, ROW, COL, BLOCK, REMOTE, GOING, COUNTS = range(7)
N_HUB, N_OWN, N_NOW, N_FED, N_HELD = range(5)


def ranked(key, size):
    down = lax.broadcasted_iota(jnp.int32, (size, size), 0)
    along = lax.broadcasted_iota(jnp.int32, (size, size), 1)
    wide = jnp.broadcast_to(key, (size, size))
    tall = jnp.sum(jnp.where(down == along, wide, 0), axis=1, keepdims=True)
    ahead = (wide < tall) | ((wide == tall) & (along < down))
    return jnp.sum(ahead.astype(jnp.int32), axis=1, keepdims=True)


def plan_kernel(hub_count, own_count, remote, position, count, rows_in, cols_in, chosen, plan):
    capacity = rows_in.shape[1]
    shift = position[0] * own_count
    rows = jnp.where(rows_in[...] < hub_count, rows_in[...], rows_in[...] - shift)
    cols = jnp.where(cols_in[...] < hub_count, cols_in[...], cols_in[...] - shift)
    plan[...] = jnp.zeros_like(plan)
    slot = lax.broadcasted_iota(jnp.int32, (1, capacity), 1)
    picked = (slot >= remote) & (slot < count[0])
    of_hub = picked & (rows < hub_count)
    of_own = picked & (rows >= hub_count)
    key = jnp.where(of_hub, 0, jnp.where(of_own, 1, 2))
    place = ranked(key, capacity)
    down = lax.broadcasted_iota(jnp.int32, (capacity, capacity), 0)
    along = lax.broadcasted_iota(jnp.int32, (capacity, capacity), 1)
    here = place == along

    def column(row):
        wide = jnp.broadcast_to(row, (capacity, capacity))
        return jnp.sum(jnp.where(down == along, wide, 0), axis=1, keepdims=True)

    def ordered(values):
        return jnp.sum(jnp.where(here, values, 0), axis=0, keepdims=True)

    plan[SLOT : SLOT + 1, :capacity] = ordered(down)
    plan[ROW : ROW + 1, :capacity] = ordered(column(rows))
    plan[COL : COL + 1, :capacity] = ordered(column(cols))

    block = lax.broadcasted_iota(jnp.int32, (own_count, remote), 0)
    target = rows[:, :remote] - hub_count
    fed = jnp.max((block == target).astype(jnp.int32), axis=1, keepdims=True)
    sent = jnp.max((block == chosen[...]).astype(jnp.int32), axis=1, keepdims=True)
    key = 3 - 2 * fed - sent
    down = lax.broadcasted_iota(jnp.int32, (own_count, own_count), 0)
    along = lax.broadcasted_iota(jnp.int32, (own_count, own_count), 1)
    row_key = jnp.sum(jnp.where(down == along, key, 0), axis=0, keepdims=True)
    place = ranked(row_key, own_count)
    plan[BLOCK : BLOCK + 1, :own_count] = jnp.sum(
        jnp.where(place == along, down, 0), axis=0, keepdims=True
    )
    plan[REMOTE : REMOTE + 1, :remote] = jnp.sum(
        jnp.where(block == target, place, 0), axis=0, keepdims=True
    )
    plan[GOING : GOING + 1, :remote] = jnp.sum(
        jnp.where(block == chosen[...], place, 0), axis=0, keepdims=True
    )
    numbers = [
        jnp.sum(of_hub.astype(jnp.int32), axis=1, keepdims=True),
        jnp.sum(of_own.astype(jnp.int32), axis=1, keepdims=True),
        jnp.sum((row_key < 1).astype(jnp.int32), axis=1, keepdims=True),
        jnp.sum((row_key < 2).astype(jnp.int32), axis=1, keepdims=True),
        jnp.sum((row_key < 3).astype(jnp.int32), axis=1, keepdims=True),
    ]
    lane = lax.broadcasted_iota(jnp.int32, (1, plan.shape[1]), 1)
    counts = jnp.zeros((1, plan.shape[1]), jnp.int32)
    for place, number in enumerate(numbers):
        counts = jnp.where(lane == place, number, counts)
    plan[COUNTS : COUNTS + 1, :] = counts


def make_plan(position, count, rows, cols, chosen, hub_count, own_count):
    capacity, remote = rows.shape[0], chosen.shape[1]
    wide = -(-max(capacity, own_count, remote) // 128) * 128
    cols = jnp.concatenate([jnp.zeros((remote,), jnp.int32), cols])
    return call(
        functools.partial(plan_kernel, hub_count, own_count, remote),
        "plan",
        24,
        10**6,
        10**4,
        shape_of((8, wide), jnp.int32),
        [SMEM, SMEM, VMEM, VMEM, VMEM],
        VMEM,
        [],
        (position, count, rows.reshape(1, capacity), cols.reshape(1, capacity), chosen),
    )


def tile_loads(source, tiles, sems):
    remote = source.shape[0] - tiles.shape[0]
    size = tiles.shape[0] // 4
    loads = []
    for part in range(4):
        cut = pl.ds(remote + part * size, size)
        copy = pltpu.make_async_copy(source.at[cut], tiles.at[pl.ds(part * size, size)], sems.at[part])
        loads.append((remote + part * size, copy))
    return loads


def for_live(count, loads, act):
    for first_slot, load in loads:

        @pl.when(count[0] > first_slot)
        def _(load=load):
            act(load)


def add_products(plan, begin, found, remote, tiles, hubs, own, total, shift, spare):
    hub_count = hubs.shape[0]

    def step(number, unused):
        where, products = [], []
        for lane in range(SLOTS):
            place = number * SLOTS + lane
            live = place < found
            place = begin + jnp.minimum(place, found - 1)
            where.append(jnp.where(live, plan[ROW, place] - shift, spare))
            col = plan[COL, place]
            of_hub = hubs[jnp.minimum(col, hub_count - 1)]
            of_own = own[jnp.maximum(col - hub_count, 0)]
            tile = tiles[plan[SLOT, place] - remote]
            products.append(dot(tile, jnp.where(col < hub_count, of_hub, of_own)))
        for row, product in zip(where, products):
            total[row] += product
        return unused

    lax.fori_loop(0, (found + SLOTS - 1) // SLOTS, step, 0)


def each_block(first_place, last_place, copy_of, act):
    def step(place, unused):
        act(copy_of(place))
        return unused

    lax.fori_loop(first_place, last_place, step, 0)


def start(copy):
    copy.start()


def wait(copy):
    copy.wait()


def run_groups(begin, end, step):
    def four(number, unused):
        step(begin + 4 * number, 4)
        return unused

    lax.fori_loop(0, (end - begin) // 4, four, 0)
    rest = (end - begin) % 4

    @pl.when(rest >= 2)
    def _():
        step(end - rest, 2)

    @pl.when(rest % 2 == 1)
    def _():
        step(end - 1, 1)


def rounded_up(number):
    return (number + GROUP - 1) // GROUP


def finish_group(first_place, number, begin, end, finish):
    for lane in range(number):
        place = first_place + lane

        @pl.when((place >= begin) & (place < end))
        def _(place=place):
            finish(place).start()


def pack_kernel(chosen, blocks, outgoing, held, sems):
    loads, stores = [], []
    for number in range(outgoing.shape[0]):
        here = held.at[number]
        loads.append(pltpu.make_async_copy(blocks.at[chosen[0, number]], here, sems.at[number]))
        stores.append(pltpu.make_async_copy(here, outgoing.at[number], sems.at[number]))
        loads[-1].start()
    for load, store in zip(loads, stores):
        load.wait()
        store.start()
    for store in stores:
        store.wait()


def pack(chosen, blocks):
    devices = chosen.shape[1]
    return call(
        pack_kernel,
        "pack",
        58,
        0,
        2 * blocks.size * 2,
        shape_of((devices,) + blocks.shape[1:], bf16),
        [SMEM, ANY],
        ANY,
        [
            pltpu.VMEM((devices,) + blocks.shape[1:], bf16),
            pltpu.SemaphoreType.DMA((devices,)),
        ],
        (chosen, blocks),
    )


def slot_place(slot, digits):
    place, weight = 0, 1
    for bit, radix in digits[:0:-1]:
        place += weight * ((slot // bit) % radix)
        weight *= radix
    return slot % 2, place


def place_shards(me, halves, table, digits, local, in_order):
    bit = digits[-1][0]
    for slot in range(table.shape[0] // local):
        half, place = slot_place(slot, digits)
        device = slot // bit * bit + (lax.rem(me, bit) ^ (slot % bit)) if in_order else me ^ slot
        first_row = pl.multiple_of(device * local, local)
        table[pl.ds(first_row, local), :] = halves[half][place * local : (place + 1) * local, :]


def split_sums(me, sums, local, kept, sent):
    odd = me % 2
    width = sums.shape[-1]
    pairs = sums.reshape(-1, 2, local, width)
    kept[...] = jnp.where(odd == 1, pairs[:, 1], pairs[:, 0]).reshape(kept.shape).astype(kept.dtype)
    sent[...] = jnp.where(odd == 1, pairs[:, 0], pairs[:, 1]).reshape(sent.shape).astype(sent.dtype)


def hub_first_kernel(
    digits, plan, count, position, place_col, half0, half1, own_hbm, tiles_hbm,
    hubs, mine, kept, sent, own, tiles, table, total, sems,
):
    hub_count, block_size, width = hubs.shape
    hub_rows = hub_count * block_size
    local = mine.shape[0] // digits[-1][1]
    remote = tiles_hbm.shape[0] - tiles.shape[0]
    loads = tile_loads(tiles_hbm, tiles, sems)
    load = pltpu.make_async_copy(own_hbm, own, sems.at[4])
    load.start()
    for_live(count, loads, start)
    me = position[0]
    place_shards(me, (half0, half1), table, digits, local, False)
    total[...] = jnp.zeros_like(total)
    step = 2 * block_size

    def rows_step(number, unused):
        cut = pl.ds(pl.multiple_of(number * step, step), step)
        lanes = lax.broadcasted_iota(jnp.int32, (step, hub_rows), 1)
        unit = jnp.where(place_col[cut, :] == lanes, 1.0, 0.0).astype(bf16)
        placed = dot(unit, table[...]).astype(bf16)
        hubs[pl.ds(number * 2, 2)] = placed.reshape(2, block_size, width)
        return unused

    lax.fori_loop(0, hub_rows // step, rows_step, 0)
    load.wait()
    for_live(count, loads, wait)
    add_products(plan, 0, plan[COUNTS, N_HUB], remote, tiles, hubs, own, total, 0, hub_count)
    split_sums(me, total[:hub_count], local, kept, sent)
    flat = hubs.reshape(hub_rows, width)
    bit, radix = digits[-1]
    for digit in range(radix):
        first_row = pl.multiple_of((digit * bit + lax.rem(me, bit)) * local, local)
        mine[digit * local : (digit + 1) * local, :] = flat[pl.ds(first_row, local), :]


def hub_first(digits, plan, count, position, place_col, halves, own, tiles, local, remote):
    block_size, width = own.shape[1:]
    hub_rows = place_col.shape[0]
    hub_count = hub_rows // block_size
    half = shape_of((hub_rows // 2, width), f32)
    return call(
        functools.partial(hub_first_kernel, digits),
        "hub_first",
        48,
        2 * hub_rows * hub_rows * width,
        14 * MIB,
        (
            shape_of((hub_count, block_size, width), bf16),
            shape_of((digits[-1][1] * local, width), bf16),
            half,
            half,
        ),
        [SMEM] * 3 + [VMEM] * 3 + [ANY] * 2,
        (VMEM,) * 4,
        [
            pltpu.VMEM(own.shape, bf16),
            pltpu.VMEM((tiles.shape[0] - remote,) + tiles.shape[1:], bf16),
            pltpu.VMEM((hub_rows, width), bf16),
            pltpu.VMEM((hub_count + 1, block_size, width), f32),
            pltpu.SemaphoreType.DMA((5,)),
        ],
        (plan, count, position, place_col) + tuple(halves) + (own, tiles),
    )


def hub_second_kernel(
    digits, plan, count, position, place_row, half0, half1, own_hbm, tiles_hbm,
    hubs, mine, kept, sent, own, tiles, total, placed, sems,
):
    hub_count, block_size, width = hubs.shape
    hub_rows = hub_count * block_size
    local = mine.shape[0]
    remote = tiles_hbm.shape[0] - tiles.shape[0]
    loads = tile_loads(tiles_hbm, tiles, sems)
    load = pltpu.make_async_copy(own_hbm, own, sems.at[4])
    load.start()
    for_live(count, loads, start)
    me = position[0]
    flat = hubs.reshape(hub_rows, width)
    place_shards(me, (half0, half1), flat, digits, local, True)
    total[...] = jnp.zeros_like(total)

    def unit_rows(start, step):
        down = lax.broadcasted_iota(jnp.int32, (step, hub_rows), 0) + start
        return jnp.where(place_row[...] == down, 1.0, 0.0).astype(bf16)

    mine[...] = dot(unit_rows(me * local, local), flat[...]).astype(bf16)
    load.wait()
    for_live(count, loads, wait)
    add_products(plan, 0, plan[COUNTS, N_HUB], remote, tiles, hubs, own, total, 0, hub_count)
    sums = total[:hub_count].reshape(hub_rows, width)
    high = sums.astype(bf16)
    low = (sums - high.astype(f32)).astype(bf16)
    step = 2 * block_size

    def rows_step(number, unused):
        start = number * step
        unit = unit_rows(start, step)
        placed[pl.ds(pl.multiple_of(start, step), step), :] = dot(unit, high) + dot(unit, low)
        return unused

    lax.fori_loop(0, hub_rows // step, rows_step, 0)
    split_sums(me, placed[...], local, kept, sent)


def hub_second(digits, plan, count, position, place_row, halves, own, tiles, local, remote):
    block_size, width = own.shape[1:]
    hub_rows = place_row.shape[1]
    hub_count = hub_rows // block_size
    return call(
        functools.partial(hub_second_kernel, digits),
        "hub_second",
        48,
        2 * hub_rows * hub_rows * width,
        14 * MIB,
        (
            shape_of((hub_count, block_size, width), bf16),
            shape_of((local, width), bf16),
            shape_of((hub_rows // 2, width), f32),
            shape_of((hub_rows // 2, width), f32),
        ),
        [SMEM] * 3 + [VMEM] * 3 + [ANY] * 2,
        (VMEM,) * 4,
        [
            pltpu.VMEM(own.shape, bf16),
            pltpu.VMEM((tiles.shape[0] - remote,) + tiles.shape[1:], bf16),
            pltpu.VMEM((hub_count + 1, block_size, width), f32),
            pltpu.VMEM((hub_rows, width), f32),
            pltpu.SemaphoreType.DMA((5,)),
        ],
        (plan, count, position, place_row) + tuple(halves) + (own, tiles),
    )


def combine(position, kept, received, bit, radix, local, sent_type):
    rows = kept.shape[0] // radix
    width = kept.shape[1]

    def kernel(position, kept_in, *refs):
        received, outs = refs[: -radix], refs[-radix:]
        total = kept_in[...].astype(f32)
        for part in received:
            total = total + part[...].astype(f32)
        digit = (position[0] // bit) % radix
        parts = total.reshape(rows // local, radix, local, width)
        for offset, out in enumerate(outs):
            value = parts[:, 0]
            for number in range(1, radix):
                value = jnp.where((digit ^ offset) == number, parts[:, number], value)
            out[...] = value.reshape(rows, width).astype(out.dtype)

    shapes = [shape_of((rows, width), f32)] + [shape_of((rows, width), sent_type)] * (radix - 1)
    return call(
        kernel,
        "combine",
        16,
        kept.size,
        12 * kept.size,
        tuple(shapes),
        [SMEM] + [VMEM] * (1 + len(received)),
        (VMEM,) * radix,
        [],
        (position, kept) + tuple(received),
    )


def total_kernel(*refs):
    total = refs[0][...].astype(f32)
    for part in refs[1:-1]:
        total = total + part[...].astype(f32)
    refs[-1][...] = total.astype(bf16)


def total(parts):
    return call(
        total_kernel,
        "total",
        16,
        parts[0].size,
        8 * parts[0].size,
        shape_of(parts[0].shape, bf16),
        [VMEM] * len(parts),
        VMEM,
        [],
        tuple(parts),
    )


def load_weights(layer, first_in, second_in, first, second, sems):
    loads = [
        pltpu.make_async_copy(first_in.at[layer], first, sems.at[0]),
        pltpu.make_async_copy(second_in.at[layer], second, sems.at[1]),
    ]
    for load in loads:
        load.start()
    return loads


def hub_network_kernel(layer, rows_in, *refs):
    parts, (first_in, second_in, out, first, second, sems) = refs[:-6], refs[-6:]
    loads = load_weights(layer, first_in, second_in, first, second, sems)
    u = rows_in[...].astype(f32)
    for part in parts:
        u = u + part[...].astype(f32)
    for load in loads:
        load.wait()
    out[...] = network(u, first, second, 512)


def hub_network(layer, rows_in, parts, first, second):
    return call(
        functools.partial(hub_network_kernel, layer),
        "hub_network",
        24,
        4 * rows_in.size * first.shape[-1],
        2 * first.size,
        shape_of(rows_in.shape, bf16),
        [VMEM] * (1 + len(parts)) + [ANY] * 2,
        VMEM,
        [
            pltpu.VMEM(first.shape[1:], bf16),
            pltpu.VMEM(second.shape[1:], bf16),
            pltpu.SemaphoreType.DMA((2,)),
        ],
        (rows_in,) + tuple(parts) + (first, second),
    )


def before_kernel(
    layer, plan, count, hubs_in, own_in, tiles_in, first_in, second_in, base, out,
    hubs, own, tiles, first, second, u, result, tile_sems, block_sems, sem,
):
    own_count = own.shape[0]
    hub_count = hubs.shape[0]
    remote = tiles_in.shape[0] - tiles.shape[0]
    load_own = pltpu.make_async_copy(own_in, own, sem.at[0])
    load_hubs = pltpu.make_async_copy(hubs_in, hubs, sem.at[1])
    loads = tile_loads(tiles_in, tiles, tile_sems)
    load_own.start()
    load_hubs.start()
    for_live(count, loads, start)
    load_own.wait()
    u[:own_count] = own[...].astype(f32)
    load_hubs.wait()
    for_live(count, loads, wait)
    weights = load_weights(layer, first_in, second_in, first, second, sem.at[pl.ds(2, 2)])
    n_fed = plan[COUNTS, N_FED]
    add_products(
        plan, plan[COUNTS, N_HUB], plan[COUNTS, N_OWN], remote, tiles, hubs, own, u, hub_count, own_count
    )

    def save(place):
        return pltpu.make_async_copy(u.at[plan[BLOCK, place]], base.at[place], block_sems.at[place])

    def finish(place):
        block = plan[BLOCK, place]
        return pltpu.make_async_copy(result.at[place], out.at[block], block_sems.at[place])

    each_block(0, n_fed, save, start)
    for load in weights:
        load.wait()

    def step(group, many):
        first_place, number = group * GROUP, many * GROUP
        places = [first_place + lane for lane in range(number)]
        values = jnp.concatenate([u[plan[BLOCK, place]] for place in places], axis=0)
        values = network(values, first, second, 512)
        result[pl.ds(first_place, number)] = values.reshape((number,) + result.shape[1:])
        finish_group(first_place, number, n_fed, own_count, finish)

    run_groups(n_fed // GROUP, own_count // GROUP, step)
    each_block(0, n_fed, save, wait)
    each_block(n_fed, own_count, finish, wait)


def before(layer, plan, count, hubs, own, tiles, first, second, remote):
    own_count, block_size, width = own.shape
    return call(
        functools.partial(before_kernel, layer),
        "before",
        58,
        4 * own.size * first.shape[-1] // 3,
        18 * MIB,
        (shape_of(own.shape, f32), shape_of(own.shape, bf16)),
        [SMEM] * 2 + [ANY] * 5,
        (ANY, ANY),
        [
            pltpu.VMEM(hubs.shape, bf16),
            pltpu.VMEM(own.shape, bf16),
            pltpu.VMEM((tiles.shape[0] - remote,) + tiles.shape[1:], bf16),
            pltpu.VMEM(first.shape[1:], bf16),
            pltpu.VMEM(second.shape[1:], bf16),
            pltpu.VMEM((own_count + 1, block_size, width), f32),
            pltpu.VMEM(own.shape, bf16),
            pltpu.SemaphoreType.DMA((4,)),
            pltpu.SemaphoreType.DMA((own_count,)),
            pltpu.SemaphoreType.DMA((4,)),
        ],
        (plan, count, hubs, own, tiles, first, second),
    )


def after_kernel(
    layer, with_send, plan, base, done, incoming, tiles, first_in, second_in, *refs
):
    out, refs = refs[0], refs[1:]
    if with_send:
        (sums, outgoing), refs = refs[:2], refs[2:]
    u, extra, inc, adj, first, second, result, base_sems, block_sems, sem = refs
    own_count = u.shape[0]
    remote = incoming.shape[0]
    parts = 4
    size = remote // parts
    loads = []
    for part in range(parts):
        cut = pl.ds(part * size, size)
        loads.append(
            (
                pltpu.make_async_copy(tiles.at[cut], adj.at[cut], sem.at[2 + 2 * part]),
                pltpu.make_async_copy(incoming.at[cut], inc.at[cut], sem.at[3 + 2 * part]),
            )
        )
        for load in loads[-1]:
            load.start()
    n_fed, n_held = plan[COUNTS, N_FED], plan[COUNTS, N_HELD]
    groups = rounded_up(n_fed)
    groups_now = rounded_up(plan[COUNTS, N_NOW]) if with_send else groups
    apart = jnp.minimum(groups * GROUP, n_held)
    early = jnp.minimum(groups, 4)

    def cut_of(group):
        return pl.ds(group * GROUP, GROUP)

    def load_base(group):
        cut = cut_of(group)
        return pltpu.make_async_copy(base.at[cut], u.at[cut], base_sems.at[group])

    def load_done(place):
        block = plan[BLOCK, place]
        return pltpu.make_async_copy(done.at[block], result.at[place], block_sems.at[place])

    def finish(place):
        block = plan[BLOCK, place]
        return pltpu.make_async_copy(result.at[place], out.at[block], block_sems.at[place])

    extra[...] = jnp.zeros_like(extra)
    for part in range(parts):
        for load in loads[part]:
            load.wait()
        if part == 0:
            weights = load_weights(layer, first_in, second_in, first, second, sem.at[pl.ds(0, 2)])
            each_block(0, early, load_base, start)
        if part == 2:
            each_block(early, groups, load_base, start)
            if with_send:
                each_block(apart, n_held, load_done, start)
        products = [dot(adj[slot], inc[slot]) for slot in range(part * size, (part + 1) * size)]
        for lane, product in enumerate(products):
            extra[plan[REMOTE, part * size + lane]] += product
    for load in weights:
        load.wait()
    n_now = jnp.minimum(groups_now * GROUP, n_fed)

    def step(group, many):
        for offset in range(many):
            load_base(group + offset).wait()
        cut = pl.ds(group * GROUP, many * GROUP)
        values = (u[cut] + extra[cut]).reshape(many * GROUP * u.shape[1], u.shape[2])
        values = network(values, first, second, 512)
        result[cut] = values.reshape((many * GROUP,) + result.shape[1:])
        finish_group(group * GROUP, many * GROUP, 0, n_now, finish)

    run_groups(0, groups_now, step)
    copies = []
    if with_send:
        each_block(n_fed, apart, load_done, start)
        each_block(n_fed, n_held, load_done, wait)
        for number in range(remote):
            copy = pltpu.make_async_copy(
                result.at[plan[GOING, number]], outgoing.at[number], sem.at[number]
            )
            copy.start()
            copies.append(copy)

        def save(group):
            cut = cut_of(group)
            return pltpu.make_async_copy(u.at[cut], sums.at[cut], base_sems.at[group])

        def keep(group, unused):
            load_base(group).wait()
            cut = cut_of(group)
            u[cut] += extra[cut]
            save(group).start()
            return unused

        lax.fori_loop(groups_now, groups, keep, 0)
        each_block(groups_now, groups, save, wait)
    each_block(0, n_now, finish, wait)
    for copy in copies:
        copy.wait()


def after(layer, plan, base, done, incoming, tiles, first, second, with_send):
    own_count = base.shape[0]
    remote = incoming.shape[0]
    shapes = [shape_of(base.shape, bf16)]
    if with_send:
        shapes += [shape_of(base.shape, f32), shape_of(incoming.shape, bf16)]
    return pl.pallas_call(
        functools.partial(after_kernel, layer, with_send),
        out_shape=tuple(shapes),
        in_specs=[SMEM] + [ANY] * 6,
        out_specs=(ANY,) * len(shapes),
        scratch_shapes=[
            pltpu.VMEM(base.shape, f32),
            pltpu.VMEM(base.shape, f32),
            pltpu.VMEM(incoming.shape, bf16),
            pltpu.VMEM((remote,) + tiles.shape[1:], bf16),
            pltpu.VMEM(first.shape[1:], bf16),
            pltpu.VMEM(second.shape[1:], bf16),
            pltpu.VMEM(base.shape, bf16),
            pltpu.SemaphoreType.DMA((own_count // GROUP,)),
            pltpu.SemaphoreType.DMA((own_count,)),
            pltpu.SemaphoreType.DMA((max(10, remote),)),
        ],
        input_output_aliases={2: 0, 1: 1} if with_send else {2: 0},
        compiler_params=pltpu.CompilerParams(vmem_limit_bytes=58 * MIB),
        cost_estimate=pl.CostEstimate(
            flops=4 * base.size * first.shape[-1], bytes_accessed=16 * MIB, transcendentals=0
        ),
        name="after",
    )(plan, base, done, incoming, tiles, first, second)


def late_kernel(
    layer, plan, sums, done, first_in, second_in, out, u, first, second, result, base_sems, block_sems, sem
):
    weights = load_weights(layer, first_in, second_in, first, second, sem)
    n_fed = plan[COUNTS, N_FED]
    groups = rounded_up(n_fed)
    groups_now = rounded_up(plan[COUNTS, N_NOW])

    def load(group):
        cut = pl.ds(group * GROUP, GROUP)
        return pltpu.make_async_copy(sums.at[cut], u.at[cut], base_sems.at[group])

    def finish(place):
        block = plan[BLOCK, place]
        return pltpu.make_async_copy(result.at[place], out.at[block], block_sems.at[place])

    each_block(groups_now, groups, load, start)
    for part in weights:
        part.wait()

    def step(group, many):
        for offset in range(many):
            load(group + offset).wait()
        cut = pl.ds(group * GROUP, many * GROUP)
        values = network(
            u[cut].reshape(many * GROUP * u.shape[1], u.shape[2]), first, second, 512
        )
        result[cut] = values.reshape((many * GROUP,) + result.shape[1:])
        finish_group(group * GROUP, many * GROUP, 0, n_fed, finish)

    run_groups(groups_now, groups, step)
    each_block(jnp.minimum(groups_now * GROUP, n_fed), n_fed, finish, wait)


def late(layer, plan, sums, done, first, second):
    own_count = sums.shape[0]
    return pl.pallas_call(
        functools.partial(late_kernel, layer),
        out_shape=shape_of(done.shape, bf16),
        in_specs=[SMEM] + [ANY] * 4,
        out_specs=ANY,
        scratch_shapes=[
            pltpu.VMEM(sums.shape, f32),
            pltpu.VMEM(first.shape[1:], bf16),
            pltpu.VMEM(second.shape[1:], bf16),
            pltpu.VMEM(sums.shape, bf16),
            pltpu.SemaphoreType.DMA((own_count // GROUP,)),
            pltpu.SemaphoreType.DMA((own_count,)),
            pltpu.SemaphoreType.DMA((2,)),
        ],
        input_output_aliases={2: 0},
        compiler_params=pltpu.CompilerParams(vmem_limit_bytes=58 * MIB),
        cost_estimate=pl.CostEstimate(
            flops=sums.size * first.shape[-1], bytes_accessed=5 * MIB, transcendentals=0
        ),
        name="late",
    )(plan, sums, done, first, second)


def exchange(x, bit):
    devices = lax.axis_size("dev")
    return lax.ppermute(x, "dev", [(i, i ^ bit) for i in range(devices)])


def all_digits():
    devices = lax.axis_size("dev")
    digits, bit = [(1, 2)], 2
    while bit < devices:
        radix = 4 if 4 * bit <= devices else 2
        digits.append((bit, radix))
        bit *= radix
    return digits


def gather_step(x, bit, radix):
    return [x] + [exchange(x, bit * offset) for offset in range(1, radix)]


def gather_far(x, digits):
    return gather_step(x, *digits[-1])


def gather_near(pieces, digits):
    for digit in digits[-2:0:-1]:
        pieces = gather_step(jnp.concatenate(pieces, axis=0), *digit)
    return pieces


def gather_last(pieces, digits):
    x = jnp.concatenate(pieces, axis=0)
    return x, exchange(x, digits[0][0])


def scatter_near(position, kept, sent, digits, local):
    received = [exchange(sent, digits[0][0])]
    for bit, radix in digits[1:-1]:
        kept, *sent = combine(position, kept, received, bit, radix, local, f32)
        received = [exchange(part, bit * (1 + number)) for number, part in enumerate(sent)]
    return kept, received


def scatter_far(position, kept, received, digits, local, sent_type):
    bit, radix = digits[-1]
    kept, *sent = combine(position, kept, received, bit, radix, local, sent_type)
    return [kept] + [exchange(part, bit * (1 + number)) for number, part in enumerate(sent)]


def share_far(kept, received, digits):
    bit, radix = digits[-1]
    parts = [kept] + received
    while radix > 1:
        mine = total(parts)
        parts = [mine, exchange(mine, bit)]
        bit, radix = 2 * bit, radix // 2
    return parts


def body(
    peripheral, hubs, tiles, tile_rows, local_cols, tile_count, send_list, hub_place, w_in, w_out
):
    position = lax.axis_index("dev")
    digits = all_digits()
    block_size = tiles.shape[1]
    width = peripheral.shape[1]
    own_count = peripheral.shape[0] // block_size
    hub_rows = hub_place.shape[0]
    hub_count = hub_rows // block_size
    local = hubs.shape[0]
    remote = send_list.shape[1]
    place_col = hub_place.reshape(hub_rows, 1)
    place_row = hub_place.reshape(1, hub_rows)
    me = position.astype(jnp.int32).reshape(1)
    own = peripheral.reshape(own_count, block_size, width)
    all_to_all = functools.partial(
        lax.all_to_all, axis_name="dev", split_axis=0, concat_axis=0, tiled=True
    )

    pieces = gather_far(hubs, digits)
    outgoing = pack(send_list, own)
    outgoing, *pieces = lax.optimization_barrier((outgoing, *pieces))
    pieces = gather_near(pieces, digits)
    outgoing, place_col, tile_rows, local_cols, *pieces = lax.optimization_barrier(
        (outgoing, place_col, tile_rows, local_cols, *pieces)
    )
    plan = make_plan(me, tile_count, tile_rows, local_cols, send_list, hub_count, own_count)
    incoming = all_to_all(outgoing)
    halves = gather_last(pieces, digits)
    hub_table, mine, kept, sent = hub_first(
        digits, plan, tile_count, me, place_col, halves, own, tiles, local, remote
    )
    base, done = before(0, plan, tile_count, hub_table, own, tiles, w_in, w_out, remote)
    kept, received = scatter_near(me, kept, sent, digits, local)
    base, done, *received = lax.optimization_barrier((base, done, *received))
    parts = share_far(kept, received, digits)
    hub_new = hub_network(0, mine, parts, w_in, w_out)
    base, hub_new = lax.optimization_barrier((base, hub_new))
    done, sums, outgoing = after(0, plan, base, done, incoming, tiles, w_in, w_out, True)

    pieces = gather_near([hub_new], digits)
    outgoing, *pieces = lax.optimization_barrier((outgoing, *pieces))
    incoming = all_to_all(outgoing)
    own = late(0, plan, sums, done, w_in, w_out)
    halves = gather_last(pieces, digits)
    hub_table, mine, kept, sent = hub_second(
        digits, plan, tile_count, me, place_row, halves, own, tiles, local, remote
    )
    base, done = before(1, plan, tile_count, hub_table, own, tiles, w_in, w_out, remote)
    kept, received = scatter_near(me, kept, sent, digits, local)
    base, done, *received = lax.optimization_barrier((base, done, *received))
    parts = scatter_far(me, kept, received, digits, local, bf16)
    (peri_out,) = after(1, plan, base, done, incoming, tiles, w_in, w_out, False)
    peri_out, *parts = lax.optimization_barrier((peri_out, *parts))
    hub_out = hub_network(1, mine, parts, w_in, w_out)
    return (peri_out.reshape(peripheral.shape), hub_out)


def solution(mesh):
    in_specs = (
        P("dev", None),
        P("dev", None),
        P("dev", None, None),
        P("dev"),
        P("dev"),
        P("dev"),
        P("dev", None),
        P(),
        P(),
        P(),
    )
    out_specs = (P("dev", None), P("dev", None))
    return jax.shard_map(body, mesh=mesh, in_specs=in_specs, out_specs=out_specs, check_vma=False)
```
